32 devices in a mesh: wide: 8 (over z, y), tensor: 4 (over x, core).
Axes of the slice: x: 2, y: 2, z: 4, core: 2. Of those that a mesh axis runs over, the one named last changes fastest.
Arguments:
- queries: bfloat16 [2, 32, 64, 128], P(None, 'wide', 'tensor'), may hold values from -32 to 32
- prefix_keys: bfloat16 [131072, 8, 128], P('wide', 'tensor'), may hold values from -6 to 6
- prefix_values: bfloat16 [131072, 8, 128], P('wide', 'tensor'), may hold values from -6 to 6
- suffix_keys: bfloat16 [32, 4096, 8, 128], P('wide', None, 'tensor'), may hold values from -8 to 8
- suffix_values: bfloat16 [32, 4096, 8, 128], P('wide', None, 'tensor'), may hold values from -6 to 6
- new_keys: bfloat16 [2, 32, 8, 128], P(None, 'wide', 'tensor'), may hold values from -12 to 12
- new_values: bfloat16 [2, 32, 8, 128], P(None, 'wide', 'tensor'), may hold values from -6 to 6
- suffix_lengths: int32 [32], replicated, may hold values from 1 to 4096, as said below
- slot_row: int32 [32], P('wide'), may hold values from 0 to 31, each once
Outputs:
- attended: bfloat16 [2, 32, 64, 128], P(None, 'wide', 'tensor')
The draws below stay inside these ranges and needn't reach their ends.
Inputs may be any that keep to these rules, and one draw needn't show every extreme that they name: `suffix_lengths`: some continuation has exactly 4096 cached suffix tokens. `slot_row`: each continuation stands in exactly one slot.
All inputs are finite; a program needn't handle non-finite values.
Results may differ from the reference program's by a relative error of at most 0.0049.
Values may be sent and summed in bfloat16 or wider, within the bound.
No kernel may reach another device: no remote copies, remote signals or barrier semaphores. Data moves between devices by JAX's collectives and lax.ppermute only.
A program may use at most 128 MiB of HBM per device.

```python
import math
import jax
import jax.numpy as jnp
from jax import lax

HD = 128
KV = 8
GROUP = 8
SUF = 4096
HEADS = 64
ROWS = 32
PREFIX = 131072


def draw_queries(key, part):
    key = jax.random.fold_in(key, 3)
    return (jnp.clip(jax.random.normal(key, (2, ROWS, HEADS, HD), jnp.float32), -6.0, 6.0) * 3.5).astype(jnp.bfloat16)


def draw_prefix_keys(key, part):
    key = jax.random.fold_in(key, 5)
    return jnp.clip(jax.random.normal(key, (PREFIX, KV, HD), jnp.float32), -6.0, 6.0).astype(jnp.bfloat16)


def draw_suffix_lengths(key, part):
    key = jax.random.fold_in(key, 7)
    pieces = jax.random.split(key, 2)
    lengths = jax.random.randint(pieces[0], (ROWS,), 1, SUF + 1)
    longest = jax.random.randint(pieces[1], (), 0, ROWS)
    return lengths.at[longest].set(SUF)


def steps_of(stream_key, dims, cuts, low, high):
    def one(position, shards_of):
        steps = jax.random.uniform(jax.random.fold_in(jax.random.fold_in(stream_key, 6), position), (shards_of,), jnp.float32, low / len(cuts), high / len(cuts))
        return jnp.repeat(jnp.exp(steps), dims[position] // shards_of).reshape((-1,) + (1,) * (len(dims) - position - 1))

    loudness = one(*cuts[0])
    for cut in cuts[1:]:
        loudness = loudness * one(*cut)
    return loudness


def centred(rng, shape, scale, reach, cuts=(), held_as=jnp.bfloat16):
    entries = jax.random.normal(rng, shape, jnp.float32) * scale
    if len(cuts) > 0:
        entries = steps_of(rng, shape, cuts, -0.22, 0.18) * entries
    return jnp.clip(entries, min=-reach, max=reach).astype(held_as)


def setup_inputs(seed: int = 0) -> dict:
    seeds = jax.random.split(jax.random.key(seed), 10)
    return {
        "queries": draw_queries(jax.random.fold_in(seeds[9], 71), 0),
        "prefix_keys": draw_prefix_keys(jax.random.fold_in(seeds[9], 71), 0),
        "prefix_values": centred(seeds[2], (PREFIX, KV, HD), 1.0, 6.0, ((0, 8), (1, 4))),
        "suffix_keys": centred(seeds[3], (ROWS, SUF, KV, HD), 1.4, 8.0, ((0, 8), (2, 4))),
        "suffix_values": centred(seeds[4], (ROWS, SUF, KV, HD), 1.0, 6.0, ((0, 8), (2, 4))),
        "new_keys": centred(seeds[5], (2, ROWS, KV, HD), 2.0, 12.0, ((1, 8), (2, 4))),
        "new_values": centred(seeds[6], (2, ROWS, KV, HD), 1.0, 6.0, ((1, 8), (2, 4))),
        "suffix_lengths": draw_suffix_lengths(jax.random.fold_in(seeds[9], 71), 0),
        "slot_row": jax.random.permutation(seeds[8], ROWS).astype(jnp.int32),
    }


LOG2E = 1.4426950408889634

def reference(queries, prefix_keys, prefix_values, suffix_keys, suffix_values, new_keys, new_values, suffix_lengths, slot_row):
    scale = LOG2E / math.sqrt(HD)
    lengths = suffix_lengths[slot_row]
    block_size = math.gcd(PREFIX, 8192)
    block_count = PREFIX // block_size
    positions = jnp.arange(SUF, dtype=jnp.int32)
    suffix_valid = positions[None, :] < lengths[:, None]
    new_valid = jnp.arange(2, dtype=jnp.int32)[:, None] >= jnp.arange(2, dtype=jnp.int32)[None, :]

    def one_head(kv_head):
        head_queries = lax.dynamic_slice_in_dim(queries, kv_head * GROUP, GROUP, 2)
        flat_queries = head_queries.reshape(2 * ROWS * GROUP, HD)
        head_keys = lax.dynamic_index_in_dim(prefix_keys, kv_head, 1, keepdims=False)
        head_values = lax.dynamic_index_in_dim(prefix_values, kv_head, 1, keepdims=False)
        key_blocks = head_keys.reshape(block_count, block_size, HD)
        value_blocks = head_values.reshape(block_count, block_size, HD)

        def max_visit(running, key_block):
            scores = jnp.dot(flat_queries, key_block.T, preferred_element_type=jnp.float32) * scale
            return (jnp.maximum(running, lax.optimization_barrier(jnp.max(scores, axis=1))), None)
        prompt_max, _ = lax.scan(max_visit, jnp.full((2 * ROWS * GROUP,), -jnp.inf, jnp.float32), key_blocks)
        queries_wide = head_queries.astype(jnp.float32)
        own_keys = lax.dynamic_index_in_dim(suffix_keys, kv_head, 2, keepdims=False).astype(jnp.float32)
        own_values = lax.dynamic_index_in_dim(suffix_values, kv_head, 2, keepdims=False).astype(jnp.float32)
        suffix_scores = jnp.einsum('trgd,rpd->trgp', queries_wide, own_keys) * scale
        suffix_scores = jnp.where(suffix_valid[None, :, None, :], suffix_scores, -jnp.inf)
        fresh_keys = lax.dynamic_index_in_dim(new_keys, kv_head, 2, keepdims=False).astype(jnp.float32)
        fresh_values = lax.dynamic_index_in_dim(new_values, kv_head, 2, keepdims=False).astype(jnp.float32)
        fresh_scores = jnp.einsum('trgd,jrd->trgj', queries_wide, fresh_keys) * scale
        fresh_scores = jnp.where(new_valid[:, None, None, :], fresh_scores, -jnp.inf)
        top_score = jnp.maximum(prompt_max.reshape(2, ROWS, GROUP), lax.optimization_barrier(jnp.max(suffix_scores, axis=-1)))
        top_score = jnp.ceil(jnp.maximum(top_score, lax.optimization_barrier(jnp.max(fresh_scores, axis=-1))))
        flat_top = top_score.reshape(2 * ROWS * GROUP)

        def sum_visit(running, blocks):
            scores = jnp.dot(flat_queries, blocks[0].T, preferred_element_type=jnp.float32) * scale
            weights = jnp.exp2(scores - flat_top[:, None])
            summed = running[0] + lax.optimization_barrier(jnp.sum(weights, axis=1))
            weighted = running[1] + jnp.dot(weights.astype(jnp.bfloat16), blocks[1], preferred_element_type=jnp.float32)
            return ((summed, weighted), None)
        start_state = (jnp.zeros((2 * ROWS * GROUP,), jnp.float32), jnp.zeros((2 * ROWS * GROUP, HD), jnp.float32))
        (prompt_total, prompt_weighted), _ = lax.scan(sum_visit, start_state, (key_blocks, value_blocks))
        suffix_weights = jnp.exp2(suffix_scores - top_score[..., None])
        fresh_weights = jnp.exp2(fresh_scores - top_score[..., None])
        totals = prompt_total.reshape(2, ROWS, GROUP) + lax.optimization_barrier(jnp.sum(suffix_weights, axis=-1)) + lax.optimization_barrier(jnp.sum(fresh_weights, axis=-1))
        suffix_rounded = lax.optimization_barrier(suffix_weights.astype(jnp.bfloat16)).astype(jnp.float32)
        fresh_rounded = lax.optimization_barrier(fresh_weights.astype(jnp.bfloat16)).astype(jnp.float32)
        weighted = prompt_weighted.reshape(2, ROWS, GROUP, HD)
        weighted = weighted + jnp.einsum('trgp,rpd->trgd', suffix_rounded, own_values)
        weighted = weighted + jnp.einsum('trgj,jrd->trgd', fresh_rounded, fresh_values)
        return (weighted / totals[..., None]).astype(jnp.bfloat16)
    per_head = lax.map(one_head, jnp.arange(KV, dtype=jnp.int32))
    return per_head.transpose(1, 2, 0, 3, 4).reshape(2, ROWS, KV * GROUP, HD)
```

```python
import functools
import math

import jax
import jax.numpy as jnp
from jax import lax
from jax.experimental import pallas as pl
from jax.experimental.pallas import tpu as pltpu
from jax.sharding import PartitionSpec as P

LOG2E = 1.4426950408889634
LANES = 128
STEPS = 2
SAFE_TOTAL = 2.0**100
F32 = jnp.float32
BF16 = jnp.bfloat16


def coarse(x):
    return jnp.floor(jnp.ceil(x) * 0.0625) * 16.0


def lane_parity(rows):
    return lax.broadcasted_iota(jnp.int32, (rows, LANES), 1) % 2 == 0


def by_head(x, kv, even, reduce, neutral):
    if kv == 1:
        return jnp.broadcast_to(reduce(x, axis=1, keepdims=True), x.shape)
    first = reduce(jnp.where(even, x, neutral), axis=1, keepdims=True)
    second = reduce(jnp.where(even, neutral, x), axis=1, keepdims=True)
    return jnp.where(even, first, second)


def fold_lanes(x, op):
    parts = [x[:, at : at + LANES] for at in range(0, x.shape[1], LANES)]
    while len(parts) > 1:
        parts = [op(a, b) for a, b in zip(parts[::2], parts[1::2])] + parts[len(parts) & ~1 :]
    return parts[0]


def split_heads(x, kv):
    if kv == 1:
        return x
    assert kv == 2
    rows = x.shape[0]
    even = (lax.broadcasted_iota(jnp.int32, (16, LANES), 0) % 2 == 0).astype(F32).astype(BF16)
    tiles = x.reshape(rows // 16, 16, LANES)
    first = (tiles * even[None]).reshape(rows, LANES)
    second = (tiles * (1 - even)[None]).reshape(rows, LANES)
    return jnp.concatenate([first, second], axis=1)


def scores_of(q, keys):
    return lax.dot_general(q, keys, (((1,), (1,)), ((), ())), preferred_element_type=F32)


def spread(m, columns):
    return jnp.concatenate([m] * (columns // LANES), axis=1)


def prompt_kernel(sources, kv, chunk, scale, *refs):
    q_refs = refs[:sources]
    k_ref, v_ref, k_hbm, v_hbm, _ = refs[sources : sources + 5]
    outs = refs[sources + 5 : 2 * sources + 5]
    q_all, top, total, acc, k_buf, v_buf = refs[2 * sources + 5 :]
    step, last = pl.program_id(0), pl.num_programs(0) - 1
    rows = q_all.shape[0]
    per = rows // sources
    group = q_refs[0].shape[2] // kv
    even = lane_parity(rows)

    @pl.when(step == 0)
    def _():
        for s in range(sources):
            q = q_refs[s][...].astype(F32)
            steps, slots, _, _ = q.shape
            tiles = [
                jnp.concatenate([q[t, r, h * group : (h + 1) * group] for h in range(kv)], axis=1)
                for t in range(steps)
                for r in range(slots)
            ]
            q_all[s * per : (s + 1) * per, :] = jnp.concatenate(tiles, axis=0).astype(BF16)
        first = scores_of(q_all[...], split_heads(k_ref[:512, :], kv)) * scale
        top[...] = coarse(by_head(fold_lanes(first, jnp.maximum), kv, even, jnp.max, -jnp.inf))
        total[...] = jnp.zeros_like(total)
        acc[...] = jnp.zeros_like(acc)

    block = k_ref.shape[0]
    for at in range(0, block, chunk):
        s = scores_of(q_all[...], split_heads(k_ref[at : at + chunk, :], kv))
        w = jnp.exp2(s * scale - spread(top[...], chunk))
        total[...] += fold_lanes(w, jnp.add)
        acc[...] += jnp.dot(
            w.astype(BF16), split_heads(v_ref[at : at + chunk, :], kv), preferred_element_type=F32
        )

    def with_running_top():
        top[...] = jnp.full_like(top, -jnp.inf)
        total[...] = jnp.zeros_like(total)
        acc[...] = jnp.zeros_like(acc)
        piece = k_buf.shape[0]

        def visit(at, carry):
            pltpu.sync_copy(k_hbm.at[pl.ds(pl.multiple_of(at * piece, piece), piece), :], k_buf)
            pltpu.sync_copy(v_hbm.at[pl.ds(pl.multiple_of(at * piece, piece), piece), :], v_buf)
            s = scores_of(q_all[...], split_heads(k_buf[...], kv)) * scale
            peak = by_head(fold_lanes(s, jnp.maximum), kv, even, jnp.max, -jnp.inf)
            new_top = jnp.maximum(top[...], coarse(peak))
            shrink = jnp.exp2(top[...] - new_top)
            top[...] = new_top
            w = jnp.exp2(s - spread(new_top, piece))
            total[...] = total[...] * shrink + fold_lanes(w, jnp.add)
            both = jnp.concatenate(
                [jnp.broadcast_to(shrink[:, h : h + 1], (rows, LANES)) for h in range(kv)], axis=1
            )
            acc[...] = acc[...] * both + jnp.dot(
                w.astype(BF16), split_heads(v_buf[...], kv), preferred_element_type=F32
            )
            return carry

        lax.fori_loop(0, k_hbm.shape[0] // piece, visit, 0)

    @pl.when(step == last)
    def _():
        pl.when(jnp.logical_not(jnp.max(total[...]) < SAFE_TOTAL))(with_running_top)

        kind = lax.broadcasted_iota(jnp.int32, (rows, LANES), 1) // 2
        sums = by_head(total[...], kv, even, jnp.sum, 0.0)
        high = sums.astype(BF16).astype(F32)
        stats = jnp.where(kind == 0, top[...], jnp.where(kind == 1, high, sums - high))
        for s in range(sources):
            span = slice(s * per, (s + 1) * per)
            outs[s][:, : kv * LANES] = acc[span, :].astype(BF16)
            outs[s][:, kv * LANES :] = stats[span, :].astype(BF16)


def prompt_partials(queries, keys, values, after, kv, scale):
    sources = len(queries)
    steps, slots, heads, head_dim = queries[0].shape
    per = steps * slots * (heads // kv)
    rows = sources * per
    block = math.gcd(keys.shape[0], 2048)
    chunk = math.gcd(block, max(256, 1024 * 512 // rows))
    grid = keys.shape[0] // block
    whole = pl.BlockSpec((steps, slots, heads, head_dim), lambda i: (0, 0, 0, 0))
    tile = pl.BlockSpec((block, head_dim), lambda i: (i, 0))
    away = pl.BlockSpec(memory_space=pl.ANY)
    out = pl.BlockSpec((per, (kv + 1) * LANES), lambda i: (0, 0))
    return pl.pallas_call(
        functools.partial(prompt_kernel, sources, kv, chunk, scale),
        grid=(grid,),
        in_specs=[whole] * sources + [tile, tile, away, away, away],
        out_specs=[out] * sources,
        out_shape=[jax.ShapeDtypeStruct((per, (kv + 1) * LANES), BF16)] * sources,
        scratch_shapes=[
            pltpu.VMEM((rows, kv * LANES), BF16),
            pltpu.VMEM((rows, LANES), F32),
            pltpu.VMEM((rows, LANES), F32),
            pltpu.VMEM((rows, kv * LANES), F32),
            pltpu.VMEM((256, head_dim), BF16),
            pltpu.VMEM((256, head_dim), BF16),
        ],
        compiler_params=pltpu.CompilerParams(
            dimension_semantics=("arbitrary",), vmem_limit_bytes=60 * 1024 * 1024
        ),
        cost_estimate=pl.CostEstimate(
            flops=8 * rows * keys.shape[0] * head_dim,
            bytes_accessed=4 * keys.shape[0] * head_dim,
            transcendentals=rows * keys.shape[0],
        ),
        name="prompt",
    )(*queries, keys, values, keys, values, after)


def suffix_kernel(
    kv,
    scale,
    first,
    lengths,
    slots,
    q_ref,
    k_ref,
    v_ref,
    nk_ref,
    nv_ref,
    _,
    acc_ref,
    top_ref,
    total_ref,
    q_all,
):
    slot, step = pl.program_id(0) + first, pl.program_id(1)
    group = q_ref.shape[2] // kv
    length = lengths[slots[slot]]
    block = k_ref.shape[1]
    rows = q_all.shape[0]

    @pl.when(step == 0)
    def _():
        q = [q_ref[t, 0].astype(F32) for t in range(STEPS)]
        wide = jnp.concatenate(
            [q[t][h * group : (h + 1) * group] for h in range(kv) for t in range(STEPS)], axis=0
        )
        q_all[...] = wide.astype(BF16)
        row = lax.broadcasted_iota(jnp.int32, (rows, LANES), 0)
        second_head = row >= STEPS * group
        second_step = (row // group) % 2 == 1
        scores, values = [], []
        for j in range(STEPS):
            nk, nv = nk_ref[j, 0].astype(F32), nv_ref[j, 0].astype(F32)
            key = jnp.where(second_head, nk[kv - 1 : kv], nk[0:1])
            values.append(jnp.where(second_head, nv[kv - 1 : kv], nv[0:1]))
            s = jnp.sum(wide * key, axis=1, keepdims=True) * scale
            scores.append(jnp.broadcast_to(s, (rows, LANES)))
        scores[1] = jnp.where(second_step, scores[1], -jnp.inf)
        peak = jnp.ceil(jnp.maximum(scores[0], scores[1]))
        weights = [jnp.exp2(s - peak) for s in scores]
        top_ref[0] = peak
        total_ref[0] = weights[0] + weights[1]
        acc_ref[0] = sum(w.astype(BF16).astype(F32) * v for w, v in zip(weights, values))

    @pl.when(step * block < kv * length)
    def _():
        column = lax.broadcasted_iota(jnp.int32, (rows, block), 1)
        head = lax.broadcasted_iota(jnp.int32, (rows, block), 0) // (STEPS * group)
        usable = (column % kv == head) & (column < kv * length - step * block)
        s = jnp.where(usable, scores_of(q_all[...], k_ref[0]) * scale, -jnp.inf)
        old = top_ref[0]
        peak = jnp.max(fold_lanes(s, jnp.maximum), axis=1, keepdims=True)
        new_top = jnp.maximum(old, jnp.ceil(peak))
        shrink = jnp.exp2(old - new_top)
        w = jnp.exp2(s - spread(new_top, block))
        top_ref[0] = new_top
        total_ref[0] = total_ref[0] * shrink + jnp.sum(
            fold_lanes(w, jnp.add), axis=1, keepdims=True
        )
        acc_ref[0] = acc_ref[0] * shrink + jnp.dot(
            w.astype(BF16), v_ref[0], preferred_element_type=F32
        )


def suffix_partials(
    queries, keys, values, new_keys, new_values, lengths, slot_row, after, span, kv, scale
):
    steps, _, heads, head_dim = queries.shape
    first, slots = span[0], span[1] - span[0]
    block = math.gcd(keys.shape[1], 2048)
    blocks = keys.shape[1] // block
    rows = steps * heads

    def cache_at(r, i, lengths, slot_row):
        last = (kv * lengths[slot_row[first + r]] - 1) // block
        return (first + r, jnp.minimum(i, last), 0)

    cache = pl.BlockSpec((1, block, head_dim), cache_at)
    fresh = pl.BlockSpec((steps, 1, kv, head_dim), lambda r, i, *_: (0, first + r, 0, 0))
    out = pl.BlockSpec((1, rows, LANES), lambda r, i, *_: (r, 0, 0))
    shape = jax.ShapeDtypeStruct((slots, rows, LANES), F32)
    return pl.pallas_call(
        functools.partial(suffix_kernel, kv, scale, first),
        grid_spec=pltpu.PrefetchScalarGridSpec(
            num_scalar_prefetch=2,
            grid=(slots, blocks),
            in_specs=[
                pl.BlockSpec((steps, 1, heads, head_dim), lambda r, i, *_: (0, first + r, 0, 0)),
                cache,
                cache,
                fresh,
                fresh,
                pl.BlockSpec(memory_space=pl.ANY),
            ],
            out_specs=[out] * 3,
            scratch_shapes=[pltpu.VMEM((rows, head_dim), BF16)],
        ),
        out_shape=[shape] * 3,
        compiler_params=pltpu.CompilerParams(
            dimension_semantics=("arbitrary", "arbitrary"), vmem_limit_bytes=60 * 1024 * 1024
        ),
        cost_estimate=pl.CostEstimate(
            flops=4 * slots * rows * keys.shape[1] * head_dim,
            bytes_accessed=4 * slots * keys.shape[1] * head_dim,
            transcendentals=slots * rows * keys.shape[1],
        ),
        name="suffix",
    )(lengths, slot_row, queries, keys, values, new_keys, new_values, after)


def combine_kernel(sources, kv, *refs):
    parts = refs[:sources]
    near, out_ref = refs[sources:-1], refs[-1]
    steps, slots, heads, _ = out_ref.shape
    group = heads // kv
    parts = [p[...].astype(F32) for p in parts]
    for t in range(steps):
        for r in range(slots):
            done = []
            for h in range(kv):
                at = slice((t * slots + r) * group, (t * slots + r + 1) * group)
                own = slice((h * steps + t) * group, (h * steps + t + 1) * group)
                held, index = divmod(r, near[0].shape[0])
                sums, tops, totals = ([x[index, own]] for x in near[3 * held : 3 * held + 3])
                for p in parts:
                    stats = p[at, kv * LANES :]
                    shape = (group, LANES)
                    tops.append(jnp.broadcast_to(stats[:, h : h + 1], shape))
                    both = stats[:, 2 + h : 3 + h] + stats[:, 4 + h : 5 + h]
                    totals.append(jnp.broadcast_to(both, shape))
                    sums.append(p[at, h * LANES : (h + 1) * LANES])
                peak = functools.reduce(jnp.maximum, tops)
                factors = [jnp.exp2(m - peak) for m in tops]
                total = sum(f * x for f, x in zip(factors, totals))
                weighted = sum(f * x for f, x in zip(factors, sums))
                done.append(weighted / total)
            out_ref[t, r] = jnp.concatenate(done, axis=0).astype(BF16)


def combine(parts, near, kv, shape):
    return pl.pallas_call(
        functools.partial(combine_kernel, len(parts), kv),
        out_shape=jax.ShapeDtypeStruct(shape, BF16),
        name="combine",
    )(*parts, *near)


def per_device(
    sources,
    queries,
    prefix_keys,
    prefix_values,
    suffix_keys,
    suffix_values,
    new_keys,
    new_values,
    suffix_lengths,
    slot_row,
):
    head_dim = queries.shape[-1]
    kv = prefix_keys.shape[1]
    scale = LOG2E / math.sqrt(head_dim)
    interleaved = lambda x: x.reshape(*x.shape[:-3], x.shape[-3] * x.shape[-2], x.shape[-1])

    def shifted(x, k):
        return lax.ppermute(x, "wide", [(i, (i + k) % sources) for i in range(sources)])

    everyone = [queries] + [shifted(queries, k) for k in range(1, sources)]
    own = (
        queries,
        interleaved(suffix_keys),
        interleaved(suffix_values),
        new_keys,
        new_values,
        suffix_lengths,
        slot_row,
    )
    slots = queries.shape[1]
    early = suffix_partials(*own, suffix_lengths, (0, slots // 2), kv, scale)
    partials = prompt_partials(everyone, interleaved(prefix_keys), interleaved(prefix_values), early[0], kv, scale)
    home = [partials[0]] + [shifted(partials[k], sources - k) for k in range(1, sources)]
    late = suffix_partials(*own, partials[0], (slots // 2, slots), kv, scale)
    return combine(home, [*early, *late], kv, queries.shape)


def solution(mesh):
    placed = (
        P(None, "wide", "tensor", None),
        P("wide", "tensor", None),
        P("wide", "tensor", None),
        P("wide", None, "tensor", None),
        P("wide", None, "tensor", None),
        P(None, "wide", "tensor", None),
        P(None, "wide", "tensor", None),
        P(),
        P("wide"),
    )
    return jax.shard_map(
        functools.partial(per_device, mesh.shape["wide"]),
        mesh=mesh,
        in_specs=placed,
        out_specs=P(None, "wide", "tensor", None),
        check_vma=False,
    )
```

```python
import functools
import math

import jax
import jax.numpy as jnp
from jax import lax
from jax.experimental import pallas as pl
from jax.experimental.pallas import tpu as pltpu
from jax.sharding import PartitionSpec as P

LOG2E = 1.4426950408889634
LANES = 128
STEPS = 2
SAFE_TOTAL = 2.0**100
F32 = jnp.float32
BF16 = jnp.bfloat16


def coarse(x):
    return jnp.floor(jnp.ceil(x) * 0.0625) * 16.0


def lane_parity(rows):
    return lax.broadcasted_iota(jnp.int32, (rows, LANES), 1) % 2 == 0


def by_head(x, kv, even, reduce, neutral):
    if kv == 1:
        return jnp.broadcast_to(reduce(x, axis=1, keepdims=True), x.shape)
    first = reduce(jnp.where(even, x, neutral), axis=1, keepdims=True)
    second = reduce(jnp.where(even, neutral, x), axis=1, keepdims=True)
    return jnp.where(even, first, second)


def fold_lanes(x, op):
    parts = [x[:, at : at + LANES] for at in range(0, x.shape[1], LANES)]
    while len(parts) > 1:
        parts = [op(a, b) for a, b in zip(parts[::2], parts[1::2])] + parts[len(parts) & ~1 :]
    return parts[0]


def split_heads(x, kv):
    if kv == 1:
        return x
    assert kv == 2
    rows = x.shape[0]
    even = (lax.broadcasted_iota(jnp.int32, (16, LANES), 0) % 2 == 0).astype(F32).astype(BF16)
    tiles = x.reshape(rows // 16, 16, LANES)
    first = (tiles * even[None]).reshape(rows, LANES)
    second = (tiles * (1 - even)[None]).reshape(rows, LANES)
    return jnp.concatenate([first, second], axis=1)


def scores_of(q, keys):
    return lax.dot_general(q, keys, (((1,), (1,)), ((), ())), preferred_element_type=F32)


def spread(m, columns):
    return jnp.concatenate([m] * (columns // LANES), axis=1)


def prompt_kernel(kv, chunk, scale, *refs):
    q_ref, k_ref, v_ref, k_hbm, v_hbm, _, out_ref = refs[:7]
    q_all, scores, top, total, acc, k_buf, v_buf = refs[7:]
    step, last = pl.program_id(0), pl.num_programs(0) - 1
    sources = q_ref.shape[0]
    rows = q_all.shape[0]
    per = rows // sources
    group = q_ref.shape[3] // kv
    even = lane_parity(rows)
    pieces = scores.shape[0]

    def score(c):
        keys = split_heads(k_ref[c * chunk : (c + 1) * chunk, :], kv)
        return scores_of(q_all[...], keys)

    def weigh(c):
        w = jnp.exp2(scores[c] * scale - spread(top[...], chunk))
        total[...] += fold_lanes(w, jnp.add)
        values = split_heads(v_ref[c * chunk : (c + 1) * chunk, :], kv)
        acc[...] += jnp.dot(w.astype(BF16), values, preferred_element_type=F32)

    @pl.when(step == 0)
    def _():
        for s in range(sources):
            q = q_ref[s].astype(F32)
            steps, slots, _, _ = q.shape
            tiles = [
                jnp.concatenate([q[t, r, h * group : (h + 1) * group] for h in range(kv)], axis=1)
                for t in range(steps)
                for r in range(slots)
            ]
            q_all[s * per : (s + 1) * per, :] = jnp.concatenate(tiles, axis=0).astype(BF16)
        total[...] = jnp.zeros_like(total)
        acc[...] = jnp.zeros_like(acc)
        for c in range(pieces):
            scores[c] = score(c)
        first = fold_lanes(scores[0], jnp.maximum) * scale
        top[...] = coarse(by_head(first, kv, even, jnp.max, -jnp.inf))

    @pl.when((step > 0) & (step < last))
    def _():
        for c in range(pieces):
            weigh(c)
            scores[c] = score(c)

    def with_running_top():
        top[...] = jnp.full_like(top, -jnp.inf)
        total[...] = jnp.zeros_like(total)
        acc[...] = jnp.zeros_like(acc)
        piece = k_buf.shape[0]

        def visit(at, carry):
            pltpu.sync_copy(k_hbm.at[pl.ds(pl.multiple_of(at * piece, piece), piece), :], k_buf)
            pltpu.sync_copy(v_hbm.at[pl.ds(pl.multiple_of(at * piece, piece), piece), :], v_buf)
            s = scores_of(q_all[...], split_heads(k_buf[...], kv)) * scale
            peak = by_head(fold_lanes(s, jnp.maximum), kv, even, jnp.max, -jnp.inf)
            new_top = jnp.maximum(top[...], coarse(peak))
            shrink = jnp.exp2(top[...] - new_top)
            top[...] = new_top
            w = jnp.exp2(s - spread(new_top, piece))
            total[...] = total[...] * shrink + fold_lanes(w, jnp.add)
            both = jnp.concatenate(
                [jnp.broadcast_to(shrink[:, h : h + 1], (rows, LANES)) for h in range(kv)], axis=1
            )
            acc[...] = acc[...] * both + jnp.dot(
                w.astype(BF16), split_heads(v_buf[...], kv), preferred_element_type=F32
            )
            return carry

        lax.fori_loop(0, k_hbm.shape[0] // piece, visit, 0)

    @pl.when(step == last)
    def _():
        for c in range(pieces):
            weigh(c)
        pl.when(jnp.logical_not(jnp.max(total[...]) < SAFE_TOTAL))(with_running_top)

        kind = lax.broadcasted_iota(jnp.int32, (rows, LANES), 1) // 2
        sums = by_head(total[...], kv, even, jnp.sum, 0.0)
        high = sums.astype(BF16).astype(F32)
        stats = jnp.where(kind == 0, top[...], jnp.where(kind == 1, high, sums - high))
        for s in range(sources):
            span = slice(s * per, (s + 1) * per)
            out_ref[s, :, : kv * LANES] = acc[span, :].astype(BF16)
            out_ref[s, :, kv * LANES :] = stats[span, :].astype(BF16)


def prompt_partials(queries, keys, values, after, kv, scale):
    sources, steps, slots, heads, head_dim = queries.shape
    per = steps * slots * (heads // kv)
    rows = sources * per
    block = math.gcd(keys.shape[0], 2048)
    chunk = math.gcd(block, max(256, 1024 * 512 // rows))
    blocks = keys.shape[0] // block
    away = pl.BlockSpec(memory_space=pl.ANY)
    return pl.pallas_call(
        functools.partial(prompt_kernel, kv, chunk, scale),
        grid=(blocks + 1,),
        in_specs=[
            pl.BlockSpec(queries.shape, lambda i: (0, 0, 0, 0, 0)),
            pl.BlockSpec((block, head_dim), lambda i: (jnp.minimum(i, blocks - 1), 0)),
            pl.BlockSpec((block, head_dim), lambda i: (jnp.maximum(i - 1, 0), 0)),
            away,
            away,
            away,
        ],
        out_specs=pl.BlockSpec((sources, per, (kv + 1) * LANES), lambda i: (0, 0, 0)),
        out_shape=jax.ShapeDtypeStruct((sources, per, (kv + 1) * LANES), BF16),
        scratch_shapes=[
            pltpu.VMEM((rows, kv * LANES), BF16),
            pltpu.VMEM((block // chunk, rows, chunk), F32),
            pltpu.VMEM((rows, LANES), F32),
            pltpu.VMEM((rows, LANES), F32),
            pltpu.VMEM((rows, kv * LANES), F32),
            pltpu.VMEM((256, head_dim), BF16),
            pltpu.VMEM((256, head_dim), BF16),
        ],
        compiler_params=pltpu.CompilerParams(
            dimension_semantics=("arbitrary",), vmem_limit_bytes=60 * 1024 * 1024
        ),
        cost_estimate=pl.CostEstimate(
            flops=8 * rows * keys.shape[0] * head_dim,
            bytes_accessed=4 * keys.shape[0] * head_dim,
            transcendentals=rows * keys.shape[0],
        ),
        name="prompt",
    )(queries, keys, values, keys, values, after)


def suffix_kernel(
    kv,
    scale,
    first,
    lengths,
    slots,
    q_ref,
    k_ref,
    v_ref,
    nk_ref,
    nv_ref,
    _,
    acc_ref,
    top_ref,
    total_ref,
    q_all,
):
    slot, step = pl.program_id(0) + first, pl.program_id(1)
    group = q_ref.shape[2] // kv
    length = lengths[slots[slot]]
    block = k_ref.shape[1]
    rows = q_all.shape[0]

    @pl.when(step == 0)
    def _():
        q = [q_ref[t, 0].astype(F32) for t in range(STEPS)]
        wide = jnp.concatenate(
            [q[t][h * group : (h + 1) * group] for h in range(kv) for t in range(STEPS)], axis=0
        )
        q_all[...] = wide.astype(BF16)
        row = lax.broadcasted_iota(jnp.int32, (rows, LANES), 0)
        second_head = row >= STEPS * group
        second_step = (row // group) % 2 == 1
        scores, values = [], []
        for j in range(STEPS):
            nk, nv = nk_ref[j, 0].astype(F32), nv_ref[j, 0].astype(F32)
            key = jnp.where(second_head, nk[kv - 1 : kv], nk[0:1])
            values.append(jnp.where(second_head, nv[kv - 1 : kv], nv[0:1]))
            s = jnp.sum(wide * key, axis=1, keepdims=True) * scale
            scores.append(jnp.broadcast_to(s, (rows, LANES)))
        scores[1] = jnp.where(second_step, scores[1], -jnp.inf)
        peak = jnp.ceil(jnp.maximum(scores[0], scores[1]))
        weights = [jnp.exp2(s - peak) for s in scores]
        top_ref[0] = peak
        total_ref[0] = weights[0] + weights[1]
        acc_ref[0] = sum(w.astype(BF16).astype(F32) * v for w, v in zip(weights, values))

    @pl.when(step * block < kv * length)
    def _():
        column = lax.broadcasted_iota(jnp.int32, (rows, block), 1)
        head = lax.broadcasted_iota(jnp.int32, (rows, block), 0) // (STEPS * group)
        usable = (column % kv == head) & (column < kv * length - step * block)
        s = jnp.where(usable, scores_of(q_all[...], k_ref[0]) * scale, -jnp.inf)
        old = top_ref[0]
        peak = jnp.max(fold_lanes(s, jnp.maximum), axis=1, keepdims=True)
        new_top = jnp.maximum(old, jnp.ceil(peak))
        shrink = jnp.exp2(old - new_top)
        w = jnp.exp2(s - spread(new_top, block))
        top_ref[0] = new_top
        total_ref[0] = total_ref[0] * shrink + jnp.sum(
            fold_lanes(w, jnp.add), axis=1, keepdims=True
        )
        acc_ref[0] = acc_ref[0] * shrink + jnp.dot(
            w.astype(BF16), v_ref[0], preferred_element_type=F32
        )


def suffix_partials(
    queries, keys, values, new_keys, new_values, lengths, slot_row, after, span, kv, scale
):
    steps, _, heads, head_dim = queries.shape
    first, slots = span[0], span[1] - span[0]
    block = math.gcd(keys.shape[1], 4096)
    blocks = keys.shape[1] // block
    rows = steps * heads

    def cache_at(r, i, lengths, slot_row):
        last = (kv * lengths[slot_row[first + r]] - 1) // block
        return (first + r, jnp.minimum(i, last), 0)

    cache = pl.BlockSpec((1, block, head_dim), cache_at)
    fresh = pl.BlockSpec((steps, 1, kv, head_dim), lambda r, i, *_: (0, first + r, 0, 0))
    out = pl.BlockSpec((1, rows, LANES), lambda r, i, *_: (r, 0, 0))
    shape = jax.ShapeDtypeStruct((slots, rows, LANES), F32)
    return pl.pallas_call(
        functools.partial(suffix_kernel, kv, scale, first),
        grid_spec=pltpu.PrefetchScalarGridSpec(
            num_scalar_prefetch=2,
            grid=(slots, blocks),
            in_specs=[
                pl.BlockSpec((steps, 1, heads, head_dim), lambda r, i, *_: (0, first + r, 0, 0)),
                cache,
                cache,
                fresh,
                fresh,
                pl.BlockSpec(memory_space=pl.ANY),
            ],
            out_specs=[out] * 3,
            scratch_shapes=[pltpu.VMEM((rows, head_dim), BF16)],
        ),
        out_shape=[shape] * 3,
        compiler_params=pltpu.CompilerParams(
            dimension_semantics=("arbitrary", "arbitrary"), vmem_limit_bytes=60 * 1024 * 1024
        ),
        cost_estimate=pl.CostEstimate(
            flops=4 * slots * rows * keys.shape[1] * head_dim,
            bytes_accessed=4 * slots * keys.shape[1] * head_dim,
            transcendentals=slots * rows * keys.shape[1],
        ),
        name="suffix",
    )(lengths, slot_row, queries, keys, values, new_keys, new_values, after)


def combine_kernel(kv, parts_ref, *refs):
    near, out_ref = refs[:-1], refs[-1]
    steps, slots, heads, _ = out_ref.shape
    group = heads // kv
    parts = [parts_ref[s].astype(F32) for s in range(parts_ref.shape[0])]
    for t in range(steps):
        for r in range(slots):
            done = []
            for h in range(kv):
                at = slice((t * slots + r) * group, (t * slots + r + 1) * group)
                own = slice((h * steps + t) * group, (h * steps + t + 1) * group)
                held, index = divmod(r, near[0].shape[0])
                sums, tops, totals = ([x[index, own]] for x in near[3 * held : 3 * held + 3])
                for p in parts:
                    stats = p[at, kv * LANES :]
                    shape = (group, LANES)
                    tops.append(jnp.broadcast_to(stats[:, h : h + 1], shape))
                    both = stats[:, 2 + h : 3 + h] + stats[:, 4 + h : 5 + h]
                    totals.append(jnp.broadcast_to(both, shape))
                    sums.append(p[at, h * LANES : (h + 1) * LANES])
                peak = functools.reduce(jnp.maximum, tops)
                factors = [jnp.exp2(m - peak) for m in tops]
                total = sum(f * x for f, x in zip(factors, totals))
                weighted = sum(f * x for f, x in zip(factors, sums))
                done.append(weighted / total)
            out_ref[t, r] = jnp.concatenate(done, axis=0).astype(BF16)


def combine(parts, near, kv, shape):
    return pl.pallas_call(
        functools.partial(combine_kernel, kv),
        out_shape=jax.ShapeDtypeStruct(shape, BF16),
        name="combine",
    )(parts, *near)


def per_device(
    sources,
    queries,
    prefix_keys,
    prefix_values,
    suffix_keys,
    suffix_values,
    new_keys,
    new_values,
    suffix_lengths,
    slot_row,
):
    head_dim = queries.shape[-1]
    kv = prefix_keys.shape[1]
    scale = LOG2E / math.sqrt(head_dim)
    interleaved = lambda x: x.reshape(*x.shape[:-3], x.shape[-3] * x.shape[-2], x.shape[-1])

    def exchange(x):
        return lax.all_to_all(x, "wide", 0, 0, tiled=True)

    everyone = exchange(jnp.broadcast_to(queries[None], (sources, *queries.shape)))
    own = (
        queries,
        interleaved(suffix_keys),
        interleaved(suffix_values),
        new_keys,
        new_values,
        suffix_lengths,
        slot_row,
    )
    slots = queries.shape[1]
    early = suffix_partials(*own, suffix_lengths, (0, slots // 2), kv, scale)
    partials = prompt_partials(everyone, interleaved(prefix_keys), interleaved(prefix_values), early[0], kv, scale)
    home = exchange(partials)
    late = suffix_partials(*own, partials, (slots // 2, slots), kv, scale)
    return combine(home, [*early, *late], kv, queries.shape)


def solution(mesh):
    placed = (
        P(None, "wide", "tensor", None),
        P("wide", "tensor", None),
        P("wide", "tensor", None),
        P("wide", None, "tensor", None),
        P("wide", None, "tensor", None),
        P(None, "wide", "tensor", None),
        P(None, "wide", "tensor", None),
        P(),
        P("wide"),
    )
    return jax.shard_map(
        functools.partial(per_device, mesh.shape["wide"]),
        mesh=mesh,
        in_specs=placed,
        out_specs=P(None, "wide", "tensor", None),
        check_vma=False,
    )
```

```python
import functools
import math

import jax
import jax.numpy as jnp
from jax import lax
from jax.experimental import pallas as pl
from jax.experimental.pallas import tpu as pltpu
from jax.sharding import PartitionSpec as P

LOG2E = 1.4426950408889634
LANES = 128
STEPS = 2
TOO_LARGE, TOO_SMALL = 2.0**100, 2.0**-60
F32 = jnp.float32
BF16 = jnp.bfloat16


def coarse(x):
    return jnp.floor(jnp.ceil(x) * 0.0625) * 16.0


def out_of_range(totals):
    return jnp.logical_not((jnp.max(totals) < TOO_LARGE) & (jnp.min(totals) > TOO_SMALL))


def lane_parity(rows):
    return lax.broadcasted_iota(jnp.int32, (rows, LANES), 1) % 2 == 0


def by_head(x, kv, even, reduce, neutral):
    if kv == 1:
        return jnp.broadcast_to(reduce(x, axis=1, keepdims=True), x.shape)
    first = reduce(jnp.where(even, x, neutral), axis=1, keepdims=True)
    second = reduce(jnp.where(even, neutral, x), axis=1, keepdims=True)
    return jnp.where(even, first, second)


def fold_lanes(x, op):
    parts = [x[:, at : at + LANES] for at in range(0, x.shape[1], LANES)]
    while len(parts) > 1:
        parts = [op(a, b) for a, b in zip(parts[::2], parts[1::2])] + parts[len(parts) & ~1 :]
    return parts[0]


def split_heads(x, kv):
    if kv == 1:
        return x
    assert kv == 2
    rows = x.shape[0]
    even = (lax.broadcasted_iota(jnp.int32, (16, LANES), 0) % 2 == 0).astype(F32).astype(BF16)
    tiles = x.reshape(rows // 16, 16, LANES)
    first = (tiles * even[None]).reshape(rows, LANES)
    second = (tiles * (1 - even)[None]).reshape(rows, LANES)
    return jnp.concatenate([first, second], axis=1)


def scores_of(q, keys):
    return lax.dot_general(q, keys, (((1,), (1,)), ((), ())), preferred_element_type=F32)


def spread(m, columns):
    return jnp.concatenate([m] * (columns // LANES), axis=1)


def prompt_kernel(kv, chunk, scale, *refs):
    q_hbm, k_ref, v_ref, k_hbm, v_hbm, _, out_ref = refs[:7]
    q_in, q_all, scores, weights, top, total, acc, k_buf, v_buf = refs[7:]
    step, last = pl.program_id(0), pl.num_programs(0) - 1
    sources = q_in.shape[0]
    rows = q_all.shape[0]
    per = rows // sources
    group = q_in.shape[3] // kv
    even = lane_parity(rows)
    pieces = scores.shape[0]

    def score(c):
        keys = split_heads(k_ref[c * chunk : (c + 1) * chunk, :], kv)
        scores[c] = scores_of(q_all[...], keys)

    def weigh(c):
        for at in range(0, rows, 16):
            w = jnp.exp2(scores[c, at : at + 16, :] * scale)
            total[at : at + 16, :] += fold_lanes(w, jnp.add)
            weights[c, at : at + 16, :] = w.astype(BF16)

    def gather(c):
        values = split_heads(v_ref[c * chunk : (c + 1) * chunk, :], kv)
        acc[...] += jnp.dot(weights[c], values, preferred_element_type=F32)

    @pl.when(step == 0)
    def _():
        pltpu.sync_copy(q_hbm, q_in)
        for s in range(sources):
            q = q_in[s].astype(F32)
            steps, slots, _, _ = q.shape
            tiles = [
                jnp.concatenate([q[t, r, h * group : (h + 1) * group] for h in range(kv)], axis=1)
                for t in range(steps)
                for r in range(slots)
            ]
            q_all[s * per : (s + 1) * per, :] = jnp.concatenate(tiles, axis=0).astype(BF16)
        top[...] = jnp.zeros_like(top)
        total[...] = jnp.zeros_like(total)
        acc[...] = jnp.zeros_like(acc)
        for c in range(pieces):
            score(c)

    @pl.when((step > 0) & (step < last))
    def _():
        for c in range(pieces):
            weigh(c)
            score(c)
            if c > 0:
                gather(c - 1)
        gather(pieces - 1)

    def with_running_top():
        top[...] = jnp.full_like(top, -jnp.inf)
        total[...] = jnp.zeros_like(total)
        acc[...] = jnp.zeros_like(acc)
        piece = k_buf.shape[0]

        def visit(at, carry):
            pltpu.sync_copy(k_hbm.at[pl.ds(pl.multiple_of(at * piece, piece), piece), :], k_buf)
            pltpu.sync_copy(v_hbm.at[pl.ds(pl.multiple_of(at * piece, piece), piece), :], v_buf)
            s = scores_of(q_all[...], split_heads(k_buf[...], kv)) * scale
            peak = by_head(fold_lanes(s, jnp.maximum), kv, even, jnp.max, -jnp.inf)
            new_top = jnp.maximum(top[...], coarse(peak))
            shrink = jnp.exp2(top[...] - new_top)
            top[...] = new_top
            w = jnp.exp2(s - spread(new_top, piece))
            total[...] = total[...] * shrink + fold_lanes(w, jnp.add)
            both = jnp.concatenate(
                [jnp.broadcast_to(shrink[:, h : h + 1], (rows, LANES)) for h in range(kv)], axis=1
            )
            acc[...] = acc[...] * both + jnp.dot(
                w.astype(BF16), split_heads(v_buf[...], kv), preferred_element_type=F32
            )
            return carry

        lax.fori_loop(0, k_hbm.shape[0] // piece, visit, 0)

    @pl.when(step == last)
    def _():
        for c in range(pieces):
            weigh(c)
            gather(c)
        sums = by_head(total[...], kv, even, jnp.sum, 0.0)
        total[...] = sums

        @pl.when(out_of_range(sums))
        def _():
            with_running_top()
            total[...] = by_head(total[...], kv, even, jnp.sum, 0.0)

        kind = lax.broadcasted_iota(jnp.int32, (rows, LANES), 1) // 2
        sums = total[...]
        high = sums.astype(BF16).astype(F32)
        stats = jnp.where(kind == 0, top[...], jnp.where(kind == 1, high, sums - high))
        for s in range(sources):
            span = slice(s * per, (s + 1) * per)
            out_ref[s, :, : kv * LANES] = acc[span, :].astype(BF16)
            out_ref[s, :, kv * LANES :] = stats[span, :].astype(BF16)


def prompt_partials(queries, keys, values, after, kv, scale):
    sources, steps, slots, heads, head_dim = queries.shape
    per = steps * slots * (heads // kv)
    rows = sources * per
    block = math.gcd(keys.shape[0], 2048)
    chunk = math.gcd(block, max(256, 1024 * 512 // rows))
    blocks = keys.shape[0] // block
    away = pl.BlockSpec(memory_space=pl.ANY)
    return pl.pallas_call(
        functools.partial(prompt_kernel, kv, chunk, scale),
        grid=(blocks + 1,),
        in_specs=[
            away,
            pl.BlockSpec((block, head_dim), lambda i: (jnp.minimum(i, blocks - 1), 0)),
            pl.BlockSpec((block, head_dim), lambda i: (jnp.maximum(i - 1, 0), 0)),
            away,
            away,
            away,
        ],
        out_specs=pl.BlockSpec((sources, per, (kv + 1) * LANES), lambda i: (0, 0, 0)),
        out_shape=jax.ShapeDtypeStruct((sources, per, (kv + 1) * LANES), BF16),
        scratch_shapes=[
            pltpu.VMEM(queries.shape, BF16),
            pltpu.VMEM((rows, kv * LANES), BF16),
            pltpu.VMEM((block // chunk, rows, chunk), F32),
            pltpu.VMEM((block // chunk, rows, chunk), BF16),
            pltpu.VMEM((rows, LANES), F32),
            pltpu.VMEM((rows, LANES), F32),
            pltpu.VMEM((rows, kv * LANES), F32),
            pltpu.VMEM((256, head_dim), BF16),
            pltpu.VMEM((256, head_dim), BF16),
        ],
        compiler_params=pltpu.CompilerParams(
            dimension_semantics=("arbitrary",), vmem_limit_bytes=60 * 1024 * 1024
        ),
        cost_estimate=pl.CostEstimate(
            flops=8 * rows * keys.shape[0] * head_dim,
            bytes_accessed=4 * keys.shape[0] * head_dim,
            transcendentals=rows * keys.shape[0],
        ),
        name="prompt",
    )(queries, keys, values, keys, values, after)


def suffix_kernel(kv, scale, first, lengths, slots, *refs):
    q_ref, k_ref, v_ref, nk_ref, nv_ref, k_hbm, v_hbm, _ = refs[:8]
    acc_ref, top_ref, total_ref, q_all, k_buf, v_buf = refs[8:]
    slot, step = pl.program_id(0) + first, pl.program_id(1)
    last = pl.num_programs(1) - 1
    group = q_ref.shape[2] // kv
    length = kv * lengths[slots[slot]]
    block = k_ref.shape[1]
    rows = kv * STEPS * group
    head = lax.broadcasted_iota(jnp.int32, (rows, LANES), 0) // (STEPS * group)
    lane = lax.broadcasted_iota(jnp.int32, (rows, LANES), 1)
    foreign = jnp.where(lane % kv == head, 0.0, -jnp.inf)

    def fresh(relative):
        row = lax.broadcasted_iota(jnp.int32, (rows, LANES), 0)
        second_head = row >= STEPS * group
        second_step = (row // group) % 2 == 1
        scores, values = [], []
        for j in range(STEPS):
            nk, nv = nk_ref[j, 0].astype(F32), nv_ref[j, 0].astype(F32)
            key = jnp.where(second_head, nk[kv - 1 : kv], nk[0:1])
            values.append(jnp.where(second_head, nv[kv - 1 : kv], nv[0:1]))
            q = q_all[:rows, :LANES].astype(F32)
            s = jnp.sum(q * key, axis=1, keepdims=True) * scale
            scores.append(jnp.broadcast_to(s, (rows, LANES)))
        scores[1] = jnp.where(second_step, scores[1], -jnp.inf)
        peak = jnp.ceil(jnp.maximum(scores[0], scores[1])) if relative else jnp.zeros_like(scores[0])
        weights = [jnp.exp2(s - peak) for s in scores]
        top_ref[0] = peak
        total_ref[0] = weights[0] + weights[1]
        acc_ref[0] = sum(w.astype(BF16).astype(F32) * v for w, v in zip(weights, values))

    @pl.when(step == 0)
    def _():
        q = [q_ref[t, 0].astype(F32) for t in range(STEPS)]
        wide = jnp.concatenate(
            [q[t][h * group : (h + 1) * group] for h in range(kv) for t in range(STEPS)], axis=0
        )
        none = jnp.zeros_like(wide)
        q_all[...] = jnp.concatenate(
            [jnp.concatenate([wide, none], axis=1), jnp.concatenate([none, wide], axis=1)], axis=0
        ).astype(BF16)
        fresh(False)

    def attend(partial):
        half = block // 2
        keys = jnp.concatenate([k_ref[0, :half], k_ref[0, half:]], axis=1)
        values = jnp.concatenate([v_ref[0, :half], v_ref[0, half:]], axis=1)
        bias = spread(jnp.concatenate([foreign, foreign], axis=0), half)
        s = scores_of(q_all[...], keys) * scale + bias
        if partial:
            at = lax.broadcasted_iota(jnp.int32, s.shape, 1)
            at += jnp.where(lax.broadcasted_iota(jnp.int32, s.shape, 0) >= rows, half, 0)
            s = jnp.where(at < length - step * block, s, -jnp.inf)
        w = jnp.exp2(s)
        sums = jnp.sum(fold_lanes(w, jnp.add), axis=1, keepdims=True)
        total_ref[0] += jnp.broadcast_to(sums[:rows] + sums[rows:], (rows, LANES))
        out = jnp.dot(w.astype(BF16), values, preferred_element_type=F32)
        acc_ref[0] += out[:rows, :LANES] + out[rows:, LANES:]

    pl.when((step + 1) * block <= length)(lambda: attend(False))
    pl.when((step * block < length) & ((step + 1) * block > length))(lambda: attend(True))

    def with_running_top():
        fresh(True)
        piece = k_buf.shape[0]

        def visit(i, carry):
            begin = pl.multiple_of(i * piece, piece)
            pltpu.sync_copy(k_hbm.at[slot, pl.ds(begin, piece), :], k_buf)
            pltpu.sync_copy(v_hbm.at[slot, pl.ds(begin, piece), :], v_buf)
            s = scores_of(q_all[:rows, :LANES], k_buf[...]) * scale + spread(foreign, piece)
            at = lax.broadcasted_iota(jnp.int32, s.shape, 1)
            s = jnp.where(at < length - begin, s, -jnp.inf)
            old = top_ref[0]
            peak = jnp.max(fold_lanes(s, jnp.maximum), axis=1, keepdims=True)
            new_top = jnp.maximum(old, jnp.ceil(peak))
            shrink = jnp.exp2(old - new_top)
            w = jnp.exp2(s - spread(new_top, piece))
            top_ref[0] = new_top
            total_ref[0] = total_ref[0] * shrink + jnp.sum(
                fold_lanes(w, jnp.add), axis=1, keepdims=True
            )
            acc_ref[0] = acc_ref[0] * shrink + jnp.dot(
                w.astype(BF16), v_buf[...], preferred_element_type=F32
            )
            return carry

        lax.fori_loop(0, (length + piece - 1) // piece, visit, 0)

    @pl.when(step == last)
    def _():
        pl.when(out_of_range(total_ref[0]))(with_running_top)


def suffix_partials(
    queries, keys, values, new_keys, new_values, lengths, slot_row, after, span, kv, scale
):
    steps, _, heads, head_dim = queries.shape
    first, slots = span[0], span[1] - span[0]
    block = math.gcd(keys.shape[1], 4096)
    blocks = keys.shape[1] // block
    rows = steps * heads

    def cache_at(r, i, lengths, slot_row):
        last = (kv * lengths[slot_row[first + r]] - 1) // block
        return (first + r, jnp.minimum(i, last), 0)

    away = pl.BlockSpec(memory_space=pl.ANY)
    cache = pl.BlockSpec((1, block, head_dim), cache_at)
    fresh = pl.BlockSpec((steps, 1, kv, head_dim), lambda r, i, *_: (0, first + r, 0, 0))
    out = pl.BlockSpec((1, rows, LANES), lambda r, i, *_: (r, 0, 0))
    shape = jax.ShapeDtypeStruct((slots, rows, LANES), F32)
    return pl.pallas_call(
        functools.partial(suffix_kernel, kv, scale, first),
        grid_spec=pltpu.PrefetchScalarGridSpec(
            num_scalar_prefetch=2,
            grid=(slots, blocks),
            in_specs=[
                pl.BlockSpec((steps, 1, heads, head_dim), lambda r, i, *_: (0, first + r, 0, 0)),
                cache,
                cache,
                fresh,
                fresh,
                away,
                away,
                away,
            ],
            out_specs=[out] * 3,
            scratch_shapes=[
                pltpu.VMEM((2 * rows, 2 * head_dim), BF16),
                pltpu.VMEM((512, head_dim), BF16),
                pltpu.VMEM((512, head_dim), BF16),
            ],
        ),
        out_shape=[shape] * 3,
        compiler_params=pltpu.CompilerParams(
            dimension_semantics=("arbitrary", "arbitrary"), vmem_limit_bytes=60 * 1024 * 1024
        ),
        cost_estimate=pl.CostEstimate(
            flops=4 * slots * rows * keys.shape[1] * head_dim,
            bytes_accessed=4 * slots * keys.shape[1] * head_dim,
            transcendentals=slots * rows * keys.shape[1],
        ),
        name="suffix",
    )(lengths, slot_row, queries, keys, values, new_keys, new_values, keys, values, after)


def combine_kernel(kv, parts_ref, *refs):
    near, out_ref = refs[:-1], refs[-1]
    steps, slots, heads, _ = out_ref.shape
    group = heads // kv
    parts = [parts_ref[s].astype(F32) for s in range(parts_ref.shape[0])]
    for t in range(steps):
        for r in range(slots):
            done = []
            for h in range(kv):
                at = slice((t * slots + r) * group, (t * slots + r + 1) * group)
                own = slice((h * steps + t) * group, (h * steps + t + 1) * group)
                held, index = divmod(r, near[0].shape[0])
                sums, tops, totals = ([x[index, own]] for x in near[3 * held : 3 * held + 3])
                for p in parts:
                    stats = p[at, kv * LANES :]
                    shape = (group, LANES)
                    tops.append(jnp.broadcast_to(stats[:, h : h + 1], shape))
                    both = stats[:, 2 + h : 3 + h] + stats[:, 4 + h : 5 + h]
                    totals.append(jnp.broadcast_to(both, shape))
                    sums.append(p[at, h * LANES : (h + 1) * LANES])
                peak = functools.reduce(jnp.maximum, tops)
                factors = [jnp.exp2(m - peak) for m in tops]
                total = sum(f * x for f, x in zip(factors, totals))
                weighted = sum(f * x for f, x in zip(factors, sums))
                done.append(weighted / total)
            out_ref[t, r] = jnp.concatenate(done, axis=0).astype(BF16)


def combine(parts, near, kv, shape):
    return pl.pallas_call(
        functools.partial(combine_kernel, kv),
        out_shape=jax.ShapeDtypeStruct(shape, BF16),
        name="combine",
    )(parts, *near)


def per_device(
    sources,
    queries,
    prefix_keys,
    prefix_values,
    suffix_keys,
    suffix_values,
    new_keys,
    new_values,
    suffix_lengths,
    slot_row,
):
    head_dim = queries.shape[-1]
    kv = prefix_keys.shape[1]
    scale = LOG2E / math.sqrt(head_dim)
    interleaved = lambda x: x.reshape(*x.shape[:-3], x.shape[-3] * x.shape[-2], x.shape[-1])

    def exchange(x):
        return lax.all_to_all(x, "wide", 0, 0, tiled=True)

    everyone = exchange(jnp.broadcast_to(queries[None], (sources, *queries.shape)))
    own = (
        queries,
        interleaved(suffix_keys),
        interleaved(suffix_values),
        new_keys,
        new_values,
        suffix_lengths,
        slot_row,
    )
    slots = queries.shape[1]
    early = suffix_partials(*own, suffix_lengths, (0, slots // 2), kv, scale)
    partials = prompt_partials(everyone, interleaved(prefix_keys), interleaved(prefix_values), early[0], kv, scale)
    home = exchange(partials)
    late = suffix_partials(*own, partials, (slots // 2, slots), kv, scale)
    return combine(home, [*early, *late], kv, queries.shape)


def solution(mesh):
    placed = (
        P(None, "wide", "tensor", None),
        P("wide", "tensor", None),
        P("wide", "tensor", None),
        P("wide", None, "tensor", None),
        P("wide", None, "tensor", None),
        P(None, "wide", "tensor", None),
        P(None, "wide", "tensor", None),
        P(),
        P("wide"),
    )
    return jax.shard_map(
        functools.partial(per_device, mesh.shape["wide"]),
        mesh=mesh,
        in_specs=placed,
        out_specs=P(None, "wide", "tensor", None),
        check_vma=False,
    )
```

```python
import functools
import math

import jax
import jax.numpy as jnp
from jax import lax
from jax.experimental import pallas as pl
from jax.experimental.pallas import tpu as pltpu
from jax.sharding import PartitionSpec as P

LOG2E = 1.4426950408889634
LANES = 128
STEPS = 2
TILE, BAND, MAX_WAVE = 256, 64, 512
TOO_LARGE, TOO_SMALL = 2.0**100, 2.0**-60
F32 = jnp.float32
BF16 = jnp.bfloat16


def coarse(x):
    return jnp.floor(jnp.ceil(x) * 0.0625) * 16.0


def out_of_range(totals):
    return jnp.logical_not((jnp.max(totals) < TOO_LARGE) & (jnp.min(totals) > TOO_SMALL))


def lane_parity(rows):
    return lax.broadcasted_iota(jnp.int32, (rows, LANES), 1) % 2 == 0


def by_head(x, kv, even, reduce, neutral):
    if kv == 1:
        return jnp.broadcast_to(reduce(x, axis=1, keepdims=True), x.shape)
    first = reduce(jnp.where(even, x, neutral), axis=1, keepdims=True)
    second = reduce(jnp.where(even, neutral, x), axis=1, keepdims=True)
    return jnp.where(even, first, second)


def fold_lanes(x, op):
    parts = [x[:, at : at + LANES] for at in range(0, x.shape[1], LANES)]
    while len(parts) > 1:
        parts = [op(a, b) for a, b in zip(parts[::2], parts[1::2])] + parts[len(parts) & ~1 :]
    return parts[0]


def split_heads(x, kv):
    if kv == 1:
        return x
    assert kv == 2
    rows = x.shape[0]
    even = (lax.broadcasted_iota(jnp.int32, (16, LANES), 0) % 2 == 0).astype(F32).astype(BF16)
    tiles = x.reshape(rows // 16, 16, LANES)
    first = (tiles * even[None]).reshape(rows, LANES)
    second = (tiles * (1 - even)[None]).reshape(rows, LANES)
    return jnp.concatenate([first, second], axis=1)


def scores_of(q, keys):
    return lax.dot_general(q, keys, (((1,), (1,)), ((), ())), preferred_element_type=F32)


def spread(m, columns):
    return jnp.concatenate([m] * (columns // LANES), axis=1)


def pad_lanes(x):
    if x.shape[1] == 2 * LANES:
        return x
    return jnp.concatenate([x, jnp.zeros_like(x)], axis=1)


def prompt_kernel(kv, piece, scale, *refs):
    q_hbm, k_hbm, v_hbm, _, out_ref = refs[:5]
    q_in, q_all, k_all, v_all, top, total, acc, k_sem, v_sem = refs[5:]
    sources = q_in.shape[0]
    rows = q_all.shape[0]
    per = rows // sources
    group = q_in.shape[3] // kv
    even = lane_parity(rows)
    pieces = k_all.shape[0] // piece
    per_piece = piece // TILE
    tiles = pieces * per_piece
    wave = math.gcd(rows, MAX_WAVE)
    bands = wave // BAND

    def span(i):
        return pl.ds(pl.multiple_of(i * piece, piece), piece)

    def k_copy(i):
        return pltpu.make_async_copy(k_hbm.at[span(i), :], k_all.at[span(i), :], k_sem.at[i])

    def v_copy(i):
        return pltpu.make_async_copy(v_hbm.at[span(i), :], v_all.at[span(i), :], v_sem.at[i])

    def start(i, carry):
        k_copy(i).start()
        v_copy(i).start()
        return carry

    lax.fori_loop(0, pieces, start, 0)
    pltpu.sync_copy(q_hbm, q_in)
    for s in range(sources):
        q = q_in[s].astype(F32)
        steps, slots, _, _ = q.shape
        parts = [
            jnp.concatenate([q[t, r, h * group : (h + 1) * group] for h in range(kv)], axis=1)
            for t in range(steps)
            for r in range(slots)
        ]
        q_all[s * per : (s + 1) * per, :] = pad_lanes(jnp.concatenate(parts, axis=0)).astype(BF16)
    top[...] = jnp.zeros_like(top)
    total[...] = jnp.zeros_like(total)

    def tile_of(ref, t):
        at = pl.multiple_of(t * TILE, TILE)
        return pad_lanes(split_heads(ref[pl.ds(at, TILE), :], kv))

    def run_wave(base, first_wave):
        def band(b):
            return slice(base + b * BAND, base + (b + 1) * BAND)

        def push_keys(t, slot):
            pltpu.matmul_push_rhs(tile_of(k_all, t), slot, 0, transpose=True)

        def push_values(t, slot):
            pltpu.matmul_push_rhs(tile_of(v_all, t), slot, 1)

        def body(*accs):
            scores = (accs[:bands], accs[bands : 2 * bands])
            sums = accs[2 * bands :]
            if first_wave:
                k_copy(0).wait()
                v_copy(0).wait()
            push_keys(0, 0)
            for b in range(bands):
                pltpu.matmul_acc_lhs(scores[0][b], q_all[band(b), :], 0 if b == 0 else None)
            push_keys(1, 1)
            push_values(0, 0)

            def visit(p, carry):
                if first_wave:

                    @pl.when(p + 1 < pieces)
                    def _():
                        k_copy(p + 1).wait()
                        v_copy(p + 1).wait()

                for u in range(per_piece):
                    now, later = u % 2, 1 - u % 2
                    t = p * per_piece + u
                    for b in range(bands):
                        first = b == 0
                        pltpu.matmul_acc_lhs(
                            scores[later][b], q_all[band(b), :], later if first else None
                        )
                        if b == bands // 2:
                            push_keys(jnp.minimum(t + 2, tiles - 1), now)
                            push_values(jnp.minimum(t + 1, tiles - 1), later)
                        w = jnp.exp2(pltpu.matmul_pop(scores[now][b]) * scale)
                        total[band(b), :] += fold_lanes(w, jnp.add)
                        pltpu.matmul_acc_lhs(sums[b], w.astype(BF16), now if first else None)
                return carry

            lax.fori_loop(0, pieces, visit, 0)
            for b in range(bands):
                acc[band(b), :] = pltpu.matmul_pop(sums[b])
            for b in range(bands):
                pltpu.matmul_pop(scores[0][b])
            pltpu.matmul_acc_lhs(scores[1][0], q_all[band(0), :], 1)
            pltpu.matmul_pop(scores[1][0])
            pltpu.matmul_acc_lhs(sums[0], q_all[band(0), :], 0)
            pltpu.matmul_pop(sums[0])

        shape = (BAND, 2 * LANES)
        pl.run_scoped(
            body, *[pltpu.ACC(0)(shape, F32)] * (2 * bands), *[pltpu.ACC(1)(shape, F32)] * bands
        )

    for base in range(0, rows, wave):
        run_wave(base, base == 0)

    def with_running_top():
        top[...] = jnp.full_like(top, -jnp.inf)
        total[...] = jnp.zeros_like(total)
        acc[...] = jnp.zeros_like(acc)

        def body(scores, weighted):
            def visit(t, carry):
                pltpu.matmul_push_rhs(tile_of(k_all, t), 0, 0, transpose=True)
                pltpu.matmul_push_rhs(tile_of(v_all, t), 0, 1)
                for at in range(0, rows, BAND):
                    band, load = slice(at, at + BAND), 0 if at == 0 else None
                    pltpu.matmul_acc_lhs(scores, q_all[band, :], load)
                    s = pltpu.matmul_pop(scores) * scale
                    best = fold_lanes(s, jnp.maximum)
                    peak = by_head(best, kv, even[band], jnp.max, -jnp.inf)
                    new_top = jnp.maximum(top[band, :], coarse(peak))
                    shrink = jnp.exp2(top[band, :] - new_top)
                    top[band, :] = new_top
                    w = jnp.exp2(s - spread(new_top, TILE))
                    total[band, :] = total[band, :] * shrink + fold_lanes(w, jnp.add)
                    pltpu.matmul_acc_lhs(weighted, w.astype(BF16), load)
                    shrinks = [jnp.broadcast_to(shrink[:, h : h + 1], best.shape) for h in range(2)]
                    kept = acc[band, :] * jnp.concatenate(shrinks, axis=1)
                    acc[band, :] = kept + pltpu.matmul_pop(weighted)
                return carry

            lax.fori_loop(0, tiles, visit, 0)

        shape = (BAND, 2 * LANES)
        pl.run_scoped(body, pltpu.ACC(0)(shape, F32), pltpu.ACC(1)(shape, F32))

    sums = by_head(total[...], kv, even, jnp.sum, 0.0)
    total[...] = sums

    @pl.when(out_of_range(sums))
    def _():
        with_running_top()
        total[...] = by_head(total[...], kv, even, jnp.sum, 0.0)

    kind = lax.broadcasted_iota(jnp.int32, (rows, LANES), 1) // 2
    sums = total[...]
    high = sums.astype(BF16).astype(F32)
    stats = jnp.where(kind == 0, top[...], jnp.where(kind == 1, high, sums - high))
    for s in range(sources):
        at = slice(s * per, (s + 1) * per)
        out_ref[s, :, : kv * LANES] = acc[at, : kv * LANES].astype(BF16)
        out_ref[s, :, kv * LANES :] = stats[at, :].astype(BF16)


def prompt_partials(queries, keys, values, after, kv, scale):
    sources, steps, slots, heads, head_dim = queries.shape
    per = steps * slots * (heads // kv)
    rows = sources * per
    piece = math.gcd(keys.shape[0], 4 * TILE)
    away = pl.BlockSpec(memory_space=pl.ANY)
    return pl.pallas_call(
        functools.partial(prompt_kernel, kv, piece, scale),
        in_specs=[away] * 4,
        out_shape=jax.ShapeDtypeStruct((sources, per, (kv + 1) * LANES), BF16),
        scratch_shapes=[
            pltpu.VMEM(queries.shape, BF16),
            pltpu.VMEM((rows, 2 * LANES), BF16),
            pltpu.VMEM(keys.shape, BF16),
            pltpu.VMEM(values.shape, BF16),
            pltpu.VMEM((rows, LANES), F32),
            pltpu.VMEM((rows, LANES), F32),
            pltpu.VMEM((rows, 2 * LANES), F32),
            pltpu.SemaphoreType.DMA((keys.shape[0] // piece,)),
            pltpu.SemaphoreType.DMA((keys.shape[0] // piece,)),
        ],
        compiler_params=pltpu.CompilerParams(vmem_limit_bytes=60 * 1024 * 1024),
        cost_estimate=pl.CostEstimate(
            flops=8 * rows * keys.shape[0] * head_dim,
            bytes_accessed=4 * keys.shape[0] * head_dim,
            transcendentals=rows * keys.shape[0],
        ),
        name="prompt",
    )(queries, keys, values, after)


def suffix_kernel(kv, scale, first, lengths, slots, *refs):
    q_ref, k_ref, v_ref, nk_ref, nv_ref, k_hbm, v_hbm, _ = refs[:8]
    acc_ref, top_ref, total_ref, q_all, k_buf, v_buf = refs[8:]
    slot, step = pl.program_id(0) + first, pl.program_id(1)
    last = pl.num_programs(1) - 1
    group = q_ref.shape[2] // kv
    length = kv * lengths[slots[slot]]
    block = k_ref.shape[1]
    rows = kv * STEPS * group
    head = lax.broadcasted_iota(jnp.int32, (rows, LANES), 0) // (STEPS * group)
    lane = lax.broadcasted_iota(jnp.int32, (rows, LANES), 1)
    foreign = jnp.where(lane % kv == head, 0.0, -jnp.inf)

    def fresh(relative):
        row = lax.broadcasted_iota(jnp.int32, (rows, LANES), 0)
        second_head = row >= STEPS * group
        second_step = (row // group) % 2 == 1
        scores, values = [], []
        for j in range(STEPS):
            nk, nv = nk_ref[j, 0].astype(F32), nv_ref[j, 0].astype(F32)
            key = jnp.where(second_head, nk[kv - 1 : kv], nk[0:1])
            values.append(jnp.where(second_head, nv[kv - 1 : kv], nv[0:1]))
            q = q_all[:rows, :LANES].astype(F32)
            s = jnp.sum(q * key, axis=1, keepdims=True) * scale
            scores.append(jnp.broadcast_to(s, (rows, LANES)))
        scores[1] = jnp.where(second_step, scores[1], -jnp.inf)
        peak = jnp.ceil(jnp.maximum(scores[0], scores[1])) if relative else jnp.zeros_like(scores[0])
        weights = [jnp.exp2(s - peak) for s in scores]
        top_ref[0] = peak
        total_ref[0] = weights[0] + weights[1]
        acc_ref[0] = sum(w.astype(BF16).astype(F32) * v for w, v in zip(weights, values))

    @pl.when(step == 0)
    def _():
        q = [q_ref[t, 0].astype(F32) for t in range(STEPS)]
        wide = jnp.concatenate(
            [q[t][h * group : (h + 1) * group] for h in range(kv) for t in range(STEPS)], axis=0
        )
        none = jnp.zeros_like(wide)
        q_all[...] = jnp.concatenate(
            [jnp.concatenate([wide, none], axis=1), jnp.concatenate([none, wide], axis=1)], axis=0
        ).astype(BF16)
        fresh(False)

    def attend(partial):
        half = block // 2
        keys = jnp.concatenate([k_ref[0, :half], k_ref[0, half:]], axis=1)
        values = jnp.concatenate([v_ref[0, :half], v_ref[0, half:]], axis=1)
        bias = spread(jnp.concatenate([foreign, foreign], axis=0), half)
        s = scores_of(q_all[...], keys) * scale + bias
        if partial:
            at = lax.broadcasted_iota(jnp.int32, s.shape, 1)
            at += jnp.where(lax.broadcasted_iota(jnp.int32, s.shape, 0) >= rows, half, 0)
            s = jnp.where(at < length - step * block, s, -jnp.inf)
        w = jnp.exp2(s)
        sums = jnp.sum(fold_lanes(w, jnp.add), axis=1, keepdims=True)
        total_ref[0] += jnp.broadcast_to(sums[:rows] + sums[rows:], (rows, LANES))
        out = jnp.dot(w.astype(BF16), values, preferred_element_type=F32)
        acc_ref[0] += out[:rows, :LANES] + out[rows:, LANES:]

    pl.when((step + 1) * block <= length)(lambda: attend(False))
    pl.when((step * block < length) & ((step + 1) * block > length))(lambda: attend(True))

    def with_running_top():
        fresh(True)
        piece = k_buf.shape[0]

        def visit(i, carry):
            begin = pl.multiple_of(i * piece, piece)
            pltpu.sync_copy(k_hbm.at[slot, pl.ds(begin, piece), :], k_buf)
            pltpu.sync_copy(v_hbm.at[slot, pl.ds(begin, piece), :], v_buf)
            s = scores_of(q_all[:rows, :LANES], k_buf[...]) * scale + spread(foreign, piece)
            at = lax.broadcasted_iota(jnp.int32, s.shape, 1)
            s = jnp.where(at < length - begin, s, -jnp.inf)
            old = top_ref[0]
            peak = jnp.max(fold_lanes(s, jnp.maximum), axis=1, keepdims=True)
            new_top = jnp.maximum(old, jnp.ceil(peak))
            shrink = jnp.exp2(old - new_top)
            w = jnp.exp2(s - spread(new_top, piece))
            top_ref[0] = new_top
            total_ref[0] = total_ref[0] * shrink + jnp.sum(
                fold_lanes(w, jnp.add), axis=1, keepdims=True
            )
            acc_ref[0] = acc_ref[0] * shrink + jnp.dot(
                w.astype(BF16), v_buf[...], preferred_element_type=F32
            )
            return carry

        lax.fori_loop(0, (length + piece - 1) // piece, visit, 0)

    @pl.when(step == last)
    def _():
        pl.when(out_of_range(total_ref[0]))(with_running_top)


def suffix_partials(
    queries, keys, values, new_keys, new_values, lengths, slot_row, after, span, kv, scale
):
    steps, _, heads, head_dim = queries.shape
    first, slots = span[0], span[1] - span[0]
    block = math.gcd(keys.shape[1], 4096)
    blocks = keys.shape[1] // block
    rows = steps * heads

    def cache_at(r, i, lengths, slot_row):
        last = (kv * lengths[slot_row[first + r]] - 1) // block
        return (first + r, jnp.minimum(i, last), 0)

    away = pl.BlockSpec(memory_space=pl.ANY)
    cache = pl.BlockSpec((1, block, head_dim), cache_at)
    fresh = pl.BlockSpec((steps, 1, kv, head_dim), lambda r, i, *_: (0, first + r, 0, 0))
    out = pl.BlockSpec((1, rows, LANES), lambda r, i, *_: (r, 0, 0))
    shape = jax.ShapeDtypeStruct((slots, rows, LANES), F32)
    return pl.pallas_call(
        functools.partial(suffix_kernel, kv, scale, first),
        grid_spec=pltpu.PrefetchScalarGridSpec(
            num_scalar_prefetch=2,
            grid=(slots, blocks),
            in_specs=[
                pl.BlockSpec((steps, 1, heads, head_dim), lambda r, i, *_: (0, first + r, 0, 0)),
                cache,
                cache,
                fresh,
                fresh,
                away,
                away,
                away,
            ],
            out_specs=[out] * 3,
            scratch_shapes=[
                pltpu.VMEM((2 * rows, 2 * head_dim), BF16),
                pltpu.VMEM((512, head_dim), BF16),
                pltpu.VMEM((512, head_dim), BF16),
            ],
        ),
        out_shape=[shape] * 3,
        compiler_params=pltpu.CompilerParams(
            dimension_semantics=("arbitrary", "arbitrary"), vmem_limit_bytes=60 * 1024 * 1024
        ),
        cost_estimate=pl.CostEstimate(
            flops=4 * slots * rows * keys.shape[1] * head_dim,
            bytes_accessed=4 * slots * keys.shape[1] * head_dim,
            transcendentals=slots * rows * keys.shape[1],
        ),
        name="suffix",
    )(lengths, slot_row, queries, keys, values, new_keys, new_values, keys, values, after)


def combine_kernel(kv, parts_ref, *refs):
    near, out_ref = refs[:-1], refs[-1]
    steps, slots, heads, _ = out_ref.shape
    group = heads // kv
    parts = [parts_ref[s].astype(F32) for s in range(parts_ref.shape[0])]
    for t in range(steps):
        for r in range(slots):
            done = []
            for h in range(kv):
                at = slice((t * slots + r) * group, (t * slots + r + 1) * group)
                own = slice((h * steps + t) * group, (h * steps + t + 1) * group)
                held, index = divmod(r, near[0].shape[0])
                sums, tops, totals = ([x[index, own]] for x in near[3 * held : 3 * held + 3])
                for p in parts:
                    stats = p[at, kv * LANES :]
                    shape = (group, LANES)
                    tops.append(jnp.broadcast_to(stats[:, h : h + 1], shape))
                    both = stats[:, 2 + h : 3 + h] + stats[:, 4 + h : 5 + h]
                    totals.append(jnp.broadcast_to(both, shape))
                    sums.append(p[at, h * LANES : (h + 1) * LANES])
                peak = functools.reduce(jnp.maximum, tops)
                factors = [jnp.exp2(m - peak) for m in tops]
                total = sum(f * x for f, x in zip(factors, totals))
                weighted = sum(f * x for f, x in zip(factors, sums))
                done.append(weighted / total)
            out_ref[t, r] = jnp.concatenate(done, axis=0).astype(BF16)


def combine(parts, near, kv, shape):
    return pl.pallas_call(
        functools.partial(combine_kernel, kv),
        out_shape=jax.ShapeDtypeStruct(shape, BF16),
        name="combine",
    )(parts, *near)


def per_device(
    sources,
    queries,
    prefix_keys,
    prefix_values,
    suffix_keys,
    suffix_values,
    new_keys,
    new_values,
    suffix_lengths,
    slot_row,
):
    head_dim = queries.shape[-1]
    kv = prefix_keys.shape[1]
    scale = LOG2E / math.sqrt(head_dim)
    interleaved = lambda x: x.reshape(*x.shape[:-3], x.shape[-3] * x.shape[-2], x.shape[-1])

    def exchange(x):
        return lax.all_to_all(x, "wide", 0, 0, tiled=True)

    everyone = exchange(jnp.broadcast_to(queries[None], (sources, *queries.shape)))
    own = (
        queries,
        interleaved(suffix_keys),
        interleaved(suffix_values),
        new_keys,
        new_values,
        suffix_lengths,
        slot_row,
    )
    slots = queries.shape[1]
    early = suffix_partials(*own, suffix_lengths, (0, slots // 2), kv, scale)
    partials = prompt_partials(everyone, interleaved(prefix_keys), interleaved(prefix_values), early[0], kv, scale)
    home = exchange(partials)
    late = suffix_partials(*own, partials, (slots // 2, slots), kv, scale)
    return combine(home, [*early, *late], kv, queries.shape)


def solution(mesh):
    placed = (
        P(None, "wide", "tensor", None),
        P("wide", "tensor", None),
        P("wide", "tensor", None),
        P("wide", None, "tensor", None),
        P("wide", None, "tensor", None),
        P(None, "wide", "tensor", None),
        P(None, "wide", "tensor", None),
        P(),
        P("wide"),
    )
    return jax.shard_map(
        functools.partial(per_device, mesh.shape["wide"]),
        mesh=mesh,
        in_specs=placed,
        out_specs=P(None, "wide", "tensor", None),
        check_vma=False,
    )
```

```python
import functools
import math

import jax
import jax.numpy as jnp
from jax import lax
from jax.experimental import pallas as pl
from jax.experimental.pallas import tpu as pltpu
from jax.sharding import PartitionSpec as P

LOG2E = 1.4426950408889634
LANES = 128
STEPS = 2
TILE, BAND, MAX_WAVE = 256, 64, 1024
TOO_LARGE, TOO_SMALL = 2.0**100, 2.0**-60
F32 = jnp.float32
BF16 = jnp.bfloat16


def coarse(x):
    return jnp.floor(jnp.ceil(x) * 0.0625) * 16.0


def out_of_range(totals):
    return jnp.logical_not((jnp.max(totals) < TOO_LARGE) & (jnp.min(totals) > TOO_SMALL))


def fold_lanes(x, op):
    parts = [x[:, at : at + LANES] for at in range(0, x.shape[1], LANES)]
    while len(parts) > 1:
        parts = [op(a, b) for a, b in zip(parts[::2], parts[1::2])] + parts[len(parts) & ~1 :]
    return parts[0]


def scores_of(q, keys):
    return lax.dot_general(q, keys, (((1,), (1,)), ((), ())), preferred_element_type=F32)


def spread(m, columns):
    return jnp.concatenate([m] * (columns // LANES), axis=1)


def pad_lanes(x):
    if x.shape[1] == 2 * LANES:
        return x
    return jnp.concatenate([x, jnp.zeros_like(x)], axis=1)


def row_reduce(x, reduce):
    return jnp.broadcast_to(reduce(x, axis=1, keepdims=True), x.shape)


def prompt_kernel(kv, piece, scale, *refs):
    q_in, k_hbm, v_hbm, _, out_ref = refs[:5]
    q_all, k_all, v_all, k_wide, v_wide, top, total, acc, k_sem, v_sem = refs[5:]
    sources = q_in.shape[0]
    rows = q_all.shape[0]
    rows_head = rows // kv
    per = rows_head // sources
    group = q_in.shape[3] // kv
    pieces = k_all.shape[0] // piece
    tile_rows = kv * TILE
    per_piece = piece // tile_rows
    tiles = pieces * per_piece
    wave = math.gcd(rows, MAX_WAVE)
    bands = wave // BAND

    def span(i):
        return pl.ds(pl.multiple_of(i * piece, piece), piece)

    def k_copy(i):
        return pltpu.make_async_copy(k_hbm.at[span(i), :], k_all.at[span(i), :], k_sem.at[i])

    def v_copy(i):
        return pltpu.make_async_copy(v_hbm.at[span(i), :], v_all.at[span(i), :], v_sem.at[i])

    def start(i, carry):
        k_copy(i).start()
        v_copy(i).start()
        return carry

    lax.fori_loop(0, pieces, start, 0)
    for s in range(sources):
        q = q_in[s].astype(F32)
        steps, slots, _, _ = q.shape
        for h in range(kv):
            part = jnp.concatenate(
                [
                    q[t, r, h * group : (h + 1) * group]
                    for t in range(steps)
                    for r in range(slots)
                ],
                axis=0,
            )
            none = jnp.zeros_like(part)
            halves = [part, none] if h == 0 else [none, part]
            at = h * rows_head + s * per
            q_all[at : at + per, :] = jnp.concatenate(halves, axis=1).astype(BF16)
    top[...] = jnp.zeros_like(top)
    total[...] = jnp.zeros_like(total)

    def tile_of(ref, wide, t):
        rows_in = ref[pl.ds(pl.multiple_of(t * tile_rows, tile_rows), tile_rows), :]
        if kv == 1:
            return pad_lanes(rows_in)
        assert kv == 2
        wide[...] = rows_in.astype(F32)
        heads = [wide[pl.ds(h, TILE, stride=kv), :] for h in range(kv)]
        return jnp.concatenate(heads, axis=1).astype(BF16)

    def run_wave(base, first_wave):
        def band(b):
            return slice(base + b * BAND, base + (b + 1) * BAND)

        def push_keys(t, slot):
            pltpu.matmul_push_rhs(tile_of(k_all, k_wide.at[slot], t), slot, 0, transpose=True)

        def push_values(t, slot):
            pltpu.matmul_push_rhs(tile_of(v_all, v_wide.at[slot], t), slot, 1)

        def body(*accs):
            scores, sums = accs[:bands], accs[bands:]
            if first_wave:
                k_copy(0).wait()
                v_copy(0).wait()
            push_keys(0, 0)
            for b in range(bands):
                pltpu.matmul_acc_lhs(scores[b], q_all[band(b), :], 0 if b == 0 else None)
            push_keys(1, 1)
            push_values(0, 0)

            def visit(p, carry):
                if first_wave:

                    @pl.when(p + 1 < pieces)
                    def _():
                        k_copy(p + 1).wait()
                        v_copy(p + 1).wait()

                for u in range(per_piece):
                    now, later = u % 2, 1 - u % 2
                    t = p * per_piece + u
                    for b in range(bands):
                        first = b == 0
                        w = jnp.exp2(pltpu.matmul_pop(scores[b]) * scale)
                        pltpu.matmul_acc_lhs(
                            scores[b], q_all[band(b), :], later if first else None
                        )
                        if b == bands // 2:
                            push_keys(jnp.minimum(t + 2, tiles - 1), now)
                            push_values(jnp.minimum(t + 1, tiles - 1), later)
                        total[band(b), :] += fold_lanes(w, jnp.add)
                        pltpu.matmul_acc_lhs(sums[b], w.astype(BF16), now if first else None)
                return carry

            lax.fori_loop(0, pieces, visit, 0)
            for b in range(bands):
                acc[band(b), :] = pltpu.matmul_pop(sums[b])
            for b in range(bands):
                pltpu.matmul_pop(scores[b])
            pltpu.matmul_acc_lhs(scores[0], q_all[band(0), :], 1)
            pltpu.matmul_pop(scores[0])
            pltpu.matmul_acc_lhs(sums[0], q_all[band(0), :], 0)
            pltpu.matmul_pop(sums[0])

        shape = (BAND, 2 * LANES)
        pl.run_scoped(body, *[pltpu.ACC(u)(shape, F32) for u in range(2) for _ in range(bands)])

    for base in range(0, rows, wave):
        run_wave(base, base == 0)

    def with_running_top():
        top[...] = jnp.full_like(top, -jnp.inf)
        total[...] = jnp.zeros_like(total)
        acc[...] = jnp.zeros_like(acc)

        def body(scores, weighted):
            def visit(t, carry):
                pltpu.matmul_push_rhs(tile_of(k_all, k_wide.at[0], t), 0, 0, transpose=True)
                pltpu.matmul_push_rhs(tile_of(v_all, v_wide.at[0], t), 0, 1)
                for at in range(0, rows, BAND):
                    band, load = slice(at, at + BAND), 0 if at == 0 else None
                    pltpu.matmul_acc_lhs(scores, q_all[band, :], load)
                    s = pltpu.matmul_pop(scores) * scale
                    peak = row_reduce(fold_lanes(s, jnp.maximum), jnp.max)
                    new_top = jnp.maximum(top[band, :], coarse(peak))
                    shrink = jnp.exp2(top[band, :] - new_top)
                    top[band, :] = new_top
                    w = jnp.exp2(s - spread(new_top, TILE))
                    total[band, :] = total[band, :] * shrink + fold_lanes(w, jnp.add)
                    pltpu.matmul_acc_lhs(weighted, w.astype(BF16), load)
                    kept = acc[band, :] * spread(shrink, 2 * LANES)
                    acc[band, :] = kept + pltpu.matmul_pop(weighted)
                return carry

            lax.fori_loop(0, tiles, visit, 0)

        shape = (BAND, 2 * LANES)
        pl.run_scoped(body, pltpu.ACC(0)(shape, F32), pltpu.ACC(1)(shape, F32))

    sums = row_reduce(total[...], jnp.sum)
    total[...] = sums

    @pl.when(out_of_range(sums))
    def _():
        with_running_top()
        total[...] = row_reduce(total[...], jnp.sum)

    lane = lax.broadcasted_iota(jnp.int32, (per, LANES), 1)
    for s in range(sources):
        stats = jnp.zeros((per, LANES), F32)
        for h in range(kv):
            at = slice(h * rows_head + s * per, h * rows_head + (s + 1) * per)
            half = slice(h * LANES, (h + 1) * LANES)
            out_ref[s, :, half] = acc[at, half].astype(BF16)
            sums = total[at, :]
            high = sums.astype(BF16).astype(F32)
            stats = jnp.where(lane == h, top[at, :], stats)
            stats = jnp.where(lane == 2 + h, high, stats)
            stats = jnp.where(lane == 4 + h, sums - high, stats)
        out_ref[s, :, kv * LANES :] = stats.astype(BF16)


def prompt_partials(queries, keys, values, after, kv, scale):
    sources, steps, slots, heads, head_dim = queries.shape
    per = steps * slots * (heads // kv)
    rows = sources * per * kv
    piece = math.gcd(keys.shape[0], 2 * kv * TILE)
    away = pl.BlockSpec(memory_space=pltpu.HBM)
    inside = pl.BlockSpec(memory_space=pltpu.VMEM)
    return pl.pallas_call(
        functools.partial(prompt_kernel, kv, piece, scale),
        in_specs=[inside, away, away, pl.BlockSpec(memory_space=pl.ANY)],
        out_shape=jax.ShapeDtypeStruct((sources, per, (kv + 1) * LANES), BF16),
        scratch_shapes=[
            pltpu.VMEM((rows, 2 * LANES), BF16),
            pltpu.VMEM(keys.shape, BF16),
            pltpu.VMEM(values.shape, BF16),
            pltpu.VMEM((2, kv * TILE, LANES), F32),
            pltpu.VMEM((2, kv * TILE, LANES), F32),
            pltpu.VMEM((rows, LANES), F32),
            pltpu.VMEM((rows, LANES), F32),
            pltpu.VMEM((rows, 2 * LANES), F32),
            pltpu.SemaphoreType.DMA((keys.shape[0] // piece,)),
            pltpu.SemaphoreType.DMA((keys.shape[0] // piece,)),
        ],
        compiler_params=pltpu.CompilerParams(vmem_limit_bytes=58 * 1024 * 1024),
        cost_estimate=pl.CostEstimate(
            flops=4 * rows * keys.shape[0] * head_dim,
            bytes_accessed=4 * keys.shape[0] * head_dim,
            transcendentals=rows * keys.shape[0] // kv,
        ),
        name="prompt",
    )(queries, keys, values, after)


def suffix_kernel(kv, scale, first, lengths, slots, *refs):
    q_ref, nk_ref, nv_ref, k_hbm, v_hbm, _ = refs[:6]
    acc_ref, top_ref, total_ref, q_all, scores, k_all, v_all, k_sem, v_sem = refs[6:]
    count, rows, _ = acc_ref.shape
    group = q_ref.shape[2] // kv
    pieces = k_sem.shape[1]
    piece = k_all.shape[1] // pieces
    half = piece // 2
    used = [kv * lengths[slots[first + r]] for r in range(count)]
    ends, end = [], 0
    for r in range(count):
        end = end + (used[r] + piece - 1) // piece
        ends.append(end)

    def place(i):
        slot, begin, length = 0, 0, used[0]
        for r in range(1, count):
            past = i >= ends[r - 1]
            slot = jnp.where(past, r, slot)
            begin = jnp.where(past, ends[r - 1], begin)
            length = jnp.where(past, used[r], length)
        return slot, i - begin, length

    def span(at):
        return pl.ds(pl.multiple_of(at * piece, piece), piece)

    def k_copy(slot, at):
        return pltpu.make_async_copy(
            k_hbm.at[first + slot, span(at), :], k_all.at[slot, span(at), :], k_sem.at[slot, at]
        )

    def v_copy(slot, at):
        return pltpu.make_async_copy(
            v_hbm.at[first + slot, span(at), :], v_all.at[slot, span(at), :], v_sem.at[slot, at]
        )

    def start(i, carry):
        slot, at, _ = place(i)
        k_copy(slot, at).start()
        v_copy(slot, at).start()
        return carry

    lax.fori_loop(0, end, start, 0)

    head = lax.broadcasted_iota(jnp.int32, (rows, LANES), 0) // (STEPS * group)
    lane = lax.broadcasted_iota(jnp.int32, (rows, LANES), 1)
    foreign = jnp.where(lane % kv == head, 0.0, -jnp.inf)

    def fresh(slot, relative):
        row = lax.broadcasted_iota(jnp.int32, (rows, LANES), 0)
        second_head = row >= STEPS * group
        second_step = (row // group) % 2 == 1
        own, values = [], []
        for j in range(STEPS):
            nk, nv = nk_ref[j, first + slot].astype(F32), nv_ref[j, first + slot].astype(F32)
            key = jnp.where(second_head, nk[kv - 1 : kv], nk[0:1])
            values.append(jnp.where(second_head, nv[kv - 1 : kv], nv[0:1]))
            q = q_all[slot, :rows, :LANES].astype(F32)
            s = jnp.sum(q * key, axis=1, keepdims=True) * scale
            own.append(jnp.broadcast_to(s, (rows, LANES)))
        own[1] = jnp.where(second_step, own[1], -jnp.inf)
        peak = jnp.ceil(jnp.maximum(own[0], own[1])) if relative else jnp.zeros_like(own[0])
        weights = [jnp.exp2(s - peak) for s in own]
        top_ref[slot] = peak
        total_ref[slot] = weights[0] + weights[1]
        acc_ref[slot] = sum(w.astype(BF16).astype(F32) * v for w, v in zip(weights, values))

    for r in range(count):
        q = [q_ref[t, first + r].astype(F32) for t in range(STEPS)]
        wide = jnp.concatenate(
            [q[t][h * group : (h + 1) * group] for h in range(kv) for t in range(STEPS)], axis=0
        )
        none = jnp.zeros_like(wide)
        q_all[r] = jnp.concatenate(
            [jnp.concatenate([wide, none], axis=1), jnp.concatenate([none, wide], axis=1)], axis=0
        ).astype(BF16)
        fresh(r, False)

    def halves(ref, slot, at):
        begin = pl.multiple_of(at * piece, piece)
        parts = [ref[slot, pl.ds(begin, half), :], ref[slot, pl.ds(begin + half, half), :]]
        return jnp.concatenate(parts, axis=1)

    def score(i):
        slot, at, _ = place(i)
        k_copy(slot, at).wait()
        scores[...] = scores_of(q_all[slot], halves(k_all, slot, at))

    score(0)

    def visit(i, carry):
        slot, at, length = place(i)
        v_copy(slot, at).wait()
        column = lax.broadcasted_iota(jnp.int32, scores.shape, 1)
        column += jnp.where(lax.broadcasted_iota(jnp.int32, scores.shape, 0) >= rows, half, 0)
        bias = spread(jnp.concatenate([foreign, foreign], axis=0), half)
        s = jnp.where(column < length - at * piece, scores[...] * scale + bias, -jnp.inf)
        pl.when(i + 1 < end)(lambda: score(i + 1))
        w = jnp.exp2(s)
        sums = jnp.sum(fold_lanes(w, jnp.add), axis=1, keepdims=True)
        total_ref[slot] += jnp.broadcast_to(sums[:rows] + sums[rows:], (rows, LANES))
        out = jnp.dot(w.astype(BF16), halves(v_all, slot, at), preferred_element_type=F32)
        acc_ref[slot] += out[:rows, :LANES] + out[rows:, LANES:]
        return carry

    lax.fori_loop(0, end, visit, 0)

    def with_running_top(slot):
        fresh(slot, True)
        some = 512

        def visit(i, carry):
            begin = pl.multiple_of(i * some, some)
            keys, values = k_all[slot, pl.ds(begin, some), :], v_all[slot, pl.ds(begin, some), :]
            s = scores_of(q_all[slot, :rows, :LANES], keys) * scale + spread(foreign, some)
            at = lax.broadcasted_iota(jnp.int32, s.shape, 1)
            s = jnp.where(at < used[slot] - begin, s, -jnp.inf)
            old = top_ref[slot]
            peak = jnp.max(fold_lanes(s, jnp.maximum), axis=1, keepdims=True)
            new_top = jnp.maximum(old, jnp.ceil(peak))
            shrink = jnp.exp2(old - new_top)
            w = jnp.exp2(s - spread(new_top, some))
            top_ref[slot] = new_top
            total_ref[slot] = total_ref[slot] * shrink + jnp.sum(
                fold_lanes(w, jnp.add), axis=1, keepdims=True
            )
            acc_ref[slot] = acc_ref[slot] * shrink + jnp.dot(
                w.astype(BF16), values, preferred_element_type=F32
            )
            return carry

        lax.fori_loop(0, (used[slot] + some - 1) // some, visit, 0)

    for r in range(count):
        pl.when(out_of_range(total_ref[r]))(functools.partial(with_running_top, r))


def suffix_partials(
    queries, keys, values, new_keys, new_values, lengths, slot_row, after, span, kv, scale
):
    steps, _, heads, head_dim = queries.shape
    first, count = span[0], span[1] - span[0]
    cached = keys.shape[1]
    piece = math.gcd(cached, 2048)
    rows = steps * heads
    scalars = pl.BlockSpec(memory_space=pltpu.SMEM)
    away = pl.BlockSpec(memory_space=pltpu.HBM)
    inside = pl.BlockSpec(memory_space=pltpu.VMEM)
    shape = jax.ShapeDtypeStruct((count, rows, LANES), F32)
    return pl.pallas_call(
        functools.partial(suffix_kernel, kv, scale, first),
        in_specs=[scalars, scalars, inside, inside, inside, away, away]
        + [pl.BlockSpec(memory_space=pl.ANY)],
        out_shape=[shape] * 3,
        scratch_shapes=[
            pltpu.VMEM((count, 2 * rows, 2 * head_dim), BF16),
            pltpu.VMEM((2 * rows, piece // 2), F32),
            pltpu.VMEM((count, cached, head_dim), BF16),
            pltpu.VMEM((count, cached, head_dim), BF16),
            pltpu.SemaphoreType.DMA((count, cached // piece)),
            pltpu.SemaphoreType.DMA((count, cached // piece)),
        ],
        compiler_params=pltpu.CompilerParams(vmem_limit_bytes=58 * 1024 * 1024),
        cost_estimate=pl.CostEstimate(
            flops=4 * count * rows * cached * head_dim,
            bytes_accessed=4 * count * cached * head_dim,
            transcendentals=count * rows * cached,
        ),
        name="suffix",
    )(lengths, slot_row, queries, new_keys, new_values, keys, values, after)


def combine_kernel(kv, parts_ref, *refs):
    near, out_ref = refs[:-1], refs[-1]
    steps, slots, heads, _ = out_ref.shape
    sources, per, _ = parts_ref.shape
    group = heads // kv
    width = kv * LANES

    wanted = lax.broadcasted_iota(jnp.int32, (LANES, 2 * width), 0)
    column = lax.broadcasted_iota(jnp.int32, (LANES, 2 * width), 1)
    head = (column % width) // LANES
    is_top = column < width
    picks = (is_top & (wanted == head)) | (
        jnp.logical_not(is_top) & ((wanted == 2 + head) | (wanted == 4 + head))
    )
    stats = parts_ref[:, :, width:].reshape(sources * per, LANES)
    stats = jnp.dot(stats, picks.astype(F32).astype(BF16), preferred_element_type=F32)

    def own(kind):
        rows = []
        for t in range(steps):
            for r in range(slots):
                held, index = divmod(r, near[0].shape[0])
                x = near[3 * held + kind]
                at = [(h * steps + t) * group for h in range(kv)]
                rows.append(jnp.concatenate([x[index, a : a + group] for a in at], axis=1))
        return jnp.concatenate(rows, axis=0)

    sums, tops, totals = [own(0)], [own(1)], [own(2)]
    for s in range(sources):
        sums.append(parts_ref[s, :, :width].astype(F32))
        tops.append(stats[s * per : (s + 1) * per, :width])
        totals.append(stats[s * per : (s + 1) * per, width:])
    peak = functools.reduce(jnp.maximum, tops)
    factors = [jnp.exp2(m - peak) for m in tops]
    total = sum(f * x for f, x in zip(factors, totals))
    done = sum(f * x for f, x in zip(factors, sums)) / total
    for t in range(steps):
        for r in range(slots):
            at = (t * slots + r) * group
            both = [done[at : at + group, h * LANES : (h + 1) * LANES] for h in range(kv)]
            out_ref[t, r] = jnp.concatenate(both, axis=0).astype(BF16)


def combine(parts, near, kv, shape):
    return pl.pallas_call(
        functools.partial(combine_kernel, kv),
        out_shape=jax.ShapeDtypeStruct(shape, BF16),
        compiler_params=pltpu.CompilerParams(vmem_limit_bytes=16 * 1024 * 1024),
        name="combine",
    )(parts, *near)


def per_device(
    sources,
    queries,
    prefix_keys,
    prefix_values,
    suffix_keys,
    suffix_values,
    new_keys,
    new_values,
    suffix_lengths,
    slot_row,
):
    head_dim = queries.shape[-1]
    kv = prefix_keys.shape[1]
    scale = LOG2E / math.sqrt(head_dim)
    interleaved = lambda x: x.reshape(*x.shape[:-3], x.shape[-3] * x.shape[-2], x.shape[-1])

    def exchange(x):
        return lax.all_to_all(x, "wide", 0, 0, tiled=True)

    everyone = exchange(jnp.broadcast_to(queries[None], (sources, *queries.shape)))
    own = (
        queries,
        interleaved(suffix_keys),
        interleaved(suffix_values),
        new_keys,
        new_values,
        suffix_lengths,
        slot_row,
    )
    slots = queries.shape[1]
    early = suffix_partials(*own, suffix_lengths, (0, slots // 2), kv, scale)
    partials = prompt_partials(everyone, interleaved(prefix_keys), interleaved(prefix_values), early[0], kv, scale)
    home = exchange(partials)
    late = suffix_partials(*own, partials, (slots // 2, slots), kv, scale)
    return combine(home, [*early, *late], kv, queries.shape)


def solution(mesh):
    placed = (
        P(None, "wide", "tensor", None),
        P("wide", "tensor", None),
        P("wide", "tensor", None),
        P("wide", None, "tensor", None),
        P("wide", None, "tensor", None),
        P(None, "wide", "tensor", None),
        P(None, "wide", "tensor", None),
        P(),
        P("wide"),
    )
    return jax.shard_map(
        functools.partial(per_device, mesh.shape["wide"]),
        mesh=mesh,
        in_specs=placed,
        out_specs=P(None, "wide", "tensor", None),
        check_vma=False,
    )
```

```python
import functools
import math

import jax
import jax.numpy as jnp
from jax import lax
from jax.experimental import pallas as pl
from jax.experimental.pallas import tpu as pltpu
from jax.sharding import PartitionSpec as P

LOG2E = 1.4426950408889634
LANES = 128
STEPS = 2
TILE, BAND, MAX_WAVE, STATS = 256, 64, 1024, 16
GRANT = 57 * 1024 * 1024
TOO_LARGE, TOO_SMALL = 2.0**100, 2.0**-60
F32 = jnp.float32
BF16 = jnp.bfloat16


def coarse(x):
    return jnp.floor(jnp.ceil(x) * 0.0625) * 16.0


def out_of_range(totals):
    return jnp.logical_not((jnp.max(totals) < TOO_LARGE) & (jnp.min(totals) > TOO_SMALL))


def fold_lanes(x, op):
    parts = [x[:, at : at + LANES] for at in range(0, x.shape[1], LANES)]
    while len(parts) > 1:
        parts = [op(a, b) for a, b in zip(parts[::2], parts[1::2])] + parts[len(parts) & ~1 :]
    return parts[0]


def scores_of(q, keys):
    return lax.dot_general(q, keys, (((1,), (1,)), ((), ())), preferred_element_type=F32)


def spread(m, columns):
    return jnp.concatenate([m] * (columns // LANES), axis=1)


def prompt_kernel(kv, piece, scale, *refs):
    q_in, k_hbm, v_hbm, _, out_ref = refs[:5]
    q_all, k_all, v_all, k_wide, v_wide, top, acc, k_sem, v_sem = refs[5:]
    sources = q_in.shape[0]
    rows = q_all.shape[0]
    rows_head = rows // kv
    per = rows_head // sources
    group = q_in.shape[3] // kv
    pieces = k_all.shape[0] // piece
    tile_rows = kv * TILE
    per_piece = piece // tile_rows
    tiles = pieces * per_piece
    wave = math.gcd(rows_head, MAX_WAVE // kv)
    bands = wave // BAND

    def span(i):
        return pl.ds(pl.multiple_of(i * piece, piece), piece)

    def k_copy(i):
        return pltpu.make_async_copy(k_hbm.at[span(i), :], k_all.at[span(i), :], k_sem.at[i])

    def v_copy(i):
        return pltpu.make_async_copy(v_hbm.at[span(i), :], v_all.at[span(i), :], v_sem.at[i])

    def start(i, carry):
        k_copy(i).start()
        v_copy(i).start()
        return carry

    lax.fori_loop(0, pieces, start, 0)

    for s in range(sources):
        q = q_in[s].astype(F32) * scale
        steps, slots, _, _ = q.shape
        for h in range(kv):
            heads = slice(h * group, (h + 1) * group)
            part = [q[t, r, heads] for t in range(steps) for r in range(slots)]
            part = jnp.concatenate(part, axis=0)
            high = part.astype(BF16)
            low = (part - high.astype(F32)).astype(BF16)
            at = h * rows_head + s * per
            q_all[at : at + per, :] = jnp.concatenate([high, low], axis=1)
    top[...] = jnp.zeros_like(top)

    def widen(ref, wide, t):
        rows_in = ref[pl.ds(pl.multiple_of(t * tile_rows, tile_rows), tile_rows), :]
        wide[...] = rows_in.astype(F32)

    def head_of(wide, h):
        return wide[pl.ds(h, TILE, stride=kv), :].astype(BF16)

    def push_keys(h):
        keys = head_of(k_wide, h)
        pltpu.matmul_push_rhs(jnp.concatenate([keys, keys], axis=1), h, 0, transpose=True)

    def push_values(h):
        values = head_of(v_wide, h)
        pltpu.matmul_push_rhs(jnp.concatenate([values, jnp.ones_like(values)], axis=1), h, 1)

    def run_wave(base, first_wave):
        every = [(h, b) for h in range(kv) for b in range(bands)]

        def band(h, b):
            at = h * rows_head + base + b * BAND
            return slice(at, at + BAND)

        def body(*accs):
            scores = dict(zip(every, accs[: kv * bands]))
            sums = dict(zip(every, accs[kv * bands :]))
            if first_wave:
                k_copy(0).wait()
                v_copy(0).wait()
            widen(k_all, k_wide, 0)
            for h in range(kv):
                push_keys(h)
            for h, b in every:
                load = h if b == 0 else None
                pltpu.matmul_acc_lhs(scores[h, b], q_all[band(h, b), :], load)
            widen(k_all, k_wide, 1)
            widen(v_all, v_wide, 0)
            for h in range(kv):
                push_keys(h)
                push_values(h)

            def visit(p, carry):
                if first_wave:

                    @pl.when(p + 1 < pieces)
                    def _():
                        k_copy(p + 1).wait()
                        v_copy(p + 1).wait()

                for u in range(per_piece):
                    t = p * per_piece + u
                    widen(k_all, k_wide, jnp.minimum(t + 2, tiles - 1))
                    widen(v_all, v_wide, jnp.minimum(t + 1, tiles - 1))
                    for h, b in every:
                        load = h if b == 0 else None
                        w = jnp.exp2(pltpu.matmul_pop(scores[h, b]))
                        pltpu.matmul_acc_lhs(scores[h, b], q_all[band(h, b), :], load)
                        pltpu.matmul_acc_lhs(sums[h, b], w.astype(BF16), load)
                        if b == bands // 2:
                            push_keys(h)
                            push_values(h)
                return carry

            lax.fori_loop(0, pieces, visit, 0)
            for at in every:
                acc[band(*at), :] = pltpu.matmul_pop(sums[at])
            for at in every:
                pltpu.matmul_pop(scores[at])
            for held in (scores[0, 0], sums[0, 0]):
                for h in range(kv):
                    pltpu.matmul_acc_lhs(held, q_all[:BAND, :], h)
                pltpu.matmul_pop(held)

        shape = (BAND, 2 * LANES)
        pl.run_scoped(body, *[pltpu.ACC(u)(shape, F32) for u in range(2) for _ in every])

    for base in range(0, rows_head, wave):
        run_wave(base, base == 0)

    def with_running_top():
        top[...] = jnp.full_like(top, -jnp.inf)
        acc[...] = jnp.zeros_like(acc)

        def body(scores, weighted):
            def visit(t, carry):
                widen(k_all, k_wide, t)
                widen(v_all, v_wide, t)
                for h in range(kv):
                    push_keys(h)
                    push_values(h)
                for at in range(0, rows, BAND):
                    band = slice(at, at + BAND)
                    load = at // rows_head if at % rows_head == 0 else None
                    pltpu.matmul_acc_lhs(scores, q_all[band, :], load)
                    s = pltpu.matmul_pop(scores)
                    peak = jnp.max(fold_lanes(s, jnp.maximum), axis=1, keepdims=True)
                    new_top = jnp.maximum(top[band, :], coarse(peak))
                    shrink = jnp.exp2(top[band, :] - new_top)
                    top[band, :] = new_top
                    w = jnp.exp2(s - spread(new_top, TILE))
                    pltpu.matmul_acc_lhs(weighted, w.astype(BF16), load)
                    kept = acc[band, :] * spread(shrink, 2 * LANES)
                    acc[band, :] = kept + pltpu.matmul_pop(weighted)
                return carry

            lax.fori_loop(0, tiles, visit, 0)

        shape = (BAND, 2 * LANES)
        pl.run_scoped(body, pltpu.ACC(0)(shape, F32), pltpu.ACC(1)(shape, F32))

    pl.when(out_of_range(acc[:, LANES:]))(with_running_top)

    def as_rows(x):
        rest = jnp.zeros((LANES - per, LANES), F32)
        return jnp.concatenate([x, rest], axis=0).T[:STATS]

    row = lax.broadcasted_iota(jnp.int32, (STATS, LANES), 0)
    for s in range(sources):
        stats = jnp.zeros((STATS, LANES), F32)
        for h in range(kv):
            at = slice(h * rows_head + s * per, h * rows_head + (s + 1) * per)
            out_ref[s, :per, h * LANES : (h + 1) * LANES] = acc[at, :LANES].astype(BF16)
            sums = as_rows(acc[at, LANES:])
            high = sums.astype(BF16).astype(F32)
            stats = jnp.where(row == h, as_rows(top[at, :]), stats)
            stats = jnp.where(row == 2 + h, high, stats)
            stats = jnp.where(row == 4 + h, sums - high, stats)
        rest = [jnp.zeros_like(stats)] * (kv - 1)
        out_ref[s, per:, :] = jnp.concatenate([stats, *rest], axis=1).astype(BF16)


def prompt_partials(queries, keys, values, after, kv, scale):
    sources, steps, slots, heads, head_dim = queries.shape
    per = steps * slots * (heads // kv)
    assert kv <= 2 and per <= LANES and per % BAND == 0
    rows = sources * per * kv
    piece = math.gcd(keys.shape[0], 4 * kv * TILE)
    away = pl.BlockSpec(memory_space=pl.ANY)
    inside = pl.BlockSpec(memory_space=pltpu.VMEM)
    return pl.pallas_call(
        functools.partial(prompt_kernel, kv, piece, scale),
        in_specs=[inside, away, away, away],
        out_shape=jax.ShapeDtypeStruct((sources, per + STATS, kv * LANES), BF16),
        scratch_shapes=[
            pltpu.VMEM((rows, 2 * LANES), BF16),
            pltpu.VMEM(keys.shape, BF16),
            pltpu.VMEM(values.shape, BF16),
            pltpu.VMEM((kv * TILE, LANES), F32),
            pltpu.VMEM((kv * TILE, LANES), F32),
            pltpu.VMEM((rows, LANES), F32),
            pltpu.VMEM((rows, 2 * LANES), F32),
            pltpu.SemaphoreType.DMA((keys.shape[0] // piece,)),
            pltpu.SemaphoreType.DMA((keys.shape[0] // piece,)),
        ],
        compiler_params=pltpu.CompilerParams(vmem_limit_bytes=GRANT),
        cost_estimate=pl.CostEstimate(
            flops=4 * rows * keys.shape[0] * head_dim,
            bytes_accessed=4 * keys.shape[0] * head_dim,
            transcendentals=rows * keys.shape[0] // kv,
        ),
        name="prompt",
    )(queries, keys, values, after)


def suffix_kernel(kv, scale, first, lengths, slots, *refs):
    q_ref, nk_ref, nv_ref, k_hbm, v_hbm, _ = refs[:6]
    near_ref, q_all, scores, k_all, v_all, k_sem, v_sem = refs[6:]
    acc_ref, top_ref, total_ref = (near_ref.at[i] for i in range(3))
    _, count, rows, _ = near_ref.shape
    group = q_ref.shape[2] // kv
    pieces = k_sem.shape[1]
    piece = k_all.shape[1] // pieces
    half = piece // 2
    used = [kv * lengths[slots[first + r]] for r in range(count)]
    ends, end = [], 0
    for r in range(count):
        end = end + (used[r] + piece - 1) // piece
        ends.append(end)

    def place(i):
        slot, begin, length = 0, 0, used[0]
        for r in range(1, count):
            past = i >= ends[r - 1]
            slot = jnp.where(past, r, slot)
            begin = jnp.where(past, ends[r - 1], begin)
            length = jnp.where(past, used[r], length)
        return slot, i - begin, length

    def span(at):
        return pl.ds(pl.multiple_of(at * piece, piece), piece)

    def k_copy(slot, at):
        return pltpu.make_async_copy(
            k_hbm.at[first + slot, span(at), :], k_all.at[slot, span(at), :], k_sem.at[slot, at]
        )

    def v_copy(slot, at):
        return pltpu.make_async_copy(
            v_hbm.at[first + slot, span(at), :], v_all.at[slot, span(at), :], v_sem.at[slot, at]
        )

    def start(i, carry):
        slot, at, _ = place(i)
        k_copy(slot, at).start()
        v_copy(slot, at).start()
        return carry

    lax.fori_loop(0, end, start, 0)

    head = lax.broadcasted_iota(jnp.int32, (rows, LANES), 0) // (STEPS * group)
    lane = lax.broadcasted_iota(jnp.int32, (rows, LANES), 1)
    foreign = jnp.where(lane % kv == head, 0.0, -jnp.inf)

    def fresh(slot, relative):
        row = lax.broadcasted_iota(jnp.int32, (rows, LANES), 0)
        second_head = row >= STEPS * group
        second_step = (row // group) % 2 == 1
        own, values = [], []
        for j in range(STEPS):
            nk, nv = nk_ref[j, first + slot].astype(F32), nv_ref[j, first + slot].astype(F32)
            key = jnp.where(second_head, nk[kv - 1 : kv], nk[0:1])
            values.append(jnp.where(second_head, nv[kv - 1 : kv], nv[0:1]))
            q = q_all[slot, :rows, :LANES].astype(F32)
            s = jnp.sum(q * key, axis=1, keepdims=True) * scale
            own.append(jnp.broadcast_to(s, (rows, LANES)))
        own[1] = jnp.where(second_step, own[1], -jnp.inf)
        peak = jnp.ceil(jnp.maximum(own[0], own[1])) if relative else jnp.zeros_like(own[0])
        weights = [jnp.exp2(s - peak) for s in own]
        top_ref[slot] = peak
        total_ref[slot] = weights[0] + weights[1]
        acc_ref[slot] = sum(w.astype(BF16).astype(F32) * v for w, v in zip(weights, values))

    for r in range(count):
        q = [q_ref[t, first + r].astype(F32) for t in range(STEPS)]
        wide = jnp.concatenate(
            [q[t][h * group : (h + 1) * group] for h in range(kv) for t in range(STEPS)], axis=0
        )
        none = jnp.zeros_like(wide)
        q_all[r] = jnp.concatenate(
            [jnp.concatenate([wide, none], axis=1), jnp.concatenate([none, wide], axis=1)], axis=0
        ).astype(BF16)
        fresh(r, False)

    def halves(ref, slot, at):
        begin = pl.multiple_of(at * piece, piece)
        parts = [ref[slot, pl.ds(begin, half), :], ref[slot, pl.ds(begin + half, half), :]]
        return jnp.concatenate(parts, axis=1)

    def score(i):
        slot, at, _ = place(i)
        k_copy(slot, at).wait()
        scores[...] = scores_of(q_all[slot], halves(k_all, slot, at))

    score(0)

    def visit(i, carry):
        slot, at, length = place(i)
        v_copy(slot, at).wait()
        column = lax.broadcasted_iota(jnp.int32, scores.shape, 1)
        column += jnp.where(lax.broadcasted_iota(jnp.int32, scores.shape, 0) >= rows, half, 0)
        bias = spread(jnp.concatenate([foreign, foreign], axis=0), half)
        s = jnp.where(column < length - at * piece, scores[...] * scale + bias, -jnp.inf)
        pl.when(i + 1 < end)(lambda: score(i + 1))
        w = jnp.exp2(s)
        sums = jnp.sum(fold_lanes(w, jnp.add), axis=1, keepdims=True)
        total_ref[slot] += jnp.broadcast_to(sums[:rows] + sums[rows:], (rows, LANES))
        out = jnp.dot(w.astype(BF16), halves(v_all, slot, at), preferred_element_type=F32)
        acc_ref[slot] += out[:rows, :LANES] + out[rows:, LANES:]
        return carry

    lax.fori_loop(0, end, visit, 0)

    def with_running_top(slot):
        fresh(slot, True)
        some = 512

        def visit(i, carry):
            begin = pl.multiple_of(i * some, some)
            keys, values = k_all[slot, pl.ds(begin, some), :], v_all[slot, pl.ds(begin, some), :]
            s = scores_of(q_all[slot, :rows, :LANES], keys) * scale + spread(foreign, some)
            at = lax.broadcasted_iota(jnp.int32, s.shape, 1)
            s = jnp.where(at < used[slot] - begin, s, -jnp.inf)
            old = top_ref[slot]
            peak = jnp.max(fold_lanes(s, jnp.maximum), axis=1, keepdims=True)
            new_top = jnp.maximum(old, jnp.ceil(peak))
            shrink = jnp.exp2(old - new_top)
            w = jnp.exp2(s - spread(new_top, some))
            top_ref[slot] = new_top
            total_ref[slot] = total_ref[slot] * shrink + jnp.sum(
                fold_lanes(w, jnp.add), axis=1, keepdims=True
            )
            acc_ref[slot] = acc_ref[slot] * shrink + jnp.dot(
                w.astype(BF16), values, preferred_element_type=F32
            )
            return carry

        lax.fori_loop(0, (used[slot] + some - 1) // some, visit, 0)

    for r in range(count):
        pl.when(out_of_range(total_ref[r]))(functools.partial(with_running_top, r))


def suffix_partials(
    queries, keys, values, new_keys, new_values, lengths, slot_row, after, span, kv, scale
):
    steps, _, heads, head_dim = queries.shape
    first, count = span[0], span[1] - span[0]
    cached = keys.shape[1]
    piece = math.gcd(cached, 2048)
    rows = steps * heads
    scalars = pl.BlockSpec(memory_space=pltpu.SMEM)
    away = pl.BlockSpec(memory_space=pl.ANY)
    inside = pl.BlockSpec(memory_space=pltpu.VMEM)
    shape = jax.ShapeDtypeStruct((3, count, rows, LANES), F32)
    return pl.pallas_call(
        functools.partial(suffix_kernel, kv, scale, first),
        in_specs=[scalars, scalars, inside, inside, inside, away, away, away],
        out_shape=shape,
        scratch_shapes=[
            pltpu.VMEM((count, 2 * rows, 2 * head_dim), BF16),
            pltpu.VMEM((2 * rows, piece // 2), F32),
            pltpu.VMEM((count, cached, head_dim), BF16),
            pltpu.VMEM((count, cached, head_dim), BF16),
            pltpu.SemaphoreType.DMA((count, cached // piece)),
            pltpu.SemaphoreType.DMA((count, cached // piece)),
        ],
        compiler_params=pltpu.CompilerParams(vmem_limit_bytes=GRANT),
        cost_estimate=pl.CostEstimate(
            flops=4 * count * rows * cached * head_dim,
            bytes_accessed=4 * count * cached * head_dim,
            transcendentals=count * rows * cached,
        ),
        name="suffix",
    )(lengths, slot_row, queries, new_keys, new_values, keys, values, after)


def combine_kernel(kv, parts_ref, *refs):
    near, out_ref = refs[:-1], refs[-1]
    steps, slots, heads, _ = out_ref.shape
    sources, height, width = parts_ref.shape
    per = height - STATS
    group = heads // kv

    wanted = lax.broadcasted_iota(jnp.int32, (STATS, 2 * width), 0)
    column = lax.broadcasted_iota(jnp.int32, (STATS, 2 * width), 1)
    head = (column % width) // LANES
    is_top = column < width
    picks = (is_top & (wanted == head)) | (
        jnp.logical_not(is_top) & ((wanted == 2 + head) | (wanted == 4 + head))
    )
    stats = jnp.concatenate([parts_ref[s, per:, :LANES] for s in range(sources)], axis=1)
    stats = lax.dot_general(
        stats,
        picks.astype(F32).astype(BF16),
        (((0,), (0,)), ((), ())),
        preferred_element_type=F32,
    )

    def own(kind):
        rows = []
        for t in range(steps):
            for r in range(slots):
                held, index = divmod(r, near[0].shape[1])
                x = near[held]
                at = [(h * steps + t) * group for h in range(kv)]
                rows.append(jnp.concatenate([x[kind, index, a : a + group] for a in at], axis=1))
        return jnp.concatenate(rows, axis=0)

    sums, tops, totals = [own(0)], [own(1)], [own(2)]
    for s in range(sources):
        at = slice(s * LANES, s * LANES + per)
        sums.append(parts_ref[s, :per, :].astype(F32))
        tops.append(stats[at, :width])
        totals.append(stats[at, width:])
    peak = functools.reduce(jnp.maximum, tops)
    factors = [jnp.exp2(m - peak) for m in tops]
    total = sum(f * x for f, x in zip(factors, totals))
    done = sum(f * x for f, x in zip(factors, sums)) / total
    for t in range(steps):
        for r in range(slots):
            at = (t * slots + r) * group
            both = [done[at : at + group, h * LANES : (h + 1) * LANES] for h in range(kv)]
            out_ref[t, r] = jnp.concatenate(both, axis=0).astype(BF16)


def combine(parts, near, kv, shape):
    return pl.pallas_call(
        functools.partial(combine_kernel, kv),
        out_shape=jax.ShapeDtypeStruct(shape, BF16),
        compiler_params=pltpu.CompilerParams(vmem_limit_bytes=16 * 1024 * 1024),
        name="combine",
    )(parts, *near)


def per_device(
    sources,
    queries,
    prefix_keys,
    prefix_values,
    suffix_keys,
    suffix_values,
    new_keys,
    new_values,
    suffix_lengths,
    slot_row,
):
    head_dim = queries.shape[-1]
    kv = prefix_keys.shape[1]
    scale = LOG2E / math.sqrt(head_dim)
    interleaved = lambda x: x.reshape(*x.shape[:-3], x.shape[-3] * x.shape[-2], x.shape[-1])

    def exchange(x):
        return lax.all_to_all(x, "wide", 0, 0, tiled=True)

    everyone = exchange(jnp.broadcast_to(queries[None], (sources, *queries.shape)))
    own = (
        queries,
        interleaved(suffix_keys),
        interleaved(suffix_values),
        new_keys,
        new_values,
        suffix_lengths,
        slot_row,
    )
    slots = queries.shape[1]
    early = suffix_partials(*own, suffix_lengths, (0, slots // 2), kv, scale)
    partials = prompt_partials(everyone, interleaved(prefix_keys), interleaved(prefix_values), early, kv, scale)
    home = exchange(partials)
    late = suffix_partials(*own, partials, (slots // 2, slots), kv, scale)
    return combine(home, [early, late], kv, queries.shape)


def solution(mesh):
    placed = (
        P(None, "wide", "tensor", None),
        P("wide", "tensor", None),
        P("wide", "tensor", None),
        P("wide", None, "tensor", None),
        P("wide", None, "tensor", None),
        P(None, "wide", "tensor", None),
        P(None, "wide", "tensor", None),
        P(),
        P("wide"),
    )
    return jax.shard_map(
        functools.partial(per_device, mesh.shape["wide"]),
        mesh=mesh,
        in_specs=placed,
        out_specs=P(None, "wide", "tensor", None),
        check_vma=False,
    )
```

```python
import functools
import math

import jax
import jax.numpy as jnp
from jax import lax
from jax.experimental import pallas as pl
from jax.experimental.pallas import tpu as pltpu
from jax.sharding import PartitionSpec as P

LOG2E = 1.4426950408889634
LANES = 128
STEPS = 2
TILE, BAND, MAX_WAVE, STATS = 256, 64, 1024, 16
GRANT = 50 * 1024 * 1024
TOO_LARGE, TOO_SMALL = 2.0**100, 2.0**-60
F32 = jnp.float32
BF16 = jnp.bfloat16


def coarse(x):
    return jnp.floor(jnp.ceil(x) * 0.0625) * 16.0


def out_of_range(totals):
    return jnp.logical_not((jnp.max(totals) < TOO_LARGE) & (jnp.min(totals) > TOO_SMALL))


def fold_lanes(x, op):
    parts = [x[:, at : at + LANES] for at in range(0, x.shape[1], LANES)]
    while len(parts) > 1:
        parts = [op(a, b) for a, b in zip(parts[::2], parts[1::2])] + parts[len(parts) & ~1 :]
    return parts[0]


def scores_of(q, keys):
    return lax.dot_general(q, keys, (((1,), (1,)), ((), ())), preferred_element_type=F32)


def spread(m, columns):
    return jnp.concatenate([m] * (columns // LANES), axis=1)


def prompt_kernel(kv, piece, scale, *refs):
    q_in, k_hbm, v_hbm, _, out_ref = refs[:5]
    q_all, k_all, v_all, k_wide, v_wide, k_ready, v_ready, top, acc, k_sem, v_sem = refs[5:]
    sources = q_in.shape[0]
    rows = q_all.shape[0]
    rows_head = rows // kv
    per = rows_head // sources
    group = q_in.shape[3] // kv
    pieces = k_all.shape[0] // piece
    tile_rows = kv * TILE
    per_piece = piece // tile_rows
    tiles = pieces * per_piece
    wave = math.gcd(rows_head, MAX_WAVE // kv)
    bands = wave // BAND

    def span(i):
        return pl.ds(pl.multiple_of(i * piece, piece), piece)

    def k_copy(i):
        return pltpu.make_async_copy(k_hbm.at[span(i), :], k_all.at[span(i), :], k_sem.at[i])

    def v_copy(i):
        return pltpu.make_async_copy(v_hbm.at[span(i), :], v_all.at[span(i), :], v_sem.at[i])

    def start(i, carry):
        k_copy(i).start()
        v_copy(i).start()
        return carry

    lax.fori_loop(0, pieces, start, 0)

    for s in range(sources):
        q = q_in[s].astype(F32) * scale
        steps, slots, _, _ = q.shape
        for h in range(kv):
            heads = slice(h * group, (h + 1) * group)
            scaled = [q[t, r, heads] for t in range(steps) for r in range(slots)]
            scaled = jnp.concatenate(scaled, axis=0)
            high = scaled.astype(BF16)
            low = (scaled - high.astype(F32)).astype(BF16)
            at = h * rows_head + s * per
            q_all[at : at + per, :] = jnp.concatenate([high, low], axis=1)
    top[...] = jnp.zeros_like(top)

    def widen(ref, wide, t):
        at = pl.multiple_of(jnp.minimum(t, tiles - 1) * tile_rows, tile_rows)
        wide[...] = ref[pl.ds(at, tile_rows), :].astype(F32)

    def part(wide, ready, slot, h):
        ready[slot, h] = wide[pl.ds(h, TILE, stride=kv), :].astype(BF16)

    def prepare(ref, wide, ready, t, slot):
        widen(ref, wide, t)
        for h in range(kv):
            part(wide, ready, slot, h)

    def push_keys(slot, h):
        keys = k_ready[slot, h]
        pltpu.matmul_push_rhs(jnp.concatenate([keys, keys], axis=1), h, 0, transpose=True)

    def push_values(slot, h):
        values = v_ready[slot, h]
        pltpu.matmul_push_rhs(jnp.concatenate([values, jnp.ones_like(values)], axis=1), h, 1)

    def run_wave(base, first_wave):
        every = [(h, b) for h in range(kv) for b in range(bands)]

        def band(h, b):
            at = h * rows_head + base + b * BAND
            return slice(at, at + BAND)

        def body(*accs):
            scores = dict(zip(every, accs[: kv * bands]))
            sums = dict(zip(every, accs[kv * bands :]))
            if first_wave:
                k_copy(0).wait()
                v_copy(0).wait()
            prepare(k_all, k_wide, k_ready, 0, 0)
            for h in range(kv):
                push_keys(0, h)
            for h, b in every:
                load = h if b == 0 else None
                pltpu.matmul_acc_lhs(scores[h, b], q_all[band(h, b), :], load)
            prepare(k_all, k_wide, k_ready, 1, 1)
            prepare(v_all, v_wide, v_ready, 0, 0)
            for h in range(kv):
                push_keys(1, h)
                push_values(0, h)
            prepare(k_all, k_wide, k_ready, 2, 0)
            prepare(v_all, v_wide, v_ready, 1, 1)

            def visit(p, carry):
                if first_wave:

                    @pl.when(p + 1 < pieces)
                    def _():
                        k_copy(p + 1).wait()
                        v_copy(p + 1).wait()

                for u in range(per_piece):
                    t = p * per_piece + u
                    now, later = u % 2, 1 - u % 2
                    widen(k_all, k_wide, t + 3)
                    widen(v_all, v_wide, t + 2)
                    for h, b in every:
                        load = h if b == 0 else None
                        w = jnp.exp2(pltpu.matmul_pop(scores[h, b]))
                        pltpu.matmul_acc_lhs(scores[h, b], q_all[band(h, b), :], load)
                        pltpu.matmul_acc_lhs(sums[h, b], w.astype(BF16), load)
                        if b == bands // 2:
                            push_keys(now, h)
                            push_values(later, h)
                            part(k_wide, k_ready, later, h)
                            part(v_wide, v_ready, now, h)
                return carry

            lax.fori_loop(0, pieces, visit, 0)
            for at in every:
                acc[band(*at), :] = pltpu.matmul_pop(sums[at])
            for at in every:
                pltpu.matmul_pop(scores[at])
            for held in (scores[0, 0], sums[0, 0]):
                for h in range(kv):
                    pltpu.matmul_acc_lhs(held, q_all[:BAND, :], h)
                pltpu.matmul_pop(held)

        shape = (BAND, 2 * LANES)
        pl.run_scoped(body, *[pltpu.ACC(u)(shape, F32) for u in range(2) for _ in every])

    for base in range(0, rows_head, wave):
        run_wave(base, base == 0)

    def with_running_top():
        top[...] = jnp.full_like(top, -jnp.inf)
        acc[...] = jnp.zeros_like(acc)

        def body(scores, weighted):
            def visit(t, carry):
                prepare(k_all, k_wide, k_ready, t, 0)
                prepare(v_all, v_wide, v_ready, t, 0)
                for h in range(kv):
                    push_keys(0, h)
                    push_values(0, h)
                for at in range(0, rows, BAND):
                    band = slice(at, at + BAND)
                    load = at // rows_head if at % rows_head == 0 else None
                    pltpu.matmul_acc_lhs(scores, q_all[band, :], load)
                    s = pltpu.matmul_pop(scores)
                    peak = jnp.max(fold_lanes(s, jnp.maximum), axis=1, keepdims=True)
                    new_top = jnp.maximum(top[band, :], coarse(peak))
                    shrink = jnp.exp2(top[band, :] - new_top)
                    top[band, :] = new_top
                    w = jnp.exp2(s - spread(new_top, TILE))
                    pltpu.matmul_acc_lhs(weighted, w.astype(BF16), load)
                    kept = acc[band, :] * spread(shrink, 2 * LANES)
                    acc[band, :] = kept + pltpu.matmul_pop(weighted)
                return carry

            lax.fori_loop(0, tiles, visit, 0)

        shape = (BAND, 2 * LANES)
        pl.run_scoped(body, pltpu.ACC(0)(shape, F32), pltpu.ACC(1)(shape, F32))

    pl.when(out_of_range(acc[:, LANES:]))(with_running_top)

    def as_rows(x):
        rest = jnp.zeros((LANES - per, LANES), F32)
        return jnp.concatenate([x, rest], axis=0).T[:STATS]

    row = lax.broadcasted_iota(jnp.int32, (STATS, LANES), 0)
    for s in range(sources):
        stats = jnp.zeros((STATS, LANES), F32)
        for h in range(kv):
            at = slice(h * rows_head + s * per, h * rows_head + (s + 1) * per)
            out_ref[s, :per, h * LANES : (h + 1) * LANES] = acc[at, :LANES].astype(BF16)
            sums = as_rows(acc[at, LANES:])
            high = sums.astype(BF16).astype(F32)
            stats = jnp.where(row == h, as_rows(top[at, :]), stats)
            stats = jnp.where(row == 2 + h, high, stats)
            stats = jnp.where(row == 4 + h, sums - high, stats)
        rest = [jnp.zeros_like(stats)] * (kv - 1)
        out_ref[s, per:, :] = jnp.concatenate([stats, *rest], axis=1).astype(BF16)


def prompt_partials(queries, keys, values, after, kv, scale):
    sources, steps, slots, heads, head_dim = queries.shape
    per = steps * slots * (heads // kv)
    assert kv <= 2 and per <= LANES and per % BAND == 0
    rows = sources * per * kv
    piece = math.gcd(keys.shape[0], 4 * kv * TILE)
    away = pl.BlockSpec(memory_space=pl.ANY)
    inside = pl.BlockSpec(memory_space=pltpu.VMEM)
    return pl.pallas_call(
        functools.partial(prompt_kernel, kv, piece, scale),
        in_specs=[inside, away, away, away],
        out_shape=jax.ShapeDtypeStruct((sources, per + STATS, kv * LANES), BF16),
        scratch_shapes=[
            pltpu.VMEM((rows, 2 * LANES), BF16),
            pltpu.VMEM(keys.shape, BF16),
            pltpu.VMEM(values.shape, BF16),
            pltpu.VMEM((kv * TILE, LANES), F32),
            pltpu.VMEM((kv * TILE, LANES), F32),
            pltpu.VMEM((2, kv, TILE, LANES), BF16),
            pltpu.VMEM((2, kv, TILE, LANES), BF16),
            pltpu.VMEM((rows, LANES), F32),
            pltpu.VMEM((rows, 2 * LANES), F32),
            pltpu.SemaphoreType.DMA((keys.shape[0] // piece,)),
            pltpu.SemaphoreType.DMA((keys.shape[0] // piece,)),
        ],
        compiler_params=pltpu.CompilerParams(vmem_limit_bytes=GRANT),
        cost_estimate=pl.CostEstimate(
            flops=4 * rows * keys.shape[0] * head_dim,
            bytes_accessed=4 * keys.shape[0] * head_dim,
            transcendentals=rows * keys.shape[0] // kv,
        ),
        name="prompt",
    )(queries, keys, values, after)


def suffix_kernel(kv, scale, first, lengths, slots, *refs):
    q_ref, nk_ref, nv_ref, k_hbm, v_hbm, _ = refs[:6]
    near_ref, q_all, scores, k_all, v_all, k_sem, v_sem = refs[6:]
    acc_ref, top_ref, total_ref = (near_ref.at[i] for i in range(3))
    _, count, rows, _ = near_ref.shape
    group = q_ref.shape[2] // kv
    pieces = k_sem.shape[1]
    piece = k_all.shape[1] // pieces
    half = piece // 2
    used = [kv * lengths[slots[first + r]] for r in range(count)]
    ends, end = [], 0
    for r in range(count):
        end = end + (used[r] + piece - 1) // piece
        ends.append(end)

    def place(i):
        slot, begin, length = 0, 0, used[0]
        for r in range(1, count):
            past = i >= ends[r - 1]
            slot = jnp.where(past, r, slot)
            begin = jnp.where(past, ends[r - 1], begin)
            length = jnp.where(past, used[r], length)
        return slot, i - begin, length

    def span(at):
        return pl.ds(pl.multiple_of(at * piece, piece), piece)

    def k_copy(slot, at):
        return pltpu.make_async_copy(
            k_hbm.at[first + slot, span(at), :], k_all.at[slot, span(at), :], k_sem.at[slot, at]
        )

    def v_copy(slot, at):
        return pltpu.make_async_copy(
            v_hbm.at[first + slot, span(at), :], v_all.at[slot, span(at), :], v_sem.at[slot, at]
        )

    def start(i, carry):
        slot, at, _ = place(i)
        k_copy(slot, at).start()
        v_copy(slot, at).start()
        return carry

    lax.fori_loop(0, end, start, 0)

    head = lax.broadcasted_iota(jnp.int32, (rows, LANES), 0) // (STEPS * group)
    lane = lax.broadcasted_iota(jnp.int32, (rows, LANES), 1)
    foreign = jnp.where(lane % kv == head, 0.0, -jnp.inf)

    def fresh(slot, relative):
        row = lax.broadcasted_iota(jnp.int32, (rows, LANES), 0)
        second_head = row >= STEPS * group
        second_step = (row // group) % 2 == 1
        own, values = [], []
        for j in range(STEPS):
            nk, nv = nk_ref[j, first + slot].astype(F32), nv_ref[j, first + slot].astype(F32)
            key = jnp.where(second_head, nk[kv - 1 : kv], nk[0:1])
            values.append(jnp.where(second_head, nv[kv - 1 : kv], nv[0:1]))
            q = q_all[slot, :rows, :LANES].astype(F32)
            s = jnp.sum(q * key, axis=1, keepdims=True) * scale
            own.append(jnp.broadcast_to(s, (rows, LANES)))
        own[1] = jnp.where(second_step, own[1], -jnp.inf)
        peak = jnp.ceil(jnp.maximum(own[0], own[1])) if relative else jnp.zeros_like(own[0])
        weights = [jnp.exp2(s - peak) for s in own]
        top_ref[slot] = peak
        total_ref[slot] = weights[0] + weights[1]
        acc_ref[slot] = sum(w.astype(BF16).astype(F32) * v for w, v in zip(weights, values))

    for r in range(count):
        q = [q_ref[t, first + r].astype(F32) for t in range(STEPS)]
        wide = jnp.concatenate(
            [q[t][h * group : (h + 1) * group] for h in range(kv) for t in range(STEPS)], axis=0
        )
        none = jnp.zeros_like(wide)
        q_all[r] = jnp.concatenate(
            [jnp.concatenate([wide, none], axis=1), jnp.concatenate([none, wide], axis=1)], axis=0
        ).astype(BF16)
        fresh(r, False)

    def halves(ref, slot, at):
        begin = pl.multiple_of(at * piece, piece)
        parts = [ref[slot, pl.ds(begin, half), :], ref[slot, pl.ds(begin + half, half), :]]
        return jnp.concatenate(parts, axis=1)

    def score(i):
        slot, at, _ = place(i)
        k_copy(slot, at).wait()
        scores[...] = scores_of(q_all[slot], halves(k_all, slot, at))

    score(0)

    def visit(i, carry):
        slot, at, length = place(i)
        v_copy(slot, at).wait()
        column = lax.broadcasted_iota(jnp.int32, scores.shape, 1)
        column += jnp.where(lax.broadcasted_iota(jnp.int32, scores.shape, 0) >= rows, half, 0)
        bias = spread(jnp.concatenate([foreign, foreign], axis=0), half)
        s = jnp.where(column < length - at * piece, scores[...] * scale + bias, -jnp.inf)
        pl.when(i + 1 < end)(lambda: score(i + 1))
        w = jnp.exp2(s)
        sums = jnp.sum(fold_lanes(w, jnp.add), axis=1, keepdims=True)
        total_ref[slot] += jnp.broadcast_to(sums[:rows] + sums[rows:], (rows, LANES))
        out = jnp.dot(w.astype(BF16), halves(v_all, slot, at), preferred_element_type=F32)
        acc_ref[slot] += out[:rows, :LANES] + out[rows:, LANES:]
        return carry

    lax.fori_loop(0, end, visit, 0)

    def with_running_top(slot):
        fresh(slot, True)
        some = 512

        def visit(i, carry):
            begin = pl.multiple_of(i * some, some)
            keys, values = k_all[slot, pl.ds(begin, some), :], v_all[slot, pl.ds(begin, some), :]
            s = scores_of(q_all[slot, :rows, :LANES], keys) * scale + spread(foreign, some)
            at = lax.broadcasted_iota(jnp.int32, s.shape, 1)
            s = jnp.where(at < used[slot] - begin, s, -jnp.inf)
            old = top_ref[slot]
            peak = jnp.max(fold_lanes(s, jnp.maximum), axis=1, keepdims=True)
            new_top = jnp.maximum(old, jnp.ceil(peak))
            shrink = jnp.exp2(old - new_top)
            w = jnp.exp2(s - spread(new_top, some))
            top_ref[slot] = new_top
            total_ref[slot] = total_ref[slot] * shrink + jnp.sum(
                fold_lanes(w, jnp.add), axis=1, keepdims=True
            )
            acc_ref[slot] = acc_ref[slot] * shrink + jnp.dot(
                w.astype(BF16), values, preferred_element_type=F32
            )
            return carry

        lax.fori_loop(0, (used[slot] + some - 1) // some, visit, 0)

    for r in range(count):
        pl.when(out_of_range(total_ref[r]))(functools.partial(with_running_top, r))


def suffix_partials(
    queries, keys, values, new_keys, new_values, lengths, slot_row, after, span, kv, scale
):
    steps, _, heads, head_dim = queries.shape
    first, count = span[0], span[1] - span[0]
    cached = keys.shape[1]
    piece = math.gcd(cached, 2048)
    rows = steps * heads
    scalars = pl.BlockSpec(memory_space=pltpu.SMEM)
    away = pl.BlockSpec(memory_space=pl.ANY)
    inside = pl.BlockSpec(memory_space=pltpu.VMEM)
    shape = jax.ShapeDtypeStruct((3, count, rows, LANES), F32)
    return pl.pallas_call(
        functools.partial(suffix_kernel, kv, scale, first),
        in_specs=[scalars, scalars, inside, inside, inside, away, away, away],
        out_shape=shape,
        scratch_shapes=[
            pltpu.VMEM((count, 2 * rows, 2 * head_dim), BF16),
            pltpu.VMEM((2 * rows, piece // 2), F32),
            pltpu.VMEM((count, cached, head_dim), BF16),
            pltpu.VMEM((count, cached, head_dim), BF16),
            pltpu.SemaphoreType.DMA((count, cached // piece)),
            pltpu.SemaphoreType.DMA((count, cached // piece)),
        ],
        compiler_params=pltpu.CompilerParams(vmem_limit_bytes=GRANT),
        cost_estimate=pl.CostEstimate(
            flops=4 * count * rows * cached * head_dim,
            bytes_accessed=4 * count * cached * head_dim,
            transcendentals=count * rows * cached,
        ),
        name="suffix",
    )(lengths, slot_row, queries, new_keys, new_values, keys, values, after)


def combine_kernel(kv, parts_ref, *refs):
    near, out_ref = refs[:-1], refs[-1]
    steps, slots, heads, _ = out_ref.shape
    sources, height, width = parts_ref.shape
    per = height - STATS
    group = heads // kv

    wanted = lax.broadcasted_iota(jnp.int32, (STATS, 2 * width), 0)
    column = lax.broadcasted_iota(jnp.int32, (STATS, 2 * width), 1)
    head = (column % width) // LANES
    is_top = column < width
    picks = (is_top & (wanted == head)) | (
        jnp.logical_not(is_top) & ((wanted == 2 + head) | (wanted == 4 + head))
    )
    stats = jnp.concatenate([parts_ref[s, per:, :LANES] for s in range(sources)], axis=1)
    stats = lax.dot_general(
        stats,
        picks.astype(F32).astype(BF16),
        (((0,), (0,)), ((), ())),
        preferred_element_type=F32,
    )

    def own(kind):
        rows = []
        for t in range(steps):
            for r in range(slots):
                held, index = divmod(r, near[0].shape[1])
                x = near[held]
                at = [(h * steps + t) * group for h in range(kv)]
                rows.append(jnp.concatenate([x[kind, index, a : a + group] for a in at], axis=1))
        return jnp.concatenate(rows, axis=0)

    sums, tops, totals = [own(0)], [own(1)], [own(2)]
    for s in range(sources):
        at = slice(s * LANES, s * LANES + per)
        sums.append(parts_ref[s, :per, :].astype(F32))
        tops.append(stats[at, :width])
        totals.append(stats[at, width:])
    peak = functools.reduce(jnp.maximum, tops)
    factors = [jnp.exp2(m - peak) for m in tops]
    total = sum(f * x for f, x in zip(factors, totals))
    done = sum(f * x for f, x in zip(factors, sums)) / total
    for t in range(steps):
        for r in range(slots):
            at = (t * slots + r) * group
            both = [done[at : at + group, h * LANES : (h + 1) * LANES] for h in range(kv)]
            out_ref[t, r] = jnp.concatenate(both, axis=0).astype(BF16)


def combine(parts, near, kv, shape):
    return pl.pallas_call(
        functools.partial(combine_kernel, kv),
        out_shape=jax.ShapeDtypeStruct(shape, BF16),
        compiler_params=pltpu.CompilerParams(vmem_limit_bytes=16 * 1024 * 1024),
        name="combine",
    )(parts, *near)


def per_device(
    sources,
    queries,
    prefix_keys,
    prefix_values,
    suffix_keys,
    suffix_values,
    new_keys,
    new_values,
    suffix_lengths,
    slot_row,
):
    head_dim = queries.shape[-1]
    kv = prefix_keys.shape[1]
    scale = LOG2E / math.sqrt(head_dim)
    interleaved = lambda x: x.reshape(*x.shape[:-3], x.shape[-3] * x.shape[-2], x.shape[-1])

    def exchange(x):
        return lax.all_to_all(x, "wide", 0, 0, tiled=True)

    everyone = exchange(jnp.broadcast_to(queries[None], (sources, *queries.shape)))
    own = (
        queries,
        interleaved(suffix_keys),
        interleaved(suffix_values),
        new_keys,
        new_values,
        suffix_lengths,
        slot_row,
    )
    slots = queries.shape[1]
    early = suffix_partials(*own, suffix_lengths, (0, slots // 2), kv, scale)
    partials = prompt_partials(everyone, interleaved(prefix_keys), interleaved(prefix_values), early, kv, scale)
    home = exchange(partials)
    late = suffix_partials(*own, partials, (slots // 2, slots), kv, scale)
    return combine(home, [early, late], kv, queries.shape)


def solution(mesh):
    placed = (
        P(None, "wide", "tensor", None),
        P("wide", "tensor", None),
        P("wide", "tensor", None),
        P("wide", None, "tensor", None),
        P("wide", None, "tensor", None),
        P(None, "wide", "tensor", None),
        P(None, "wide", "tensor", None),
        P(),
        P("wide"),
    )
    return jax.shard_map(
        functools.partial(per_device, mesh.shape["wide"]),
        mesh=mesh,
        in_specs=placed,
        out_specs=P(None, "wide", "tensor", None),
        check_vma=False,
    )
```

```python
import functools
import math

import jax
import jax.numpy as jnp
from jax import lax
from jax.experimental import pallas as pl
from jax.experimental.pallas import tpu as pltpu
from jax.sharding import PartitionSpec as P

LOG2E = 1.4426950408889634
LANES = 128
STEPS = 2
TILE, BAND, MAX_WAVE, STATS = 256, 64, 1024, 16
WIDE_GRANT, GRANT = 57 * 1024 * 1024, 50 * 1024 * 1024
UNROLL, LAG = 8, 1
TOO_LARGE, TOO_SMALL = 2.0**100, 2.0**-60
F32 = jnp.float32
BF16 = jnp.bfloat16


def coarse(x):
    return jnp.floor(jnp.ceil(x) * 0.0625) * 16.0


def out_of_range(totals):
    return jnp.logical_not((jnp.max(totals) < TOO_LARGE) & (jnp.min(totals) > TOO_SMALL))


def fold_lanes(x, op):
    parts = [x[:, at : at + LANES] for at in range(0, x.shape[1], LANES)]
    while len(parts) > 1:
        parts = [op(a, b) for a, b in zip(parts[::2], parts[1::2])] + parts[len(parts) & ~1 :]
    return parts[0]


def scores_of(q, keys):
    return lax.dot_general(q, keys, (((1,), (1,)), ((), ())), preferred_element_type=F32)


def spread(m, columns):
    return jnp.concatenate([m] * (columns // LANES), axis=1)


def prompt_kernel(kv, piece, scale, *refs):
    q_in, k_hbm, v_hbm, _, out_ref = refs[:5]
    q_all, k_all, v_all, k_wide, v_wide, top, acc, k_sem, v_sem = refs[5:]
    sources = q_in.shape[0]
    rows = q_all.shape[0]
    rows_head = rows // kv
    per = rows_head // sources
    group = q_in.shape[3] // kv
    pieces = k_all.shape[0] // piece
    tile_rows = kv * TILE
    per_piece = piece // tile_rows
    tiles = pieces * per_piece
    unroll = math.gcd(tiles, UNROLL)
    wave = math.gcd(rows_head, MAX_WAVE // kv)
    bands = wave // BAND

    def span(i):
        return pl.ds(pl.multiple_of(i * piece, piece), piece)

    def k_copy(i):
        return pltpu.make_async_copy(k_hbm.at[span(i), :], k_all.at[span(i), :], k_sem.at[i])

    def v_copy(i):
        return pltpu.make_async_copy(v_hbm.at[span(i), :], v_all.at[span(i), :], v_sem.at[i])

    def start(i, carry):
        k_copy(i).start()
        v_copy(i).start()
        return carry

    lax.fori_loop(0, pieces, start, 0)

    for s in range(sources):
        q = q_in[s].astype(F32) * scale
        steps, slots, _, _ = q.shape
        for h in range(kv):
            heads = slice(h * group, (h + 1) * group)
            part = [q[t, r, heads] for t in range(steps) for r in range(slots)]
            part = jnp.concatenate(part, axis=0)
            high = part.astype(BF16)
            low = (part - high.astype(F32)).astype(BF16)
            at = h * rows_head + s * per
            q_all[at : at + per, :] = jnp.concatenate([high, low], axis=1)
    top[...] = jnp.zeros_like(top)

    def widen(ref, wide, t):
        rows_in = ref[pl.ds(pl.multiple_of(t * tile_rows, tile_rows), tile_rows), :]
        wide[...] = rows_in.astype(F32)

    def head_of(wide, h):
        return wide[pl.ds(h, TILE, stride=kv), :].astype(BF16)

    def push_keys(h):
        keys = head_of(k_wide, h)
        pltpu.matmul_push_rhs(jnp.concatenate([keys, keys], axis=1), h, 0, transpose=True)

    def push_values(h):
        values = head_of(v_wide, h)
        pltpu.matmul_push_rhs(jnp.concatenate([values, jnp.ones_like(values)], axis=1), h, 1)

    def run_wave(base, first_wave):
        every = [(h, b) for h in range(kv) for b in range(bands)]

        def band(h, b):
            at = h * rows_head + base + b * BAND
            return slice(at, at + BAND)

        def body(*accs):
            scores = dict(zip(every, accs[: kv * bands]))
            sums = dict(zip(every, accs[kv * bands :]))
            if first_wave:
                k_copy(0).wait()
                v_copy(0).wait()
            widen(k_all, k_wide, 0)
            for h in range(kv):
                push_keys(h)
            for h, b in every:
                load = h if b == 0 else None
                pltpu.matmul_acc_lhs(scores[h, b], q_all[band(h, b), :], load)
            widen(k_all, k_wide, 1)
            widen(v_all, v_wide, 0)
            for h in range(kv):
                push_keys(h)
                push_values(h)

            def visit(p, carry):
                if first_wave:
                    for i in range(unroll // per_piece):
                        ahead = (p * unroll + 1) // per_piece + 1 + i

                        @pl.when(ahead < pieces)
                        def _():
                            k_copy(ahead).wait()
                            v_copy(ahead).wait()

                late = []
                for u in range(unroll):
                    t = p * unroll + u
                    widen(k_all, k_wide, jnp.minimum(t + 2, tiles - 1))
                    widen(v_all, v_wide, jnp.minimum(t + 1, tiles - 1))
                    for h, b in every:
                        load = h if b == 0 else None
                        w = jnp.exp2(pltpu.matmul_pop(scores[h, b])).astype(BF16)
                        pltpu.matmul_acc_lhs(scores[h, b], q_all[band(h, b), :], load)
                        late.append((sums[h, b], w, load))
                        if len(late) > LAG:
                            pltpu.matmul_acc_lhs(*late.pop(0))
                        if b == bands // 2:
                            push_keys(h)
                            push_values(h)
                for held in late:
                    pltpu.matmul_acc_lhs(*held)
                return carry

            lax.fori_loop(0, tiles // unroll, visit, 0)
            for at in every:
                acc[band(*at), :] = pltpu.matmul_pop(sums[at])
            for at in every:
                pltpu.matmul_pop(scores[at])
            for held in (scores[0, 0], sums[0, 0]):
                for h in range(kv):
                    pltpu.matmul_acc_lhs(held, q_all[:BAND, :], h)
                pltpu.matmul_pop(held)

        shape = (BAND, 2 * LANES)
        pl.run_scoped(body, *[pltpu.ACC(u)(shape, F32) for u in range(2) for _ in every])

    for base in range(0, rows_head, wave):
        run_wave(base, base == 0)

    def with_running_top():
        top[...] = jnp.full_like(top, -jnp.inf)
        acc[...] = jnp.zeros_like(acc)

        def body(scores, weighted):
            def visit(t, carry):
                widen(k_all, k_wide, t)
                widen(v_all, v_wide, t)
                for h in range(kv):
                    push_keys(h)
                    push_values(h)
                for at in range(0, rows, BAND):
                    band = slice(at, at + BAND)
                    load = at // rows_head if at % rows_head == 0 else None
                    pltpu.matmul_acc_lhs(scores, q_all[band, :], load)
                    s = pltpu.matmul_pop(scores)
                    peak = jnp.max(fold_lanes(s, jnp.maximum), axis=1, keepdims=True)
                    new_top = jnp.maximum(top[band, :], coarse(peak))
                    shrink = jnp.exp2(top[band, :] - new_top)
                    top[band, :] = new_top
                    w = jnp.exp2(s - spread(new_top, TILE))
                    pltpu.matmul_acc_lhs(weighted, w.astype(BF16), load)
                    kept = acc[band, :] * spread(shrink, 2 * LANES)
                    acc[band, :] = kept + pltpu.matmul_pop(weighted)
                return carry

            lax.fori_loop(0, tiles, visit, 0)

        shape = (BAND, 2 * LANES)
        pl.run_scoped(body, pltpu.ACC(0)(shape, F32), pltpu.ACC(1)(shape, F32))

    pl.when(out_of_range(acc[:, LANES:]))(with_running_top)

    def as_rows(x):
        rest = jnp.zeros((LANES - per, LANES), F32)
        return jnp.concatenate([x, rest], axis=0).T[:STATS]

    row = lax.broadcasted_iota(jnp.int32, (STATS, LANES), 0)
    for s in range(sources):
        stats = jnp.zeros((STATS, LANES), F32)
        for h in range(kv):
            at = slice(h * rows_head + s * per, h * rows_head + (s + 1) * per)
            out_ref[s, :per, h * LANES : (h + 1) * LANES] = acc[at, :LANES].astype(BF16)
            sums = as_rows(acc[at, LANES:])
            high = sums.astype(BF16).astype(F32)
            stats = jnp.where(row == h, as_rows(top[at, :]), stats)
            stats = jnp.where(row == 2 + h, high, stats)
            stats = jnp.where(row == 4 + h, sums - high, stats)
        rest = [jnp.zeros_like(stats)] * (kv - 1)
        out_ref[s, per:, :] = jnp.concatenate([stats, *rest], axis=1).astype(BF16)


def prompt_partials(queries, keys, values, after, kv, scale):
    sources, steps, slots, heads, head_dim = queries.shape
    per = steps * slots * (heads // kv)
    assert kv <= 2 and per <= LANES and per % BAND == 0
    rows = sources * per * kv
    piece = math.gcd(keys.shape[0], UNROLL // 2 * kv * TILE)
    away = pl.BlockSpec(memory_space=pl.ANY)
    inside = pl.BlockSpec(memory_space=pltpu.VMEM)
    return pl.pallas_call(
        functools.partial(prompt_kernel, kv, piece, scale),
        in_specs=[inside, away, away, away],
        out_shape=jax.ShapeDtypeStruct((sources, per + STATS, kv * LANES), BF16),
        scratch_shapes=[
            pltpu.VMEM((rows, 2 * LANES), BF16),
            pltpu.VMEM(keys.shape, BF16),
            pltpu.VMEM(values.shape, BF16),
            pltpu.VMEM((kv * TILE, LANES), F32),
            pltpu.VMEM((kv * TILE, LANES), F32),
            pltpu.VMEM((rows, LANES), F32),
            pltpu.VMEM((rows, 2 * LANES), F32),
            pltpu.SemaphoreType.DMA((keys.shape[0] // piece,)),
            pltpu.SemaphoreType.DMA((keys.shape[0] // piece,)),
        ],
        compiler_params=pltpu.CompilerParams(vmem_limit_bytes=GRANT),
        cost_estimate=pl.CostEstimate(
            flops=4 * rows * keys.shape[0] * head_dim,
            bytes_accessed=4 * keys.shape[0] * head_dim,
            transcendentals=rows * keys.shape[0] // kv,
        ),
        name="prompt",
    )(queries, keys, values, after)


def suffix_kernel(kv, scale, first, lengths, slots, *refs):
    q_ref, nk_ref, nv_ref, k_hbm, v_hbm, _ = refs[:6]
    near_ref, q_all, scores, k_all, v_all, k_sem, v_sem = refs[6:]
    acc_ref, top_ref, total_ref = (near_ref.at[i] for i in range(3))
    _, count, rows, _ = near_ref.shape
    group = q_ref.shape[2] // kv
    pieces = k_sem.shape[1]
    piece = k_all.shape[1] // pieces
    half = piece // 2
    used = [kv * lengths[slots[first + r]] for r in range(count)]
    ends, end = [], 0
    for r in range(count):
        end = end + (used[r] + piece - 1) // piece
        ends.append(end)

    def place(i):
        slot, begin, length = 0, 0, used[0]
        for r in range(1, count):
            past = i >= ends[r - 1]
            slot = jnp.where(past, r, slot)
            begin = jnp.where(past, ends[r - 1], begin)
            length = jnp.where(past, used[r], length)
        return slot, i - begin, length

    def span(at):
        return pl.ds(pl.multiple_of(at * piece, piece), piece)

    def k_copy(slot, at):
        return pltpu.make_async_copy(
            k_hbm.at[first + slot, span(at), :], k_all.at[slot, span(at), :], k_sem.at[slot, at]
        )

    def v_copy(slot, at):
        return pltpu.make_async_copy(
            v_hbm.at[first + slot, span(at), :], v_all.at[slot, span(at), :], v_sem.at[slot, at]
        )

    def start(i, carry):
        slot, at, _ = place(i)
        k_copy(slot, at).start()
        v_copy(slot, at).start()
        return carry

    lax.fori_loop(0, end, start, 0)

    head = lax.broadcasted_iota(jnp.int32, (rows, LANES), 0) // (STEPS * group)
    lane = lax.broadcasted_iota(jnp.int32, (rows, LANES), 1)
    foreign = jnp.where(lane % kv == head, 0.0, -jnp.inf)

    def fresh(slot, relative):
        row = lax.broadcasted_iota(jnp.int32, (rows, LANES), 0)
        second_head = row >= STEPS * group
        second_step = (row // group) % 2 == 1
        own, values = [], []
        for j in range(STEPS):
            nk, nv = nk_ref[j, first + slot].astype(F32), nv_ref[j, first + slot].astype(F32)
            key = jnp.where(second_head, nk[kv - 1 : kv], nk[0:1])
            values.append(jnp.where(second_head, nv[kv - 1 : kv], nv[0:1]))
            q = q_all[slot, :rows, :LANES].astype(F32)
            s = jnp.sum(q * key, axis=1, keepdims=True) * scale
            own.append(jnp.broadcast_to(s, (rows, LANES)))
        own[1] = jnp.where(second_step, own[1], -jnp.inf)
        peak = jnp.ceil(jnp.maximum(own[0], own[1])) if relative else jnp.zeros_like(own[0])
        weights = [jnp.exp2(s - peak) for s in own]
        top_ref[slot] = peak
        total_ref[slot] = weights[0] + weights[1]
        acc_ref[slot] = sum(w.astype(BF16).astype(F32) * v for w, v in zip(weights, values))

    for r in range(count):
        q = [q_ref[t, first + r].astype(F32) for t in range(STEPS)]
        wide = jnp.concatenate(
            [q[t][h * group : (h + 1) * group] for h in range(kv) for t in range(STEPS)], axis=0
        )
        none = jnp.zeros_like(wide)
        q_all[r] = jnp.concatenate(
            [jnp.concatenate([wide, none], axis=1), jnp.concatenate([none, wide], axis=1)], axis=0
        ).astype(BF16)
        fresh(r, False)

    def halves(ref, slot, at):
        begin = pl.multiple_of(at * piece, piece)
        parts = [ref[slot, pl.ds(begin, half), :], ref[slot, pl.ds(begin + half, half), :]]
        return jnp.concatenate(parts, axis=1)

    def score(i):
        slot, at, _ = place(i)
        k_copy(slot, at).wait()
        scores[...] = scores_of(q_all[slot], halves(k_all, slot, at))

    score(0)

    def visit(i, carry):
        slot, at, length = place(i)
        v_copy(slot, at).wait()
        column = lax.broadcasted_iota(jnp.int32, scores.shape, 1)
        column += jnp.where(lax.broadcasted_iota(jnp.int32, scores.shape, 0) >= rows, half, 0)
        bias = spread(jnp.concatenate([foreign, foreign], axis=0), half)
        s = jnp.where(column < length - at * piece, scores[...] * scale + bias, -jnp.inf)
        pl.when(i + 1 < end)(lambda: score(i + 1))
        w = jnp.exp2(s)
        sums = jnp.sum(fold_lanes(w, jnp.add), axis=1, keepdims=True)
        total_ref[slot] += jnp.broadcast_to(sums[:rows] + sums[rows:], (rows, LANES))
        out = jnp.dot(w.astype(BF16), halves(v_all, slot, at), preferred_element_type=F32)
        acc_ref[slot] += out[:rows, :LANES] + out[rows:, LANES:]
        return carry

    lax.fori_loop(0, end, visit, 0)

    def with_running_top(slot):
        fresh(slot, True)
        some = 512

        def visit(i, carry):
            begin = pl.multiple_of(i * some, some)
            keys, values = k_all[slot, pl.ds(begin, some), :], v_all[slot, pl.ds(begin, some), :]
            s = scores_of(q_all[slot, :rows, :LANES], keys) * scale + spread(foreign, some)
            at = lax.broadcasted_iota(jnp.int32, s.shape, 1)
            s = jnp.where(at < used[slot] - begin, s, -jnp.inf)
            old = top_ref[slot]
            peak = jnp.max(fold_lanes(s, jnp.maximum), axis=1, keepdims=True)
            new_top = jnp.maximum(old, jnp.ceil(peak))
            shrink = jnp.exp2(old - new_top)
            w = jnp.exp2(s - spread(new_top, some))
            top_ref[slot] = new_top
            total_ref[slot] = total_ref[slot] * shrink + jnp.sum(
                fold_lanes(w, jnp.add), axis=1, keepdims=True
            )
            acc_ref[slot] = acc_ref[slot] * shrink + jnp.dot(
                w.astype(BF16), values, preferred_element_type=F32
            )
            return carry

        lax.fori_loop(0, (used[slot] + some - 1) // some, visit, 0)

    for r in range(count):
        pl.when(out_of_range(total_ref[r]))(functools.partial(with_running_top, r))


def suffix_partials(
    queries, keys, values, new_keys, new_values, lengths, slot_row, after, span, kv, scale
):
    steps, _, heads, head_dim = queries.shape
    first, count = span[0], span[1] - span[0]
    cached = keys.shape[1]
    piece = math.gcd(cached, 2048)
    rows = steps * heads
    scalars = pl.BlockSpec(memory_space=pltpu.SMEM)
    away = pl.BlockSpec(memory_space=pl.ANY)
    inside = pl.BlockSpec(memory_space=pltpu.VMEM)
    shape = jax.ShapeDtypeStruct((3, count, rows, LANES), F32)
    return pl.pallas_call(
        functools.partial(suffix_kernel, kv, scale, first),
        in_specs=[scalars, scalars, inside, inside, inside, away, away, away],
        out_shape=shape,
        scratch_shapes=[
            pltpu.VMEM((count, 2 * rows, 2 * head_dim), BF16),
            pltpu.VMEM((2 * rows, piece // 2), F32),
            pltpu.VMEM((count, cached, head_dim), BF16),
            pltpu.VMEM((count, cached, head_dim), BF16),
            pltpu.SemaphoreType.DMA((count, cached // piece)),
            pltpu.SemaphoreType.DMA((count, cached // piece)),
        ],
        compiler_params=pltpu.CompilerParams(vmem_limit_bytes=GRANT if first else WIDE_GRANT),
        cost_estimate=pl.CostEstimate(
            flops=4 * count * rows * cached * head_dim,
            bytes_accessed=4 * count * cached * head_dim,
            transcendentals=count * rows * cached,
        ),
        name="suffix",
    )(lengths, slot_row, queries, new_keys, new_values, keys, values, after)


def combine_kernel(kv, parts_ref, *refs):
    near, out_ref = refs[:-1], refs[-1]
    steps, slots, heads, _ = out_ref.shape
    sources, height, width = parts_ref.shape
    per = height - STATS
    group = heads // kv

    wanted = lax.broadcasted_iota(jnp.int32, (STATS, 2 * width), 0)
    column = lax.broadcasted_iota(jnp.int32, (STATS, 2 * width), 1)
    head = (column % width) // LANES
    is_top = column < width
    picks = (is_top & (wanted == head)) | (
        jnp.logical_not(is_top) & ((wanted == 2 + head) | (wanted == 4 + head))
    )
    stats = jnp.concatenate([parts_ref[s, per:, :LANES] for s in range(sources)], axis=1)
    stats = lax.dot_general(
        stats,
        picks.astype(F32).astype(BF16),
        (((0,), (0,)), ((), ())),
        preferred_element_type=F32,
    )

    def own(kind):
        rows = []
        for t in range(steps):
            for r in range(slots):
                held, index = divmod(r, near[0].shape[1])
                x = near[held]
                at = [(h * steps + t) * group for h in range(kv)]
                rows.append(jnp.concatenate([x[kind, index, a : a + group] for a in at], axis=1))
        return jnp.concatenate(rows, axis=0)

    sums, tops, totals = [own(0)], [own(1)], [own(2)]
    for s in range(sources):
        at = slice(s * LANES, s * LANES + per)
        sums.append(parts_ref[s, :per, :].astype(F32))
        tops.append(stats[at, :width])
        totals.append(stats[at, width:])
    peak = functools.reduce(jnp.maximum, tops)
    factors = [jnp.exp2(m - peak) for m in tops]
    total = sum(f * x for f, x in zip(factors, totals))
    done = sum(f * x for f, x in zip(factors, sums)) / total
    for t in range(steps):
        for r in range(slots):
            at = (t * slots + r) * group
            both = [done[at : at + group, h * LANES : (h + 1) * LANES] for h in range(kv)]
            out_ref[t, r] = jnp.concatenate(both, axis=0).astype(BF16)


def combine(parts, near, kv, shape):
    return pl.pallas_call(
        functools.partial(combine_kernel, kv),
        out_shape=jax.ShapeDtypeStruct(shape, BF16),
        compiler_params=pltpu.CompilerParams(vmem_limit_bytes=16 * 1024 * 1024),
        name="combine",
    )(parts, *near)


def per_device(
    sources,
    queries,
    prefix_keys,
    prefix_values,
    suffix_keys,
    suffix_values,
    new_keys,
    new_values,
    suffix_lengths,
    slot_row,
):
    head_dim = queries.shape[-1]
    kv = prefix_keys.shape[1]
    scale = LOG2E / math.sqrt(head_dim)
    interleaved = lambda x: x.reshape(*x.shape[:-3], x.shape[-3] * x.shape[-2], x.shape[-1])

    def exchange(x):
        return lax.all_to_all(x, "wide", 0, 0, tiled=True)

    everyone = exchange(jnp.broadcast_to(queries[None], (sources, *queries.shape)))
    own = (
        queries,
        interleaved(suffix_keys),
        interleaved(suffix_values),
        new_keys,
        new_values,
        suffix_lengths,
        slot_row,
    )
    slots = queries.shape[1]
    early = suffix_partials(*own, suffix_lengths, (0, slots // 2), kv, scale)
    partials = prompt_partials(everyone, interleaved(prefix_keys), interleaved(prefix_values), early, kv, scale)
    home = exchange(partials)
    late = suffix_partials(*own, partials, (slots // 2, slots), kv, scale)
    return combine(home, [early, late], kv, queries.shape)


def solution(mesh):
    placed = (
        P(None, "wide", "tensor", None),
        P("wide", "tensor", None),
        P("wide", "tensor", None),
        P("wide", None, "tensor", None),
        P("wide", None, "tensor", None),
        P(None, "wide", "tensor", None),
        P(None, "wide", "tensor", None),
        P(),
        P("wide"),
    )
    return jax.shard_map(
        functools.partial(per_device, mesh.shape["wide"]),
        mesh=mesh,
        in_specs=placed,
        out_specs=P(None, "wide", "tensor", None),
        check_vma=False,
    )
```

```python
import functools
import math

import jax
import jax.numpy as jnp
from jax import lax
from jax.experimental import pallas as pl
from jax.experimental.pallas import tpu as pltpu
from jax.sharding import PartitionSpec as P

LOG2E = 1.4426950408889634
LANES = 128
STEPS = 2
TILE, BAND, MAX_WAVE, STATS = 256, 64, 1024, 16
GRANT = 50 * 1024 * 1024
UNROLL, LAG = 8, 1
TOO_LARGE, TOO_SMALL = 2.0**100, 2.0**-60
F32 = jnp.float32
BF16 = jnp.bfloat16


def coarse(x):
    return jnp.floor(jnp.ceil(x) * 0.0625) * 16.0


def out_of_range(totals):
    return jnp.logical_not((jnp.max(totals) < TOO_LARGE) & (jnp.min(totals) > TOO_SMALL))


def fold_lanes(x, op):
    parts = [x[:, at : at + LANES] for at in range(0, x.shape[1], LANES)]
    while len(parts) > 1:
        parts = [op(a, b) for a, b in zip(parts[::2], parts[1::2])] + parts[len(parts) & ~1 :]
    return parts[0]


def scores_of(q, keys):
    return lax.dot_general(q, keys, (((1,), (1,)), ((), ())), preferred_element_type=F32)


def spread(m, columns):
    return jnp.concatenate([m] * (columns // LANES), axis=1)


def prompt_kernel(kv, piece, scale, *refs):
    q_in, k_hbm, v_hbm, _, out_ref = refs[:5]
    q_all, k_all, v_all, k_wide, v_wide, top, acc, k_sem, v_sem = refs[5:]
    sources = q_in.shape[0]
    rows = q_all.shape[0]
    rows_head = rows // kv
    per = rows_head // sources
    group = q_in.shape[3] // kv
    pieces = k_all.shape[0] // piece
    tile_rows = kv * TILE
    per_piece = piece // tile_rows
    tiles = pieces * per_piece
    unroll = math.gcd(tiles, UNROLL)
    wave = math.gcd(rows_head, MAX_WAVE // kv)
    bands = wave // BAND

    def span(i):
        return pl.ds(pl.multiple_of(i * piece, piece), piece)

    def k_copy(i):
        return pltpu.make_async_copy(k_hbm.at[span(i), :], k_all.at[span(i), :], k_sem.at[i])

    def v_copy(i):
        return pltpu.make_async_copy(v_hbm.at[span(i), :], v_all.at[span(i), :], v_sem.at[i])

    def start(i, carry):
        k_copy(i).start()
        v_copy(i).start()
        return carry

    lax.fori_loop(0, pieces, start, 0)

    for s in range(sources):
        q = q_in[s].astype(F32) * scale
        steps, slots, _, _ = q.shape
        for h in range(kv):
            heads = slice(h * group, (h + 1) * group)
            part = [q[t, r, heads] for t in range(steps) for r in range(slots)]
            part = jnp.concatenate(part, axis=0)
            high = part.astype(BF16)
            low = (part - high.astype(F32)).astype(BF16)
            at = h * rows_head + s * per
            q_all[at : at + per, :] = jnp.concatenate([high, low], axis=1)
    top[...] = jnp.zeros_like(top)

    def widen(ref, wide, t):
        rows_in = ref[pl.ds(pl.multiple_of(t * tile_rows, tile_rows), tile_rows), :]
        wide[...] = rows_in.astype(F32)

    def head_of(wide, h):
        return wide[pl.ds(h, TILE, stride=kv), :].astype(BF16)

    def push_keys(h):
        keys = head_of(k_wide, h)
        pltpu.matmul_push_rhs(jnp.concatenate([keys, keys], axis=1), h, 0, transpose=True)

    def push_values(h):
        values = head_of(v_wide, h)
        pltpu.matmul_push_rhs(jnp.concatenate([values, jnp.ones_like(values)], axis=1), h, 1)

    def run_wave(base, first_wave):
        every = [(h, b) for h in range(kv) for b in range(bands)]

        def band(h, b):
            at = h * rows_head + base + b * BAND
            return slice(at, at + BAND)

        def body(*accs):
            scores = dict(zip(every, accs[: kv * bands]))
            sums = dict(zip(every, accs[kv * bands :]))
            if first_wave:
                k_copy(0).wait()
                v_copy(0).wait()
            widen(k_all, k_wide, 0)
            for h in range(kv):
                push_keys(h)
            for h, b in every:
                load = h if b == 0 else None
                pltpu.matmul_acc_lhs(scores[h, b], q_all[band(h, b), :], load)
            widen(k_all, k_wide, 1)
            widen(v_all, v_wide, 0)
            for h in range(kv):
                push_keys(h)
                push_values(h)

            def visit(p, carry):
                if first_wave:
                    for i in range(unroll // per_piece):
                        ahead = (p * unroll + 1) // per_piece + 1 + i

                        @pl.when(ahead < pieces)
                        def _():
                            k_copy(ahead).wait()
                            v_copy(ahead).wait()

                late = []
                for u in range(unroll):
                    t = p * unroll + u
                    widen(k_all, k_wide, jnp.minimum(t + 2, tiles - 1))
                    widen(v_all, v_wide, jnp.minimum(t + 1, tiles - 1))
                    for h, b in every:
                        load = h if b == 0 else None
                        w = jnp.exp2(pltpu.matmul_pop(scores[h, b])).astype(BF16)
                        pltpu.matmul_acc_lhs(scores[h, b], q_all[band(h, b), :], load)
                        late.append((sums[h, b], w, load))
                        if len(late) > LAG:
                            pltpu.matmul_acc_lhs(*late.pop(0))
                        if b == bands // 2:
                            push_keys(h)
                            push_values(h)
                for held in late:
                    pltpu.matmul_acc_lhs(*held)
                return carry

            lax.fori_loop(0, tiles // unroll, visit, 0)
            for at in every:
                acc[band(*at), :] = pltpu.matmul_pop(sums[at])
            for at in every:
                pltpu.matmul_pop(scores[at])
            for held in (scores[0, 0], sums[0, 0]):
                for h in range(kv):
                    pltpu.matmul_acc_lhs(held, q_all[:BAND, :], h)
                pltpu.matmul_pop(held)

        shape = (BAND, 2 * LANES)
        pl.run_scoped(body, *[pltpu.ACC(u)(shape, F32) for u in range(2) for _ in every])

    for base in range(0, rows_head, wave):
        run_wave(base, base == 0)

    def with_running_top():
        top[...] = jnp.full_like(top, -jnp.inf)
        acc[...] = jnp.zeros_like(acc)

        def body(scores, weighted):
            def visit(t, carry):
                widen(k_all, k_wide, t)
                widen(v_all, v_wide, t)
                for h in range(kv):
                    push_keys(h)
                    push_values(h)
                for at in range(0, rows, BAND):
                    band = slice(at, at + BAND)
                    load = at // rows_head if at % rows_head == 0 else None
                    pltpu.matmul_acc_lhs(scores, q_all[band, :], load)
                    s = pltpu.matmul_pop(scores)
                    peak = jnp.max(fold_lanes(s, jnp.maximum), axis=1, keepdims=True)
                    new_top = jnp.maximum(top[band, :], coarse(peak))
                    shrink = jnp.exp2(top[band, :] - new_top)
                    top[band, :] = new_top
                    w = jnp.exp2(s - spread(new_top, TILE))
                    pltpu.matmul_acc_lhs(weighted, w.astype(BF16), load)
                    kept = acc[band, :] * spread(shrink, 2 * LANES)
                    acc[band, :] = kept + pltpu.matmul_pop(weighted)
                return carry

            lax.fori_loop(0, tiles, visit, 0)

        shape = (BAND, 2 * LANES)
        pl.run_scoped(body, pltpu.ACC(0)(shape, F32), pltpu.ACC(1)(shape, F32))

    pl.when(out_of_range(acc[:, LANES:]))(with_running_top)

    lane = lax.broadcasted_iota(jnp.int32, (per, LANES), 1)

    def as_rows(columns):
        tile = jnp.zeros((per, LANES), F32)
        for i in range(kv * sources):
            tile = jnp.where(lane == i, columns(slice(i * per, (i + 1) * per)), tile)
        rest = jnp.zeros((LANES - per, LANES), F32)
        return jnp.concatenate([tile, rest], axis=0).T

    tops = as_rows(lambda at: top[at, :])
    sums = as_rows(lambda at: acc[at, LANES:])
    high = sums.astype(BF16).astype(F32)
    row = lax.broadcasted_iota(jnp.int32, (STATS, LANES), 0)
    for s in range(sources):
        stats = jnp.zeros((STATS, LANES), F32)
        for h in range(kv):
            i = h * sources + s
            at = slice(i * per, (i + 1) * per)
            out_ref[s, :per, h * LANES : (h + 1) * LANES] = acc[at, :LANES].astype(BF16)
            for k, kind in enumerate((tops, high, sums - high)):
                stats = jnp.where(row == 2 * k + h, kind[i : i + 1], stats)
        rest = [jnp.zeros_like(stats)] * (kv - 1)
        out_ref[s, per:, :] = jnp.concatenate([stats, *rest], axis=1).astype(BF16)


def prompt_partials(queries, keys, values, after, kv, scale):
    sources, steps, slots, heads, head_dim = queries.shape
    per = steps * slots * (heads // kv)
    assert kv <= 2 and per <= LANES and per % BAND == 0
    rows = sources * per * kv
    piece = math.gcd(keys.shape[0], UNROLL // 2 * kv * TILE)
    away = pl.BlockSpec(memory_space=pl.ANY)
    inside = pl.BlockSpec(memory_space=pltpu.VMEM)
    return pl.pallas_call(
        functools.partial(prompt_kernel, kv, piece, scale),
        in_specs=[inside, away, away, away],
        out_shape=jax.ShapeDtypeStruct((sources, per + STATS, kv * LANES), BF16),
        scratch_shapes=[
            pltpu.VMEM((rows, 2 * LANES), BF16),
            pltpu.VMEM(keys.shape, BF16),
            pltpu.VMEM(values.shape, BF16),
            pltpu.VMEM((kv * TILE, LANES), F32),
            pltpu.VMEM((kv * TILE, LANES), F32),
            pltpu.VMEM((rows, LANES), F32),
            pltpu.VMEM((rows, 2 * LANES), F32),
            pltpu.SemaphoreType.DMA((keys.shape[0] // piece,)),
            pltpu.SemaphoreType.DMA((keys.shape[0] // piece,)),
        ],
        compiler_params=pltpu.CompilerParams(vmem_limit_bytes=GRANT),
        cost_estimate=pl.CostEstimate(
            flops=4 * rows * keys.shape[0] * head_dim,
            bytes_accessed=4 * keys.shape[0] * head_dim,
            transcendentals=rows * keys.shape[0] // kv,
        ),
        name="prompt",
    )(queries, keys, values, after)


def suffix_kernel(kv, scale, first, lengths, slots, *refs):
    q_ref, nk_ref, nv_ref, k_hbm, v_hbm, _ = refs[:6]
    near_ref, q_all, scores, k_all, v_all, k_sem, v_sem = refs[6:]
    acc_ref, top_ref, total_ref = (near_ref.at[i] for i in range(3))
    _, count, rows, _ = near_ref.shape
    group = q_ref.shape[2] // kv
    pieces = k_sem.shape[1]
    piece = k_all.shape[1] // pieces
    half = piece // 2
    used = [kv * lengths[slots[first + r]] for r in range(count)]
    ends, end = [], 0
    for r in range(count):
        end = end + (used[r] + piece - 1) // piece
        ends.append(end)

    def place(i):
        slot, begin, length = 0, 0, used[0]
        for r in range(1, count):
            past = i >= ends[r - 1]
            slot = jnp.where(past, r, slot)
            begin = jnp.where(past, ends[r - 1], begin)
            length = jnp.where(past, used[r], length)
        return slot, i - begin, length

    def span(at):
        return pl.ds(pl.multiple_of(at * piece, piece), piece)

    def k_copy(slot, at):
        return pltpu.make_async_copy(
            k_hbm.at[first + slot, span(at), :], k_all.at[slot, span(at), :], k_sem.at[slot, at]
        )

    def v_copy(slot, at):
        return pltpu.make_async_copy(
            v_hbm.at[first + slot, span(at), :], v_all.at[slot, span(at), :], v_sem.at[slot, at]
        )

    def start(i, carry):
        slot, at, _ = place(i)
        k_copy(slot, at).start()
        v_copy(slot, at).start()
        return carry

    lax.fori_loop(0, end, start, 0)

    head = lax.broadcasted_iota(jnp.int32, (rows, LANES), 0) // (STEPS * group)
    lane = lax.broadcasted_iota(jnp.int32, (rows, LANES), 1)
    foreign = jnp.where(lane % kv == head, 0.0, -jnp.inf)

    def fresh(slot, relative):
        row = lax.broadcasted_iota(jnp.int32, (rows, LANES), 0)
        second_head = row >= STEPS * group
        second_step = (row // group) % 2 == 1
        own, values = [], []
        for j in range(STEPS):
            nk, nv = nk_ref[j, first + slot].astype(F32), nv_ref[j, first + slot].astype(F32)
            key = jnp.where(second_head, nk[kv - 1 : kv], nk[0:1])
            values.append(jnp.where(second_head, nv[kv - 1 : kv], nv[0:1]))
            q = q_all[slot, :rows, :LANES].astype(F32)
            s = jnp.sum(q * key, axis=1, keepdims=True) * scale
            own.append(jnp.broadcast_to(s, (rows, LANES)))
        own[1] = jnp.where(second_step, own[1], -jnp.inf)
        peak = jnp.ceil(jnp.maximum(own[0], own[1])) if relative else jnp.zeros_like(own[0])
        weights = [jnp.exp2(s - peak) for s in own]
        top_ref[slot] = peak
        total_ref[slot] = weights[0] + weights[1]
        acc_ref[slot] = sum(w.astype(BF16).astype(F32) * v for w, v in zip(weights, values))

    for r in range(count):
        q = [q_ref[t, first + r].astype(F32) for t in range(STEPS)]
        wide = jnp.concatenate(
            [q[t][h * group : (h + 1) * group] for h in range(kv) for t in range(STEPS)], axis=0
        )
        none = jnp.zeros_like(wide)
        q_all[r] = jnp.concatenate(
            [jnp.concatenate([wide, none], axis=1), jnp.concatenate([none, wide], axis=1)], axis=0
        ).astype(BF16)
        fresh(r, False)

    def halves(ref, slot, at):
        begin = pl.multiple_of(at * piece, piece)
        parts = [ref[slot, pl.ds(begin, half), :], ref[slot, pl.ds(begin + half, half), :]]
        return jnp.concatenate(parts, axis=1)

    def score(i):
        slot, at, _ = place(i)
        k_copy(slot, at).wait()
        scores[...] = scores_of(q_all[slot], halves(k_all, slot, at))

    score(0)

    def visit(i, carry):
        slot, at, length = place(i)
        v_copy(slot, at).wait()
        column = lax.broadcasted_iota(jnp.int32, scores.shape, 1)
        column += jnp.where(lax.broadcasted_iota(jnp.int32, scores.shape, 0) >= rows, half, 0)
        bias = spread(jnp.concatenate([foreign, foreign], axis=0), half)
        s = jnp.where(column < length - at * piece, scores[...] * scale + bias, -jnp.inf)
        pl.when(i + 1 < end)(lambda: score(i + 1))
        w = jnp.exp2(s)
        sums = jnp.sum(fold_lanes(w, jnp.add), axis=1, keepdims=True)
        total_ref[slot] += jnp.broadcast_to(sums[:rows] + sums[rows:], (rows, LANES))
        out = jnp.dot(w.astype(BF16), halves(v_all, slot, at), preferred_element_type=F32)
        acc_ref[slot] += out[:rows, :LANES] + out[rows:, LANES:]
        return carry

    lax.fori_loop(0, end, visit, 0)

    def with_running_top(slot):
        fresh(slot, True)
        some = 512

        def visit(i, carry):
            begin = pl.multiple_of(i * some, some)
            keys, values = k_all[slot, pl.ds(begin, some), :], v_all[slot, pl.ds(begin, some), :]
            s = scores_of(q_all[slot, :rows, :LANES], keys) * scale + spread(foreign, some)
            at = lax.broadcasted_iota(jnp.int32, s.shape, 1)
            s = jnp.where(at < used[slot] - begin, s, -jnp.inf)
            old = top_ref[slot]
            peak = jnp.max(fold_lanes(s, jnp.maximum), axis=1, keepdims=True)
            new_top = jnp.maximum(old, jnp.ceil(peak))
            shrink = jnp.exp2(old - new_top)
            w = jnp.exp2(s - spread(new_top, some))
            top_ref[slot] = new_top
            total_ref[slot] = total_ref[slot] * shrink + jnp.sum(
                fold_lanes(w, jnp.add), axis=1, keepdims=True
            )
            acc_ref[slot] = acc_ref[slot] * shrink + jnp.dot(
                w.astype(BF16), values, preferred_element_type=F32
            )
            return carry

        lax.fori_loop(0, (used[slot] + some - 1) // some, visit, 0)

    for r in range(count):
        pl.when(out_of_range(total_ref[r]))(functools.partial(with_running_top, r))


def suffix_partials(
    queries, keys, values, new_keys, new_values, lengths, slot_row, after, span, kv, scale
):
    steps, _, heads, head_dim = queries.shape
    first, count = span[0], span[1] - span[0]
    cached = keys.shape[1]
    piece = math.gcd(cached, 2048)
    rows = steps * heads
    scalars = pl.BlockSpec(memory_space=pltpu.SMEM)
    away = pl.BlockSpec(memory_space=pl.ANY)
    inside = pl.BlockSpec(memory_space=pltpu.VMEM)
    shape = jax.ShapeDtypeStruct((3, count, rows, LANES), F32)
    return pl.pallas_call(
        functools.partial(suffix_kernel, kv, scale, first),
        in_specs=[scalars, scalars, inside, inside, inside, away, away, away],
        out_shape=shape,
        scratch_shapes=[
            pltpu.VMEM((count, 2 * rows, 2 * head_dim), BF16),
            pltpu.VMEM((2 * rows, piece // 2), F32),
            pltpu.VMEM((count, cached, head_dim), BF16),
            pltpu.VMEM((count, cached, head_dim), BF16),
            pltpu.SemaphoreType.DMA((count, cached // piece)),
            pltpu.SemaphoreType.DMA((count, cached // piece)),
        ],
        compiler_params=pltpu.CompilerParams(vmem_limit_bytes=GRANT),
        cost_estimate=pl.CostEstimate(
            flops=4 * count * rows * cached * head_dim,
            bytes_accessed=4 * count * cached * head_dim,
            transcendentals=count * rows * cached,
        ),
        name="suffix",
    )(lengths, slot_row, queries, new_keys, new_values, keys, values, after)


def combine_kernel(kv, parts_ref, *refs):
    near, out_ref = refs[:-1], refs[-1]
    steps, slots, heads, _ = out_ref.shape
    sources, height, width = parts_ref.shape
    per = height - STATS
    group = heads // kv

    wanted = lax.broadcasted_iota(jnp.int32, (STATS, 2 * width), 0)
    column = lax.broadcasted_iota(jnp.int32, (STATS, 2 * width), 1)
    head = (column % width) // LANES
    is_top = column < width
    picks = (is_top & (wanted == head)) | (
        jnp.logical_not(is_top) & ((wanted == 2 + head) | (wanted == 4 + head))
    )
    stats = jnp.concatenate([parts_ref[s, per:, :LANES] for s in range(sources)], axis=1)
    stats = lax.dot_general(
        stats,
        picks.astype(F32).astype(BF16),
        (((0,), (0,)), ((), ())),
        preferred_element_type=F32,
    )

    def own(kind):
        rows = []
        for t in range(steps):
            for r in range(slots):
                early = near[0].shape[1]
                x, index = (near[0], r) if r < early else (near[1], r - early)
                at = [(h * steps + t) * group for h in range(kv)]
                rows.append(jnp.concatenate([x[kind, index, a : a + group] for a in at], axis=1))
        return jnp.concatenate(rows, axis=0)

    sums, tops, totals = [own(0)], [own(1)], [own(2)]
    for s in range(sources):
        at = slice(s * LANES, s * LANES + per)
        sums.append(parts_ref[s, :per, :].astype(F32))
        tops.append(stats[at, :width])
        totals.append(stats[at, width:])
    peak = functools.reduce(jnp.maximum, tops)
    factors = [jnp.exp2(m - peak) for m in tops]
    total = sum(f * x for f, x in zip(factors, totals))
    done = sum(f * x for f, x in zip(factors, sums)) / total
    for t in range(steps):
        for r in range(slots):
            at = (t * slots + r) * group
            both = [done[at : at + group, h * LANES : (h + 1) * LANES] for h in range(kv)]
            out_ref[t, r] = jnp.concatenate(both, axis=0).astype(BF16)


def combine(parts, near, kv, shape):
    return pl.pallas_call(
        functools.partial(combine_kernel, kv),
        out_shape=jax.ShapeDtypeStruct(shape, BF16),
        compiler_params=pltpu.CompilerParams(vmem_limit_bytes=16 * 1024 * 1024),
        name="combine",
    )(parts, *near)


def per_device(
    sources,
    queries,
    prefix_keys,
    prefix_values,
    suffix_keys,
    suffix_values,
    new_keys,
    new_values,
    suffix_lengths,
    slot_row,
):
    head_dim = queries.shape[-1]
    kv = prefix_keys.shape[1]
    scale = LOG2E / math.sqrt(head_dim)
    interleaved = lambda x: x.reshape(*x.shape[:-3], x.shape[-3] * x.shape[-2], x.shape[-1])

    def exchange(x):
        return lax.all_to_all(x, "wide", 0, 0, tiled=True)

    everyone = exchange(jnp.broadcast_to(queries[None], (sources, *queries.shape)))
    own = (
        queries,
        interleaved(suffix_keys),
        interleaved(suffix_values),
        new_keys,
        new_values,
        suffix_lengths,
        slot_row,
    )
    slots = queries.shape[1]
    early = suffix_partials(*own, suffix_lengths, (0, slots // 4), kv, scale)
    partials = prompt_partials(everyone, interleaved(prefix_keys), interleaved(prefix_values), early, kv, scale)
    home = exchange(partials)
    late = suffix_partials(*own, partials, (slots // 4, slots), kv, scale)
    return combine(home, [early, late], kv, queries.shape)


def solution(mesh):
    placed = (
        P(None, "wide", "tensor", None),
        P("wide", "tensor", None),
        P("wide", "tensor", None),
        P("wide", None, "tensor", None),
        P("wide", None, "tensor", None),
        P(None, "wide", "tensor", None),
        P(None, "wide", "tensor", None),
        P(),
        P("wide"),
    )
    return jax.shard_map(
        functools.partial(per_device, mesh.shape["wide"]),
        mesh=mesh,
        in_specs=placed,
        out_specs=P(None, "wide", "tensor", None),
        check_vma=False,
    )
```

```python
import functools
import math

import jax
import jax.numpy as jnp
from jax import lax
from jax.experimental import pallas as pl
from jax.experimental.pallas import tpu as pltpu
from jax.sharding import PartitionSpec as P

LOG2E = 1.4426950408889634
LANES = 128
STEPS = 2
TILE, BAND, MAX_WAVE, STATS = 256, 64, 1024, 16
GRANT = 50 * 1024 * 1024
UNROLL, LAG = 8, 2
TOO_LARGE, TOO_SMALL = 2.0**100, 2.0**-60
F32 = jnp.float32
BF16 = jnp.bfloat16


def coarse(x):
    return jnp.floor(jnp.ceil(x) * 0.0625) * 16.0


def out_of_range(totals):
    return jnp.logical_not((jnp.max(totals) < TOO_LARGE) & (jnp.min(totals) > TOO_SMALL))


def fold_lanes(x, op):
    parts = [x[:, at : at + LANES] for at in range(0, x.shape[1], LANES)]
    while len(parts) > 1:
        parts = [op(a, b) for a, b in zip(parts[::2], parts[1::2])] + parts[len(parts) & ~1 :]
    return parts[0]


def scores_of(q, keys):
    return lax.dot_general(q, keys, (((1,), (1,)), ((), ())), preferred_element_type=F32)


def spread(m, columns):
    return jnp.concatenate([m] * (columns // LANES), axis=1)


def prompt_kernel(kv, piece, scale, *refs):
    q_in, k_hbm, v_hbm, _, out_ref = refs[:5]
    q_all, k_all, v_all, k_wide, v_wide, top, acc, k_sem, v_sem = refs[5:]
    sources = q_in.shape[0]
    rows = q_all.shape[0]
    rows_head = rows // kv
    per = rows_head // sources
    group = q_in.shape[3] // kv
    pieces = k_all.shape[0] // piece
    tile_rows = kv * TILE
    per_piece = piece // tile_rows
    tiles = pieces * per_piece
    unroll = math.gcd(tiles, UNROLL)
    wave = math.gcd(rows_head, MAX_WAVE // kv)
    bands = wave // BAND

    def span(i):
        return pl.ds(pl.multiple_of(i * piece, piece), piece)

    def k_copy(i):
        return pltpu.make_async_copy(k_hbm.at[span(i), :], k_all.at[span(i), :], k_sem.at[i])

    def v_copy(i):
        return pltpu.make_async_copy(v_hbm.at[span(i), :], v_all.at[span(i), :], v_sem.at[i])

    def start(i, carry):
        k_copy(i).start()
        v_copy(i).start()
        return carry

    lax.fori_loop(0, pieces, start, 0)

    for s in range(sources):
        q = q_in[s].astype(F32) * scale
        steps, slots, _, _ = q.shape
        for h in range(kv):
            heads = slice(h * group, (h + 1) * group)
            part = [q[t, r, heads] for t in range(steps) for r in range(slots)]
            part = jnp.concatenate(part, axis=0)
            high = part.astype(BF16)
            low = (part - high.astype(F32)).astype(BF16)
            at = h * rows_head + s * per
            q_all[at : at + per, :] = jnp.concatenate([high, low], axis=1)
    top[...] = jnp.zeros_like(top)

    def widen(ref, wide, t):
        rows_in = ref[pl.ds(pl.multiple_of(t * tile_rows, tile_rows), tile_rows), :]
        wide[...] = rows_in.astype(F32)

    def head_of(wide, h):
        return wide[pl.ds(h, TILE, stride=kv), :].astype(BF16)

    def push_keys(h):
        keys = head_of(k_wide, h)
        pltpu.matmul_push_rhs(jnp.concatenate([keys, keys], axis=1), h, 0, transpose=True)

    def push_values(h):
        values = head_of(v_wide, h)
        pltpu.matmul_push_rhs(jnp.concatenate([values, jnp.ones_like(values)], axis=1), h, 1)

    def run_wave(base, first_wave):
        every = [(h, b) for h in range(kv) for b in range(bands)]

        def band(h, b):
            at = h * rows_head + base + b * BAND
            return slice(at, at + BAND)

        def body(*accs):
            scores = dict(zip(every, accs[: kv * bands]))
            sums = dict(zip(every, accs[kv * bands :]))
            if first_wave:
                k_copy(0).wait()
                v_copy(0).wait()
            widen(k_all, k_wide, 0)
            for h in range(kv):
                push_keys(h)
            for h, b in every:
                load = h if b == 0 else None
                pltpu.matmul_acc_lhs(scores[h, b], q_all[band(h, b), :], load)
            widen(k_all, k_wide, 1)
            widen(v_all, v_wide, 0)
            for h in range(kv):
                push_keys(h)
                push_values(h)

            def visit(p, carry):
                if first_wave:
                    for i in range(unroll // per_piece):
                        ahead = (p * unroll + 1) // per_piece + 1 + i

                        @pl.when(ahead < pieces)
                        def _():
                            k_copy(ahead).wait()
                            v_copy(ahead).wait()

                late = []
                for u in range(unroll):
                    t = p * unroll + u
                    widen(k_all, k_wide, jnp.minimum(t + 2, tiles - 1))
                    widen(v_all, v_wide, jnp.minimum(t + 1, tiles - 1))
                    for h, b in every:
                        load = h if b == 0 else None
                        w = jnp.exp2(pltpu.matmul_pop(scores[h, b])).astype(BF16)
                        pltpu.matmul_acc_lhs(scores[h, b], q_all[band(h, b), :], load)
                        late.append((sums[h, b], w, load))
                        if len(late) > LAG:
                            pltpu.matmul_acc_lhs(*late.pop(0))
                        if b == bands // 2:
                            push_keys(h)
                            push_values(h)
                for held in late:
                    pltpu.matmul_acc_lhs(*held)
                return carry

            lax.fori_loop(0, tiles // unroll, visit, 0)
            for at in every:
                acc[band(*at), :] = pltpu.matmul_pop(sums[at])
            for at in every:
                pltpu.matmul_pop(scores[at])
            for held in (scores[0, 0], sums[0, 0]):
                for h in range(kv):
                    pltpu.matmul_acc_lhs(held, q_all[:BAND, :], h)
                pltpu.matmul_pop(held)

        shape = (BAND, 2 * LANES)
        pl.run_scoped(body, *[pltpu.ACC(u)(shape, F32) for u in range(2) for _ in every])

    for base in range(0, rows_head, wave):
        run_wave(base, base == 0)

    def with_running_top():
        top[...] = jnp.full_like(top, -jnp.inf)
        acc[...] = jnp.zeros_like(acc)

        def body(scores, weighted):
            def visit(t, carry):
                widen(k_all, k_wide, t)
                widen(v_all, v_wide, t)
                for h in range(kv):
                    push_keys(h)
                    push_values(h)
                for at in range(0, rows, BAND):
                    band = slice(at, at + BAND)
                    load = at // rows_head if at % rows_head == 0 else None
                    pltpu.matmul_acc_lhs(scores, q_all[band, :], load)
                    s = pltpu.matmul_pop(scores)
                    peak = jnp.max(fold_lanes(s, jnp.maximum), axis=1, keepdims=True)
                    new_top = jnp.maximum(top[band, :], coarse(peak))
                    shrink = jnp.exp2(top[band, :] - new_top)
                    top[band, :] = new_top
                    w = jnp.exp2(s - spread(new_top, TILE))
                    pltpu.matmul_acc_lhs(weighted, w.astype(BF16), load)
                    kept = acc[band, :] * spread(shrink, 2 * LANES)
                    acc[band, :] = kept + pltpu.matmul_pop(weighted)
                return carry

            lax.fori_loop(0, tiles, visit, 0)

        shape = (BAND, 2 * LANES)
        pl.run_scoped(body, pltpu.ACC(0)(shape, F32), pltpu.ACC(1)(shape, F32))

    pl.when(out_of_range(acc[:, LANES:]))(with_running_top)

    lane = lax.broadcasted_iota(jnp.int32, (per, LANES), 1)

    def as_rows(columns):
        tile = jnp.zeros((per, LANES), F32)
        for i in range(kv * sources):
            tile = jnp.where(lane == i, columns(slice(i * per, (i + 1) * per)), tile)
        rest = jnp.zeros((LANES - per, LANES), F32)
        return jnp.concatenate([tile, rest], axis=0).T

    tops = as_rows(lambda at: top[at, :])
    sums = as_rows(lambda at: acc[at, LANES:])
    high = sums.astype(BF16).astype(F32)
    row = lax.broadcasted_iota(jnp.int32, (STATS, LANES), 0)
    for s in range(sources):
        stats = jnp.zeros((STATS, LANES), F32)
        for h in range(kv):
            i = h * sources + s
            at = slice(i * per, (i + 1) * per)
            out_ref[s, :per, h * LANES : (h + 1) * LANES] = acc[at, :LANES].astype(BF16)
            for k, kind in enumerate((tops, high, sums - high)):
                stats = jnp.where(row == 2 * k + h, kind[i : i + 1], stats)
        rest = [jnp.zeros_like(stats)] * (kv - 1)
        out_ref[s, per:, :] = jnp.concatenate([stats, *rest], axis=1).astype(BF16)


def prompt_partials(queries, keys, values, after, kv, scale):
    sources, steps, slots, heads, head_dim = queries.shape
    per = steps * slots * (heads // kv)
    assert kv <= 2 and per <= LANES and per % BAND == 0
    rows = sources * per * kv
    piece = math.gcd(keys.shape[0], UNROLL // 4 * kv * TILE)
    away = pl.BlockSpec(memory_space=pl.ANY)
    inside = pl.BlockSpec(memory_space=pltpu.VMEM)
    return pl.pallas_call(
        functools.partial(prompt_kernel, kv, piece, scale),
        in_specs=[inside, away, away, away],
        out_shape=jax.ShapeDtypeStruct((sources, per + STATS, kv * LANES), BF16),
        scratch_shapes=[
            pltpu.VMEM((rows, 2 * LANES), BF16),
            pltpu.VMEM(keys.shape, BF16),
            pltpu.VMEM(values.shape, BF16),
            pltpu.VMEM((kv * TILE, LANES), F32),
            pltpu.VMEM((kv * TILE, LANES), F32),
            pltpu.VMEM((rows, LANES), F32),
            pltpu.VMEM((rows, 2 * LANES), F32),
            pltpu.SemaphoreType.DMA((keys.shape[0] // piece,)),
            pltpu.SemaphoreType.DMA((keys.shape[0] // piece,)),
        ],
        compiler_params=pltpu.CompilerParams(vmem_limit_bytes=GRANT),
        cost_estimate=pl.CostEstimate(
            flops=4 * rows * keys.shape[0] * head_dim,
            bytes_accessed=4 * keys.shape[0] * head_dim,
            transcendentals=rows * keys.shape[0] // kv,
        ),
        name="prompt",
    )(queries, keys, values, after)


def suffix_kernel(kv, scale, first, lengths, slots, *refs):
    q_ref, nk_ref, nv_ref, k_hbm, v_hbm, _ = refs[:6]
    near_ref, q_all, scores, k_all, v_all, k_sem, v_sem = refs[6:]
    acc_ref, top_ref, total_ref = (near_ref.at[i] for i in range(3))
    _, count, rows, _ = near_ref.shape
    group = q_ref.shape[2] // kv
    pieces = k_sem.shape[1]
    piece = k_all.shape[1] // pieces
    half = piece // 2
    used = [kv * lengths[slots[first + r]] for r in range(count)]
    ends, end = [], 0
    for r in range(count):
        end = end + (used[r] + piece - 1) // piece
        ends.append(end)

    def place(i):
        slot, begin, length = 0, 0, used[0]
        for r in range(1, count):
            past = i >= ends[r - 1]
            slot = jnp.where(past, r, slot)
            begin = jnp.where(past, ends[r - 1], begin)
            length = jnp.where(past, used[r], length)
        return slot, i - begin, length

    def span(at):
        return pl.ds(pl.multiple_of(at * piece, piece), piece)

    def k_copy(slot, at):
        return pltpu.make_async_copy(
            k_hbm.at[first + slot, span(at), :], k_all.at[slot, span(at), :], k_sem.at[slot, at]
        )

    def v_copy(slot, at):
        return pltpu.make_async_copy(
            v_hbm.at[first + slot, span(at), :], v_all.at[slot, span(at), :], v_sem.at[slot, at]
        )

    def start(i, carry):
        slot, at, _ = place(i)
        k_copy(slot, at).start()
        v_copy(slot, at).start()
        return carry

    lax.fori_loop(0, end, start, 0)

    head = lax.broadcasted_iota(jnp.int32, (rows, LANES), 0) // (STEPS * group)
    lane = lax.broadcasted_iota(jnp.int32, (rows, LANES), 1)
    foreign = jnp.where(lane % kv == head, 0.0, -jnp.inf)

    def fresh(slot, relative):
        row = lax.broadcasted_iota(jnp.int32, (rows, LANES), 0)
        second_head = row >= STEPS * group
        second_step = (row // group) % 2 == 1
        own, values = [], []
        for j in range(STEPS):
            nk, nv = nk_ref[j, first + slot].astype(F32), nv_ref[j, first + slot].astype(F32)
            key = jnp.where(second_head, nk[kv - 1 : kv], nk[0:1])
            values.append(jnp.where(second_head, nv[kv - 1 : kv], nv[0:1]))
            q = q_all[slot, :rows, :LANES].astype(F32)
            s = jnp.sum(q * key, axis=1, keepdims=True) * scale
            own.append(jnp.broadcast_to(s, (rows, LANES)))
        own[1] = jnp.where(second_step, own[1], -jnp.inf)
        peak = jnp.ceil(jnp.maximum(own[0], own[1])) if relative else jnp.zeros_like(own[0])
        weights = [jnp.exp2(s - peak) for s in own]
        top_ref[slot] = peak
        total_ref[slot] = weights[0] + weights[1]
        acc_ref[slot] = sum(w.astype(BF16).astype(F32) * v for w, v in zip(weights, values))

    for r in range(count):
        q = [q_ref[t, first + r].astype(F32) for t in range(STEPS)]
        wide = jnp.concatenate(
            [q[t][h * group : (h + 1) * group] for h in range(kv) for t in range(STEPS)], axis=0
        )
        none = jnp.zeros_like(wide)
        q_all[r] = jnp.concatenate(
            [jnp.concatenate([wide, none], axis=1), jnp.concatenate([none, wide], axis=1)], axis=0
        ).astype(BF16)
        fresh(r, False)

    def halves(ref, slot, at):
        begin = pl.multiple_of(at * piece, piece)
        parts = [ref[slot, pl.ds(begin, half), :], ref[slot, pl.ds(begin + half, half), :]]
        return jnp.concatenate(parts, axis=1)

    def score(i):
        slot, at, _ = place(i)
        k_copy(slot, at).wait()
        scores[...] = scores_of(q_all[slot], halves(k_all, slot, at))

    score(0)

    def visit(i, carry):
        slot, at, length = place(i)
        v_copy(slot, at).wait()
        column = lax.broadcasted_iota(jnp.int32, scores.shape, 1)
        column += jnp.where(lax.broadcasted_iota(jnp.int32, scores.shape, 0) >= rows, half, 0)
        bias = spread(jnp.concatenate([foreign, foreign], axis=0), half)
        s = jnp.where(column < length - at * piece, scores[...] * scale + bias, -jnp.inf)
        pl.when(i + 1 < end)(lambda: score(i + 1))
        w = jnp.exp2(s)
        sums = jnp.sum(fold_lanes(w, jnp.add), axis=1, keepdims=True)
        total_ref[slot] += jnp.broadcast_to(sums[:rows] + sums[rows:], (rows, LANES))
        out = jnp.dot(w.astype(BF16), halves(v_all, slot, at), preferred_element_type=F32)
        acc_ref[slot] += out[:rows, :LANES] + out[rows:, LANES:]
        return carry

    lax.fori_loop(0, end, visit, 0)

    def with_running_top(slot):
        fresh(slot, True)
        some = 512

        def visit(i, carry):
            begin = pl.multiple_of(i * some, some)
            keys, values = k_all[slot, pl.ds(begin, some), :], v_all[slot, pl.ds(begin, some), :]
            s = scores_of(q_all[slot, :rows, :LANES], keys) * scale + spread(foreign, some)
            at = lax.broadcasted_iota(jnp.int32, s.shape, 1)
            s = jnp.where(at < used[slot] - begin, s, -jnp.inf)
            old = top_ref[slot]
            peak = jnp.max(fold_lanes(s, jnp.maximum), axis=1, keepdims=True)
            new_top = jnp.maximum(old, jnp.ceil(peak))
            shrink = jnp.exp2(old - new_top)
            w = jnp.exp2(s - spread(new_top, some))
            top_ref[slot] = new_top
            total_ref[slot] = total_ref[slot] * shrink + jnp.sum(
                fold_lanes(w, jnp.add), axis=1, keepdims=True
            )
            acc_ref[slot] = acc_ref[slot] * shrink + jnp.dot(
                w.astype(BF16), values, preferred_element_type=F32
            )
            return carry

        lax.fori_loop(0, (used[slot] + some - 1) // some, visit, 0)

    for r in range(count):
        pl.when(out_of_range(total_ref[r]))(functools.partial(with_running_top, r))


def suffix_partials(
    queries, keys, values, new_keys, new_values, lengths, slot_row, after, span, kv, scale
):
    steps, _, heads, head_dim = queries.shape
    first, count = span[0], span[1] - span[0]
    cached = keys.shape[1]
    piece = math.gcd(cached, 2048)
    rows = steps * heads
    scalars = pl.BlockSpec(memory_space=pltpu.SMEM)
    away = pl.BlockSpec(memory_space=pl.ANY)
    inside = pl.BlockSpec(memory_space=pltpu.VMEM)
    shape = jax.ShapeDtypeStruct((3, count, rows, LANES), F32)
    return pl.pallas_call(
        functools.partial(suffix_kernel, kv, scale, first),
        in_specs=[scalars, scalars, inside, inside, inside, away, away, away],
        out_shape=shape,
        scratch_shapes=[
            pltpu.VMEM((count, 2 * rows, 2 * head_dim), BF16),
            pltpu.VMEM((2 * rows, piece // 2), F32),
            pltpu.VMEM((count, cached, head_dim), BF16),
            pltpu.VMEM((count, cached, head_dim), BF16),
            pltpu.SemaphoreType.DMA((count, cached // piece)),
            pltpu.SemaphoreType.DMA((count, cached // piece)),
        ],
        compiler_params=pltpu.CompilerParams(vmem_limit_bytes=GRANT),
        cost_estimate=pl.CostEstimate(
            flops=4 * count * rows * cached * head_dim,
            bytes_accessed=4 * count * cached * head_dim,
            transcendentals=count * rows * cached,
        ),
        name="suffix",
    )(lengths, slot_row, queries, new_keys, new_values, keys, values, after)


def combine_kernel(kv, parts_ref, *refs):
    near, out_ref = refs[:-1], refs[-1]
    steps, slots, heads, _ = out_ref.shape
    sources, height, width = parts_ref.shape
    per = height - STATS
    group = heads // kv

    wanted = lax.broadcasted_iota(jnp.int32, (STATS, 2 * width), 0)
    column = lax.broadcasted_iota(jnp.int32, (STATS, 2 * width), 1)
    head = (column % width) // LANES
    is_top = column < width
    picks = (is_top & (wanted == head)) | (
        jnp.logical_not(is_top) & ((wanted == 2 + head) | (wanted == 4 + head))
    )
    stats = jnp.concatenate([parts_ref[s, per:, :LANES] for s in range(sources)], axis=1)
    stats = lax.dot_general(
        stats,
        picks.astype(F32).astype(BF16),
        (((0,), (0,)), ((), ())),
        preferred_element_type=F32,
    )

    def own(kind):
        rows = []
        for t in range(steps):
            for r in range(slots):
                early = near[0].shape[1]
                x, index = (near[0], r) if r < early else (near[1], r - early)
                at = [(h * steps + t) * group for h in range(kv)]
                rows.append(jnp.concatenate([x[kind, index, a : a + group] for a in at], axis=1))
        return jnp.concatenate(rows, axis=0)

    sums, tops, totals = [own(0)], [own(1)], [own(2)]
    for s in range(sources):
        at = slice(s * LANES, s * LANES + per)
        sums.append(parts_ref[s, :per, :].astype(F32))
        tops.append(stats[at, :width])
        totals.append(stats[at, width:])
    peak = functools.reduce(jnp.maximum, tops)
    factors = [jnp.exp2(m - peak) for m in tops]
    total = sum(f * x for f, x in zip(factors, totals))
    done = sum(f * x for f, x in zip(factors, sums)) / total
    for t in range(steps):
        for r in range(slots):
            at = (t * slots + r) * group
            both = [done[at : at + group, h * LANES : (h + 1) * LANES] for h in range(kv)]
            out_ref[t, r] = jnp.concatenate(both, axis=0).astype(BF16)


def combine(parts, near, kv, shape):
    return pl.pallas_call(
        functools.partial(combine_kernel, kv),
        out_shape=jax.ShapeDtypeStruct(shape, BF16),
        compiler_params=pltpu.CompilerParams(vmem_limit_bytes=16 * 1024 * 1024),
        name="combine",
    )(parts, *near)


def per_device(
    sources,
    queries,
    prefix_keys,
    prefix_values,
    suffix_keys,
    suffix_values,
    new_keys,
    new_values,
    suffix_lengths,
    slot_row,
):
    head_dim = queries.shape[-1]
    kv = prefix_keys.shape[1]
    scale = LOG2E / math.sqrt(head_dim)
    interleaved = lambda x: x.reshape(*x.shape[:-3], x.shape[-3] * x.shape[-2], x.shape[-1])

    def exchange(x):
        return lax.all_to_all(x, "wide", 0, 0, tiled=True)

    everyone = exchange(jnp.broadcast_to(queries[None], (sources, *queries.shape)))
    own = (
        queries,
        interleaved(suffix_keys),
        interleaved(suffix_values),
        new_keys,
        new_values,
        suffix_lengths,
        slot_row,
    )
    slots = queries.shape[1]
    early = suffix_partials(*own, suffix_lengths, (0, slots // 4), kv, scale)
    partials = prompt_partials(everyone, interleaved(prefix_keys), interleaved(prefix_values), early, kv, scale)
    home = exchange(partials)
    late = suffix_partials(*own, partials, (slots // 4, slots), kv, scale)
    return combine(home, [early, late], kv, queries.shape)


def solution(mesh):
    placed = (
        P(None, "wide", "tensor", None),
        P("wide", "tensor", None),
        P("wide", "tensor", None),
        P("wide", None, "tensor", None),
        P("wide", None, "tensor", None),
        P(None, "wide", "tensor", None),
        P(None, "wide", "tensor", None),
        P(),
        P("wide"),
    )
    return jax.shard_map(
        functools.partial(per_device, mesh.shape["wide"]),
        mesh=mesh,
        in_specs=placed,
        out_specs=P(None, "wide", "tensor", None),
        check_vma=False,
    )
```

```python
import functools
import math

import jax
import jax.numpy as jnp
from jax import lax
from jax.experimental import pallas as pl
from jax.experimental.pallas import tpu as pltpu
from jax.sharding import PartitionSpec as P

LOG2E = 1.4426950408889634
LANES = 128
STEPS = 2
TILE, BAND, MAX_WAVE, STATS = 256, 32, 1024, 16
GRANT = 50 * 1024 * 1024
UNROLL, LAG = 8, 1
TOO_LARGE, TOO_SMALL = 2.0**100, 2.0**-60
F32 = jnp.float32
BF16 = jnp.bfloat16


def coarse(x):
    return jnp.floor(jnp.ceil(x) * 0.0625) * 16.0


def out_of_range(totals):
    return jnp.logical_not((jnp.max(totals) < TOO_LARGE) & (jnp.min(totals) > TOO_SMALL))


def fold_lanes(x, op):
    parts = [x[:, at : at + LANES] for at in range(0, x.shape[1], LANES)]
    while len(parts) > 1:
        parts = [op(a, b) for a, b in zip(parts[::2], parts[1::2])] + parts[len(parts) & ~1 :]
    return parts[0]


def scores_of(q, keys):
    return lax.dot_general(q, keys, (((1,), (1,)), ((), ())), preferred_element_type=F32)


def spread(m, columns):
    return jnp.concatenate([m] * (columns // LANES), axis=1)


def prompt_kernel(kv, piece, scale, *refs):
    q_in, k_hbm, v_hbm, _, out_ref = refs[:5]
    q_all, k_all, v_all, k_wide, v_wide, top, acc, k_sem, v_sem = refs[5:]
    sources = q_in.shape[0]
    rows = q_all.shape[0]
    rows_head = rows // kv
    per = rows_head // sources
    group = q_in.shape[3] // kv
    pieces = k_all.shape[0] // piece
    tile_rows = kv * TILE
    per_piece = piece // tile_rows
    tiles = pieces * per_piece
    unroll = math.gcd(tiles, UNROLL)
    wave = math.gcd(rows_head, MAX_WAVE // kv)
    bands = wave // BAND

    def span(i):
        return pl.ds(pl.multiple_of(i * piece, piece), piece)

    def k_copy(i):
        return pltpu.make_async_copy(k_hbm.at[span(i), :], k_all.at[span(i), :], k_sem.at[i])

    def v_copy(i):
        return pltpu.make_async_copy(v_hbm.at[span(i), :], v_all.at[span(i), :], v_sem.at[i])

    def start(i, carry):
        k_copy(i).start()
        v_copy(i).start()
        return carry

    lax.fori_loop(0, pieces, start, 0)

    for s in range(sources):
        q = q_in[s].astype(F32) * scale
        steps, slots, _, _ = q.shape
        for h in range(kv):
            heads = slice(h * group, (h + 1) * group)
            part = [q[t, r, heads] for t in range(steps) for r in range(slots)]
            part = jnp.concatenate(part, axis=0)
            high = part.astype(BF16)
            low = (part - high.astype(F32)).astype(BF16)
            at = h * rows_head + s * per
            q_all[at : at + per, :] = jnp.concatenate([high, low], axis=1)
    top[...] = jnp.zeros_like(top)

    def widen(ref, wide, t):
        rows_in = ref[pl.ds(pl.multiple_of(t * tile_rows, tile_rows), tile_rows), :]
        wide[...] = rows_in.astype(F32)

    def head_of(wide, h):
        return wide[pl.ds(h, TILE, stride=kv), :].astype(BF16)

    def push_keys(h):
        keys = head_of(k_wide, h)
        pltpu.matmul_push_rhs(jnp.concatenate([keys, keys], axis=1), h, 0, transpose=True)

    def push_values(h):
        values = head_of(v_wide, h)
        pltpu.matmul_push_rhs(jnp.concatenate([values, jnp.ones_like(values)], axis=1), h, 1)

    def run_wave(base, first_wave):
        every = [(h, b) for h in range(kv) for b in range(bands)]

        def band(h, b):
            at = h * rows_head + base + b * BAND
            return slice(at, at + BAND)

        def body(*accs):
            scores = dict(zip(every, accs[: kv * bands]))
            sums = dict(zip(every, accs[kv * bands :]))
            if first_wave:
                k_copy(0).wait()
                v_copy(0).wait()
            widen(k_all, k_wide, 0)
            for h in range(kv):
                push_keys(h)
            for h, b in every:
                load = h if b == 0 else None
                pltpu.matmul_acc_lhs(scores[h, b], q_all[band(h, b), :], load)
            widen(k_all, k_wide, 1)
            widen(v_all, v_wide, 0)
            for h in range(kv):
                push_keys(h)
                push_values(h)

            def visit(p, carry):
                if first_wave:
                    for i in range(unroll // per_piece):
                        ahead = (p * unroll + 1) // per_piece + 1 + i

                        @pl.when(ahead < pieces)
                        def _():
                            k_copy(ahead).wait()
                            v_copy(ahead).wait()

                late = []
                for u in range(unroll):
                    t = p * unroll + u
                    widen(k_all, k_wide, jnp.minimum(t + 2, tiles - 1))
                    widen(v_all, v_wide, jnp.minimum(t + 1, tiles - 1))
                    for h, b in every:
                        load = h if b == 0 else None
                        w = jnp.exp2(pltpu.matmul_pop(scores[h, b])).astype(BF16)
                        pltpu.matmul_acc_lhs(scores[h, b], q_all[band(h, b), :], load)
                        late.append((sums[h, b], w, load))
                        if len(late) > LAG:
                            pltpu.matmul_acc_lhs(*late.pop(0))
                        if b == bands // 2:
                            push_keys(h)
                            push_values(h)
                for held in late:
                    pltpu.matmul_acc_lhs(*held)
                return carry

            lax.fori_loop(0, tiles // unroll, visit, 0)
            for at in every:
                acc[band(*at), :] = pltpu.matmul_pop(sums[at])
            for at in every:
                pltpu.matmul_pop(scores[at])
            for held in (scores[0, 0], sums[0, 0]):
                for h in range(kv):
                    pltpu.matmul_acc_lhs(held, q_all[:BAND, :], h)
                pltpu.matmul_pop(held)

        shape = (BAND, 2 * LANES)
        pl.run_scoped(body, *[pltpu.ACC(u)(shape, F32) for u in range(2) for _ in every])

    for base in range(0, rows_head, wave):
        run_wave(base, base == 0)

    def with_running_top():
        top[...] = jnp.full_like(top, -jnp.inf)
        acc[...] = jnp.zeros_like(acc)

        def body(scores, weighted):
            def visit(t, carry):
                widen(k_all, k_wide, t)
                widen(v_all, v_wide, t)
                for h in range(kv):
                    push_keys(h)
                    push_values(h)
                for at in range(0, rows, BAND):
                    band = slice(at, at + BAND)
                    load = at // rows_head if at % rows_head == 0 else None
                    pltpu.matmul_acc_lhs(scores, q_all[band, :], load)
                    s = pltpu.matmul_pop(scores)
                    peak = jnp.max(fold_lanes(s, jnp.maximum), axis=1, keepdims=True)
                    new_top = jnp.maximum(top[band, :], coarse(peak))
                    shrink = jnp.exp2(top[band, :] - new_top)
                    top[band, :] = new_top
                    w = jnp.exp2(s - spread(new_top, TILE))
                    pltpu.matmul_acc_lhs(weighted, w.astype(BF16), load)
                    kept = acc[band, :] * spread(shrink, 2 * LANES)
                    acc[band, :] = kept + pltpu.matmul_pop(weighted)
                return carry

            lax.fori_loop(0, tiles, visit, 0)

        shape = (BAND, 2 * LANES)
        pl.run_scoped(body, pltpu.ACC(0)(shape, F32), pltpu.ACC(1)(shape, F32))

    pl.when(out_of_range(acc[:, LANES:]))(with_running_top)

    lane = lax.broadcasted_iota(jnp.int32, (per, LANES), 1)

    def as_rows(columns):
        tile = jnp.zeros((per, LANES), F32)
        for i in range(kv * sources):
            tile = jnp.where(lane == i, columns(slice(i * per, (i + 1) * per)), tile)
        rest = jnp.zeros((LANES - per, LANES), F32)
        return jnp.concatenate([tile, rest], axis=0).T

    tops = as_rows(lambda at: top[at, :])
    sums = as_rows(lambda at: acc[at, LANES:])
    high = sums.astype(BF16).astype(F32)
    row = lax.broadcasted_iota(jnp.int32, (STATS, LANES), 0)
    for s in range(sources):
        stats = jnp.zeros((STATS, LANES), F32)
        for h in range(kv):
            i = h * sources + s
            at = slice(i * per, (i + 1) * per)
            out_ref[s, :per, h * LANES : (h + 1) * LANES] = acc[at, :LANES].astype(BF16)
            for k, kind in enumerate((tops, high, sums - high)):
                stats = jnp.where(row == 2 * k + h, kind[i : i + 1], stats)
        rest = [jnp.zeros_like(stats)] * (kv - 1)
        out_ref[s, per:, :] = jnp.concatenate([stats, *rest], axis=1).astype(BF16)


def prompt_partials(queries, keys, values, after, kv, scale):
    sources, steps, slots, heads, head_dim = queries.shape
    per = steps * slots * (heads // kv)
    assert kv <= 2 and per <= LANES and per % BAND == 0
    rows = sources * per * kv
    piece = math.gcd(keys.shape[0], UNROLL // 2 * kv * TILE)
    away = pl.BlockSpec(memory_space=pl.ANY)
    inside = pl.BlockSpec(memory_space=pltpu.VMEM)
    return pl.pallas_call(
        functools.partial(prompt_kernel, kv, piece, scale),
        in_specs=[inside, away, away, away],
        out_shape=jax.ShapeDtypeStruct((sources, per + STATS, kv * LANES), BF16),
        scratch_shapes=[
            pltpu.VMEM((rows, 2 * LANES), BF16),
            pltpu.VMEM(keys.shape, BF16),
            pltpu.VMEM(values.shape, BF16),
            pltpu.VMEM((kv * TILE, LANES), F32),
            pltpu.VMEM((kv * TILE, LANES), F32),
            pltpu.VMEM((rows, LANES), F32),
            pltpu.VMEM((rows, 2 * LANES), F32),
            pltpu.SemaphoreType.DMA((keys.shape[0] // piece,)),
            pltpu.SemaphoreType.DMA((keys.shape[0] // piece,)),
        ],
        compiler_params=pltpu.CompilerParams(vmem_limit_bytes=GRANT),
        cost_estimate=pl.CostEstimate(
            flops=4 * rows * keys.shape[0] * head_dim,
            bytes_accessed=4 * keys.shape[0] * head_dim,
            transcendentals=rows * keys.shape[0] // kv,
        ),
        name="prompt",
    )(queries, keys, values, after)


def suffix_kernel(kv, scale, first, lengths, slots, *refs):
    q_ref, nk_ref, nv_ref, k_hbm, v_hbm, _ = refs[:6]
    near_ref, q_all, scores, k_all, v_all, k_sem, v_sem = refs[6:]
    acc_ref, top_ref, total_ref = (near_ref.at[i] for i in range(3))
    _, count, rows, _ = near_ref.shape
    group = q_ref.shape[2] // kv
    pieces = k_sem.shape[1]
    piece = k_all.shape[1] // pieces
    half = piece // 2
    used = [kv * lengths[slots[first + r]] for r in range(count)]
    ends, end = [], 0
    for r in range(count):
        end = end + (used[r] + piece - 1) // piece
        ends.append(end)

    def place(i):
        slot, begin, length = 0, 0, used[0]
        for r in range(1, count):
            past = i >= ends[r - 1]
            slot = jnp.where(past, r, slot)
            begin = jnp.where(past, ends[r - 1], begin)
            length = jnp.where(past, used[r], length)
        return slot, i - begin, length

    def span(at):
        return pl.ds(pl.multiple_of(at * piece, piece), piece)

    def k_copy(slot, at):
        return pltpu.make_async_copy(
            k_hbm.at[first + slot, span(at), :], k_all.at[slot, span(at), :], k_sem.at[slot, at]
        )

    def v_copy(slot, at):
        return pltpu.make_async_copy(
            v_hbm.at[first + slot, span(at), :], v_all.at[slot, span(at), :], v_sem.at[slot, at]
        )

    def start(i, carry):
        slot, at, _ = place(i)
        k_copy(slot, at).start()
        v_copy(slot, at).start()
        return carry

    lax.fori_loop(0, end, start, 0)

    head = lax.broadcasted_iota(jnp.int32, (rows, LANES), 0) // (STEPS * group)
    lane = lax.broadcasted_iota(jnp.int32, (rows, LANES), 1)
    foreign = jnp.where(lane % kv == head, 0.0, -jnp.inf)

    def fresh(slot, relative):
        row = lax.broadcasted_iota(jnp.int32, (rows, LANES), 0)
        second_head = row >= STEPS * group
        second_step = (row // group) % 2 == 1
        own, values = [], []
        for j in range(STEPS):
            nk, nv = nk_ref[j, first + slot].astype(F32), nv_ref[j, first + slot].astype(F32)
            key = jnp.where(second_head, nk[kv - 1 : kv], nk[0:1])
            values.append(jnp.where(second_head, nv[kv - 1 : kv], nv[0:1]))
            q = q_all[slot, :rows, :LANES].astype(F32)
            s = jnp.sum(q * key, axis=1, keepdims=True) * scale
            own.append(jnp.broadcast_to(s, (rows, LANES)))
        own[1] = jnp.where(second_step, own[1], -jnp.inf)
        peak = jnp.ceil(jnp.maximum(own[0], own[1])) if relative else jnp.zeros_like(own[0])
        weights = [jnp.exp2(s - peak) for s in own]
        top_ref[slot] = peak
        total_ref[slot] = weights[0] + weights[1]
        acc_ref[slot] = sum(w.astype(BF16).astype(F32) * v for w, v in zip(weights, values))

    for r in range(count):
        q = [q_ref[t, first + r].astype(F32) for t in range(STEPS)]
        wide = jnp.concatenate(
            [q[t][h * group : (h + 1) * group] for h in range(kv) for t in range(STEPS)], axis=0
        )
        none = jnp.zeros_like(wide)
        q_all[r] = jnp.concatenate(
            [jnp.concatenate([wide, none], axis=1), jnp.concatenate([none, wide], axis=1)], axis=0
        ).astype(BF16)
        fresh(r, False)

    def halves(ref, slot, at):
        begin = pl.multiple_of(at * piece, piece)
        parts = [ref[slot, pl.ds(begin, half), :], ref[slot, pl.ds(begin + half, half), :]]
        return jnp.concatenate(parts, axis=1)

    def score(i):
        slot, at, _ = place(i)
        k_copy(slot, at).wait()
        scores[...] = scores_of(q_all[slot], halves(k_all, slot, at))

    score(0)

    def visit(i, carry):
        slot, at, length = place(i)
        v_copy(slot, at).wait()
        column = lax.broadcasted_iota(jnp.int32, scores.shape, 1)
        column += jnp.where(lax.broadcasted_iota(jnp.int32, scores.shape, 0) >= rows, half, 0)
        bias = spread(jnp.concatenate([foreign, foreign], axis=0), half)
        s = jnp.where(column < length - at * piece, scores[...] * scale + bias, -jnp.inf)
        pl.when(i + 1 < end)(lambda: score(i + 1))
        w = jnp.exp2(s)
        sums = jnp.sum(fold_lanes(w, jnp.add), axis=1, keepdims=True)
        total_ref[slot] += jnp.broadcast_to(sums[:rows] + sums[rows:], (rows, LANES))
        out = jnp.dot(w.astype(BF16), halves(v_all, slot, at), preferred_element_type=F32)
        acc_ref[slot] += out[:rows, :LANES] + out[rows:, LANES:]
        return carry

    lax.fori_loop(0, end, visit, 0)

    def with_running_top(slot):
        fresh(slot, True)
        some = 512

        def visit(i, carry):
            begin = pl.multiple_of(i * some, some)
            keys, values = k_all[slot, pl.ds(begin, some), :], v_all[slot, pl.ds(begin, some), :]
            s = scores_of(q_all[slot, :rows, :LANES], keys) * scale + spread(foreign, some)
            at = lax.broadcasted_iota(jnp.int32, s.shape, 1)
            s = jnp.where(at < used[slot] - begin, s, -jnp.inf)
            old = top_ref[slot]
            peak = jnp.max(fold_lanes(s, jnp.maximum), axis=1, keepdims=True)
            new_top = jnp.maximum(old, jnp.ceil(peak))
            shrink = jnp.exp2(old - new_top)
            w = jnp.exp2(s - spread(new_top, some))
            top_ref[slot] = new_top
            total_ref[slot] = total_ref[slot] * shrink + jnp.sum(
                fold_lanes(w, jnp.add), axis=1, keepdims=True
            )
            acc_ref[slot] = acc_ref[slot] * shrink + jnp.dot(
                w.astype(BF16), values, preferred_element_type=F32
            )
            return carry

        lax.fori_loop(0, (used[slot] + some - 1) // some, visit, 0)

    for r in range(count):
        pl.when(out_of_range(total_ref[r]))(functools.partial(with_running_top, r))


def suffix_partials(
    queries, keys, values, new_keys, new_values, lengths, slot_row, after, span, kv, scale
):
    steps, _, heads, head_dim = queries.shape
    first, count = span[0], span[1] - span[0]
    cached = keys.shape[1]
    piece = math.gcd(cached, 2048)
    rows = steps * heads
    scalars = pl.BlockSpec(memory_space=pltpu.SMEM)
    away = pl.BlockSpec(memory_space=pl.ANY)
    inside = pl.BlockSpec(memory_space=pltpu.VMEM)
    shape = jax.ShapeDtypeStruct((3, count, rows, LANES), F32)
    return pl.pallas_call(
        functools.partial(suffix_kernel, kv, scale, first),
        in_specs=[scalars, scalars, inside, inside, inside, away, away, away],
        out_shape=shape,
        scratch_shapes=[
            pltpu.VMEM((count, 2 * rows, 2 * head_dim), BF16),
            pltpu.VMEM((2 * rows, piece // 2), F32),
            pltpu.VMEM((count, cached, head_dim), BF16),
            pltpu.VMEM((count, cached, head_dim), BF16),
            pltpu.SemaphoreType.DMA((count, cached // piece)),
            pltpu.SemaphoreType.DMA((count, cached // piece)),
        ],
        compiler_params=pltpu.CompilerParams(vmem_limit_bytes=GRANT),
        cost_estimate=pl.CostEstimate(
            flops=4 * count * rows * cached * head_dim,
            bytes_accessed=4 * count * cached * head_dim,
            transcendentals=count * rows * cached,
        ),
        name="suffix",
    )(lengths, slot_row, queries, new_keys, new_values, keys, values, after)


def combine_kernel(kv, parts_ref, *refs):
    near, out_ref = refs[:-1], refs[-1]
    steps, slots, heads, _ = out_ref.shape
    sources, height, width = parts_ref.shape
    per = height - STATS
    group = heads // kv

    wanted = lax.broadcasted_iota(jnp.int32, (STATS, 2 * width), 0)
    column = lax.broadcasted_iota(jnp.int32, (STATS, 2 * width), 1)
    head = (column % width) // LANES
    is_top = column < width
    picks = (is_top & (wanted == head)) | (
        jnp.logical_not(is_top) & ((wanted == 2 + head) | (wanted == 4 + head))
    )
    stats = jnp.concatenate([parts_ref[s, per:, :LANES] for s in range(sources)], axis=1)
    stats = lax.dot_general(
        stats,
        picks.astype(F32).astype(BF16),
        (((0,), (0,)), ((), ())),
        preferred_element_type=F32,
    )

    def own(kind):
        rows = []
        for t in range(steps):
            for r in range(slots):
                early = near[0].shape[1]
                x, index = (near[0], r) if r < early else (near[1], r - early)
                at = [(h * steps + t) * group for h in range(kv)]
                rows.append(jnp.concatenate([x[kind, index, a : a + group] for a in at], axis=1))
        return jnp.concatenate(rows, axis=0)

    sums, tops, totals = [own(0)], [own(1)], [own(2)]
    for s in range(sources):
        at = slice(s * LANES, s * LANES + per)
        sums.append(parts_ref[s, :per, :].astype(F32))
        tops.append(stats[at, :width])
        totals.append(stats[at, width:])
    peak = functools.reduce(jnp.maximum, tops)
    factors = [jnp.exp2(m - peak) for m in tops]
    total = sum(f * x for f, x in zip(factors, totals))
    done = sum(f * x for f, x in zip(factors, sums)) / total
    for t in range(steps):
        for r in range(slots):
            at = (t * slots + r) * group
            both = [done[at : at + group, h * LANES : (h + 1) * LANES] for h in range(kv)]
            out_ref[t, r] = jnp.concatenate(both, axis=0).astype(BF16)


def combine(parts, near, kv, shape):
    return pl.pallas_call(
        functools.partial(combine_kernel, kv),
        out_shape=jax.ShapeDtypeStruct(shape, BF16),
        compiler_params=pltpu.CompilerParams(vmem_limit_bytes=16 * 1024 * 1024),
        name="combine",
    )(parts, *near)


def per_device(
    sources,
    queries,
    prefix_keys,
    prefix_values,
    suffix_keys,
    suffix_values,
    new_keys,
    new_values,
    suffix_lengths,
    slot_row,
):
    head_dim = queries.shape[-1]
    kv = prefix_keys.shape[1]
    scale = LOG2E / math.sqrt(head_dim)
    interleaved = lambda x: x.reshape(*x.shape[:-3], x.shape[-3] * x.shape[-2], x.shape[-1])

    def exchange(x):
        return lax.all_to_all(x, "wide", 0, 0, tiled=True)

    everyone = exchange(jnp.broadcast_to(queries[None], (sources, *queries.shape)))
    own = (
        queries,
        interleaved(suffix_keys),
        interleaved(suffix_values),
        new_keys,
        new_values,
        suffix_lengths,
        slot_row,
    )
    slots = queries.shape[1]
    early = suffix_partials(*own, suffix_lengths, (0, slots // 4), kv, scale)
    partials = prompt_partials(everyone, interleaved(prefix_keys), interleaved(prefix_values), early, kv, scale)
    home = exchange(partials)
    late = suffix_partials(*own, partials, (slots // 4, slots), kv, scale)
    return combine(home, [early, late], kv, queries.shape)


def solution(mesh):
    placed = (
        P(None, "wide", "tensor", None),
        P("wide", "tensor", None),
        P("wide", "tensor", None),
        P("wide", None, "tensor", None),
        P("wide", None, "tensor", None),
        P(None, "wide", "tensor", None),
        P(None, "wide", "tensor", None),
        P(),
        P("wide"),
    )
    return jax.shard_map(
        functools.partial(per_device, mesh.shape["wide"]),
        mesh=mesh,
        in_specs=placed,
        out_specs=P(None, "wide", "tensor", None),
        check_vma=False,
    )
```
